32 devices in a mesh: role: 4 (over y, x), gx: 2 (over core), gz: 4 (over z).
Axes of the slice: x: 2, y: 2, z: 4, core: 2. Of those that a mesh axis runs over, the one named last changes fastest.
Arguments:
- pressure_old: float32 [64, 128, 512], P('gz', 'gx', 'role'), may hold values from -2.5 to -0.2
- vg_alpha: float32 [64, 128, 512], P('gz', 'gx', 'role'), may hold values from 0.5 to 1.5
- vg_n: float32 [64, 128, 512], P('gz', 'gx', 'role'), may hold values from 1.3 to 2.5
- conductivity_sat: float32 [64, 128, 512], P('gz', 'gx', 'role'), may hold values from 0.05 to 1
- porosity: float32 [64, 128, 512], P('gz', 'gx', 'role'), may hold values from 0.25 to 0.45
- tile_owner: int32 [128, 4], replicated, may hold values from -1 to 7, as said below
- land_temp: float32 [4, 8, 6, 16, 128], P('role', ('gx', 'gz')), may hold values from -6 to 6
- transpiration: float32 [4, 8, 6, 128], P('role', ('gx', 'gz')), may hold values from 0.2 to 1
- air_temp: float32 [4, 8, 6, 128], P('role', ('gx', 'gz')), may hold values from -6 to 6
- root_layers: int32 [4, 8, 6, 128], P('role', ('gx', 'gz')), may hold values from 1 to 16
Outputs:
- pressure_new: float32 [64, 128, 512], P('gz', 'gx', 'role')
- land_temp_new: float32 [4, 8, 6, 16, 128], P('role', ('gx', 'gz'))
The draws below stay inside these ranges and needn't reach their ends.
Inputs may be any that keep to these rules, and one draw needn't show every extreme that they name: `tile_owner`: -1 marks an inactive tile; otherwise the value is the land device, numbered along gx and gz with gz fastest, within the tile's role group; at most 3 tiles of one block have the same owner, and in every block one owner holds exactly 3 of them.
All inputs are finite; a program needn't handle non-finite values.
Results may differ from the reference program's by a relative error of at most 0.00002.
Values sent between devices are 32-bit elements; how exact they have to be, the bound alone decides.
No kernel may reach another device: no remote copies, remote signals or barrier semaphores. Data moves between devices by JAX's collectives and lax.ppermute only.
A program may use at most 64 MiB of HBM per device.

```python
import math
import jax
import jax.numpy as jnp
from jax import lax

LAYERS = 16
LEVELS_PER_LAYER = 4
NZ = 64
CX = 64
CY = 128
CAP = 3
SWEEPS = 3
HEAT_STEPS = 4
NX = 128
NY = 512
GROUPS = 8
SLOTS = 6
N_ROLE = 4
N_GX = 2
N_GZ = 4


def draw_tile_owner(key, part):
    groups = N_GX * N_GZ
    blocks = N_GX * N_ROLE
    key_heavy, key_perm, key_rot, key_coin = jax.random.split(key, 4)
    heavy = jax.random.randint(key_heavy, (N_ROLE,), 0, groups)
    perm_keys = jax.random.split(key_perm, blocks)
    position = jax.vmap(lambda single: jax.random.permutation(single, CX))(perm_keys)
    rotation = jax.random.randint(key_rot, (blocks, 1), 0, groups - 1)
    coins = jax.random.randint(key_coin, (blocks, CX), 0, 4) < 3
    heavy_block = jnp.tile(heavy, N_GX)[:, None]
    later = position - CAP
    others = (later + rotation) % (groups - 1)
    other_owner = others + (others >= heavy_block).astype(jnp.int32)
    active_other = (later >= 0) & (later < (groups - 1) * CAP) & coins
    owner = jnp.where(position < CAP, heavy_block, jnp.where(active_other, other_owner, -1))
    owner = owner.astype(jnp.int32).reshape(N_GX, N_ROLE, CX).transpose(0, 2, 1)
    return owner.reshape(N_GX * CX, N_ROLE)


def place_ends(drawn, key, smallest, high):
    extent = drawn.shape
    index_at = [jax.random.randint(jax.random.fold_in(key, axis), (), 0, extent[axis]) for axis in range(len(extent))]
    drawn = drawn.at[tuple(index_at)].set(smallest)
    longest = extent.index(max(extent))
    index_at[longest] = (index_at[longest] + 1) % extent[longest]
    return drawn.at[tuple(index_at)].set(high)


def block_levels(key, extent, cuts, smallest, largest):
    def one(dim, blocks):
        draws = jax.random.uniform(jax.random.fold_in(jax.random.fold_in(key, 6), dim), (blocks,), jnp.float32, smallest / len(cuts), largest / len(cuts))
        return jnp.repeat(jnp.exp(draws), extent[dim] // blocks).reshape((-1,) + (1,) * (len(extent) - dim - 1))

    gain = one(*cuts[0])
    for cut in cuts[1:]:
        gain = gain * one(*cut)
    return gain


def gaussian(stream_key, extent, scale, limit, cuts=(), held_as=jnp.bfloat16):
    array = jax.random.normal(stream_key, extent, jnp.float32) * scale
    if len(cuts) > 0:
        array = block_levels(stream_key, extent, cuts, -0.22, 0.18) * array
    return jnp.clip(array, min=-limit, max=limit).astype(held_as)


def setup_inputs(seed: int = 0) -> dict:
    arg_keys = jax.random.split(jax.random.key(seed), 11)
    return {
        "pressure_old": jnp.clip(-2.5 + 2.3 * jax.random.uniform(arg_keys[0], (NZ, NX, NY), jnp.float32) ** block_levels(arg_keys[0], (NZ, NX, NY), ((0, 4), (1, 2), (2, 4)), -0.2, 0.2), -2.5, -0.2),
        "vg_alpha": jnp.clip(jnp.exp(math.log(1.5) - 1.0986123 * jax.random.uniform(arg_keys[1], (NZ, NX, NY), jnp.float32) ** block_levels(arg_keys[1], (NZ, NX, NY), ((0, 4), (1, 2), (2, 4)), -0.2, 0.2)), 0.5, 1.5),
        "vg_n": jnp.clip(1.3 + 1.2 * jax.random.uniform(arg_keys[2], (NZ, NX, NY), jnp.float32) ** block_levels(arg_keys[2], (NZ, NX, NY), ((0, 4), (1, 2), (2, 4)), -0.2, 0.2), 1.3, 2.5),
        "conductivity_sat": jnp.clip(jnp.exp(math.log(1.0) - 2.9957323 * jax.random.uniform(arg_keys[3], (NZ, NX, NY), jnp.float32) ** block_levels(arg_keys[3], (NZ, NX, NY), ((0, 4), (1, 2), (2, 4)), -0.2, 0.2)), 0.05, 1.0),
        "porosity": jnp.clip(0.25 + 0.19999999 * jax.random.uniform(arg_keys[4], (NZ, NX, NY), jnp.float32) ** block_levels(arg_keys[4], (NZ, NX, NY), ((0, 4), (1, 2), (2, 4)), -0.2, 0.2), 0.25, 0.45),
        "tile_owner": draw_tile_owner(jax.random.fold_in(arg_keys[10], 71), 0),
        "land_temp": gaussian(arg_keys[6], (N_ROLE, GROUPS, SLOTS, LAYERS, CY), 1.0, 6.0, ((0, 4), (1, 8)), jnp.float32),
        "transpiration": jnp.clip(0.2 + 0.8 * jax.random.uniform(arg_keys[7], (N_ROLE, GROUPS, SLOTS, CY), jnp.float32) ** block_levels(arg_keys[7], (N_ROLE, GROUPS, SLOTS, CY), ((0, 4), (1, 8)), -0.2, 0.2), 0.2, 1.0),
        "air_temp": gaussian(arg_keys[8], (N_ROLE, GROUPS, SLOTS, CY), 1.5, 6.0, ((0, 4), (1, 8)), jnp.float32),
        "root_layers": place_ends(jax.random.randint(arg_keys[9], (N_ROLE, GROUPS, SLOTS, CY), 1, 17), jax.random.fold_in(arg_keys[9], 1), 1, 16).astype(jnp.int32),
    }


def soil_curves(head, alpha, vgn, ksat):
    suction = jnp.sqrt(head * head + 0.01)
    logx = vgn * jnp.log(alpha * suction)
    expo = 1.0 - 1.0 / vgn
    softer = jnp.log1p(jnp.exp(logx))
    satur = jnp.exp(-expo * softer)
    cond = ksat * jnp.sqrt(satur) * (1.0 - jnp.exp(expo * (logx - softer))) ** 2
    return (satur, cond)

def layer_mean(values, axis):
    shape = values.shape
    split = shape[:axis] + (shape[axis] // 4, 4) + shape[axis + 1:]
    parts = values.reshape(split)
    first = lax.index_in_dim(parts, 0, axis + 1, keepdims=False)
    second = lax.index_in_dim(parts, 1, axis + 1, keepdims=False)
    third = lax.index_in_dim(parts, 2, axis + 1, keepdims=False)
    fourth = lax.index_in_dim(parts, 3, axis + 1, keepdims=False)
    return (first + second + third + fourth) * 0.25

def land_step(satur, head, temps, tpot, air, roots):
    nlayer = satur.shape[-2]
    layer = jnp.arange(nlayer, dtype=jnp.float32)[:, None]
    depth = jnp.arange(nlayer, dtype=jnp.int32)[:, None]
    weights = jnp.exp(-layer / 4.0) * (depth < roots[..., None, :]).astype(jnp.float32)
    weights = weights / lax.optimization_barrier(jnp.sum(weights, axis=-2, keepdims=True))
    stress = 1.0 / (1.0 + head * head / 2.25)
    uptake = tpot[..., None, :] * weights * stress
    kappa = 0.25 + 0.9 * satur
    inner = 0.5 * (kappa[..., :-1, :] + kappa[..., 1:, :])
    k_above = jnp.concatenate([kappa[..., :1, :], inner], axis=-2)
    k_below = jnp.concatenate([inner, jnp.zeros_like(kappa[..., :1, :])], axis=-2)
    for substep in range(HEAT_STEPS):
        above = jnp.concatenate([air[..., None, :], temps[..., :-1, :]], axis=-2)
        below = jnp.concatenate([temps[..., 1:, :], temps[..., -1:, :]], axis=-2)
        temps = temps + 0.2 * (k_above * (above - temps) + k_below * (below - temps)) - 0.3 * uptake
    return (uptake, temps)

def sweep_update(padh, padk, masks, head, cond, water, theta_old, sink, omega):
    mask_up, mask_down, mask_xm, mask_xp, mask_ym, mask_yp = masks
    near_up = padh[:-2, 1:-1, 1:-1]
    near_down = padh[2:, 1:-1, 1:-1]
    near_xm = padh[1:-1, :-2, 1:-1]
    near_xp = padh[1:-1, 2:, 1:-1]
    near_ym = padh[1:-1, 1:-1, :-2]
    near_yp = padh[1:-1, 1:-1, 2:]
    kf_up = 0.5 * (cond + padk[:-2, 1:-1, 1:-1]) * mask_up
    kf_down = 0.5 * (cond + padk[2:, 1:-1, 1:-1]) * mask_down
    kf_xm = 0.5 * (cond + padk[1:-1, :-2, 1:-1]) * mask_xm
    kf_xp = 0.5 * (cond + padk[1:-1, 2:, 1:-1]) * mask_xp
    kf_ym = 0.5 * (cond + padk[1:-1, 1:-1, :-2]) * mask_ym
    kf_yp = 0.5 * (cond + padk[1:-1, 1:-1, 2:]) * mask_yp
    flux = kf_up * (head - near_up) + kf_down * (head - near_down)
    flux = flux + kf_xm * (head - near_xm) + kf_xp * (head - near_xp)
    flux = flux + kf_ym * (head - near_ym) + kf_yp * (head - near_yp)
    resid = water - theta_old + flux + (kf_down - kf_up) + sink
    diag = 1.0 + (kf_up + kf_down + kf_xm + kf_xp + kf_ym + kf_yp)
    return head - omega * resid / diag

def reference(pressure_old, vg_alpha, vg_n, conductivity_sat, porosity, tile_owner, land_temp, transpiration, air_temp, root_layers):
    groups = N_GX * N_GZ
    satur_old, cond_old = soil_curves(pressure_old, vg_alpha, vg_n, conductivity_sat)
    theta_old = porosity * satur_old
    layer_sat = layer_mean(satur_old, 0)
    layer_head = layer_mean(pressure_old, 0)
    tile_sat = layer_sat.reshape(LAYERS, NX, N_ROLE, CY).transpose(1, 2, 0, 3)
    tile_head = layer_head.reshape(LAYERS, NX, N_ROLE, CY).transpose(1, 2, 0, 3)
    owners3 = tile_owner.reshape(N_GX, CX, N_ROLE)
    onehot = (owners3[..., None] == jnp.arange(groups, dtype=jnp.int32)).astype(jnp.int32)
    before = (jnp.cumsum(onehot, axis=1) - onehot).astype(jnp.int32)
    rank = lax.optimization_barrier(jnp.sum(before * onehot, axis=-1)).astype(jnp.int32).reshape(NX, N_ROLE)
    block_row = (jnp.arange(NX, dtype=jnp.int32) // CX)[:, None]
    slot = jnp.broadcast_to(block_row * CAP + rank, (NX, N_ROLE)).astype(jnp.int32)
    active = tile_owner >= 0
    owner_safe = jnp.where(active, tile_owner, 0).astype(jnp.int32)
    owner_drop = jnp.where(active, tile_owner, groups).astype(jnp.int32)
    role_index = jnp.broadcast_to(jnp.arange(N_ROLE, dtype=jnp.int32)[None, :], (NX, N_ROLE))
    temps = land_temp[role_index, owner_safe, slot]
    tpot = transpiration[role_index, owner_safe, slot]
    air = air_temp[role_index, owner_safe, slot]
    roots = root_layers[role_index, owner_safe, slot]
    uptake, new_temps = land_step(tile_sat, tile_head, temps, tpot, air, roots)
    land_temp_new = land_temp.at[role_index, owner_drop, slot].set(new_temps, mode='drop')
    uptake = uptake * active.astype(jnp.float32)[:, :, None, None]
    sink = uptake.transpose(2, 0, 1, 3).reshape(LAYERS, NX, NY)
    sink = jnp.repeat(sink, LEVELS_PER_LAYER, axis=0)
    zglob = jnp.arange(NZ)
    xglob = jnp.arange(NX)
    yglob = jnp.arange(NY)
    masks = ((zglob > 0).astype(jnp.float32)[:, None, None], (zglob < NZ - 1).astype(jnp.float32)[:, None, None], (xglob > 0).astype(jnp.float32)[None, :, None], (xglob < NX - 1).astype(jnp.float32)[None, :, None], (yglob > 0).astype(jnp.float32)[None, None, :], (yglob < NY - 1).astype(jnp.float32)[None, None, :])
    head = pressure_old
    cond = cond_old
    water = theta_old
    for sweep_index in range(SWEEPS):
        if sweep_index > 0:
            satur, cond = soil_curves(head, vg_alpha, vg_n, conductivity_sat)
            water = porosity * satur
        omega = 1.0 / (1.0 + 0.6 * math.cos(math.pi * (2 * sweep_index + 1) / (2 * SWEEPS)))
        head = sweep_update(jnp.pad(head, 1), jnp.pad(cond, 1), masks, head, cond, water, theta_old, sink, omega)
    return (head, land_temp_new)
```

```python
import functools
import math

import jax
import jax.numpy as jnp
from jax import lax
from jax.experimental import pallas as pl
from jax.experimental.pallas import tpu as pltpu
from jax.sharding import PartitionSpec as P

LAYERS_PER_BLOCK = 4
LEVELS_PER_LAYER = 4
CAP = 3
SWEEPS = 3
HEAT_STEPS = 4
HALO = SWEEPS
AXES = ("role", "gx", "gz")
VMEM = pl.BlockSpec(memory_space=pltpu.VMEM)
SMEM = pl.BlockSpec(memory_space=pltpu.SMEM)
ANY = pl.BlockSpec(memory_space=pl.ANY)
PARAMS = pltpu.CompilerParams(vmem_limit_bytes=40 * 1024 * 1024)

LEVELS = 16
ROWS = 64
COLS = 128
EDGE = 8
WIDE = ROWS + EDGE
H0 = 0
NH = LEVELS + 2 * HALO
A0 = H0 + NH
NC = LEVELS + 2 * HALO - 2
N0 = A0 + NC
S0 = N0 + NC
K_LO = S0 + NC
K_HI = K_LO + 1
P0 = K_HI + 1
NP = LEVELS + 2 * HALO - 4
M_LO = P0 + NP
M_HI = M_LO + 1
TP = M_HI + 1
RT = TP + 1
PLANES = RT + 1
PACKS = (PLANES + 7) // 8
SIDE = 16
Z_SEND = 12
Y_SEND = (PLANES * HALO + 7) // 8 * 8


def omega(sweep):
    return 1.0 / (1.0 + 0.6 * math.cos(math.pi * (2 * sweep + 1) / (2 * SWEEPS)))


def place(axis):
    return lax.axis_index(axis)


def is_even(axis):
    return lax.rem(place(axis), 2) == 0


def pairing(sizes, axis, odd):
    pairs = []
    which = AXES.index(axis)
    for index in range(math.prod(sizes)):
        at = [index // (sizes[1] * sizes[2]), index // sizes[2] % sizes[1], index % sizes[2]]
        count = sizes[which]
        there = list(at)
        if not odd:
            there[which] = at[which] ^ 1
        else:
            there[which] = at[which] + (1 if at[which] % 2 else -1)
            if not 0 <= there[which] < count:
                there = list(at)
                if axis == "gx":
                    there[1] = count - 1 - at[1]
                else:
                    there[1] = at[1] ^ 1
        pairs.append((index, (there[0] * sizes[1] + there[1]) * sizes[2] + there[2]))
    return pairs


def xor_pairs(sizes, axis, bit):
    pairs = []
    which = AXES.index(axis)
    for index in range(math.prod(sizes)):
        at = [index // (sizes[1] * sizes[2]), index // sizes[2] % sizes[1], index % sizes[2]]
        at[which] ^= bit
        pairs.append((index, (at[0] * sizes[1] + at[1]) * sizes[2] + at[2]))
    return pairs


def curves(head, alpha2, half_n, half_ks, expo):
    logx = half_n * jnp.log(alpha2 * (head * head + 0.01))
    softer = jnp.log(1.0 + jnp.exp(logx))
    root = jnp.exp(-0.5 * expo * softer)
    gap = 1.0 - jnp.exp(expo * (logx - softer))
    return root * root, half_ks * root * (gap * gap)


def expo_of(half_n):
    return 1.0 - 0.5 / half_n


def z_faces(h, a, n, s, p, out_e, out_o, hb, ab, nb, sb, pb, sem):
    copies = []
    for side in range(2):
        for src, dst, count in ((h, hb, 4), (a, ab, 3), (n, nb, 3), (s, sb, 3), (p, pb, 1)):
            start = 0 if side == 0 else LEVELS - count
            copy = pltpu.make_async_copy(src.at[pl.ds(start, count)], dst.at[side], sem.at[len(copies)])
            copy.start()
            copies.append(copy)
    for copy in copies:
        copy.wait()

    def put(out, side):
        def level(buf, count, dist):
            return buf[side, dist - 1 if side == 0 else count - dist]

        for dist in (1, 2, 3):
            out[dist - 1] = level(hb, 4, dist)
        for dist in (1, 2):
            alpha = level(ab, 3, dist)
            out[2 + dist] = alpha * alpha
            out[4 + dist] = 0.5 * level(nb, 3, dist)
            out[6 + dist] = 0.5 * level(sb, 3, dist)
        out[9] = level(pb, 1, 1)
        alpha = level(ab, 3, 3)
        half_n = 0.5 * level(nb, 3, 3)
        out[10] = curves(level(hb, 4, 3), alpha * alpha, half_n, 0.5 * level(sb, 3, 3), expo_of(half_n))[1]
        out[11] = (hb[side, 0] + hb[side, 1] + hb[side, 2] + hb[side, 3]) * 0.25

    even = is_even("gz")

    @pl.when(even)
    def _():
        put(out_e, 1)
        put(out_o, 0)

    @pl.when(jnp.logical_not(even))
    def _():
        put(out_e, 0)
        put(out_o, 1)


def rank_rows(owners, counts, groups, visit):
    def clear(i, carry):
        counts[i] = 0
        return carry

    def step(x, carry):
        owner = owners[x]

        @pl.when(owner >= 0)
        def _():
            rank = counts[owner]
            counts[owner] = rank + 1
            visit(x, owner, rank)

        return carry

    lax.fori_loop(0, groups, clear, 0)
    lax.fori_loop(0, ROWS, step, 0)


def land_pack(count_gx, count_gz, owners, h, a, n, s, p, tr, rt, y, t, planes, means, counts, slots):
    groups = count_gx * count_gz
    me_gx = place("gx")
    me = me_gx * count_gz + place("gz")

    def clear(i, carry):
        slots[i] = -1
        return carry

    lax.fori_loop(0, groups * CAP, clear, 0)

    def visit(x, owner, rank):
        slots[owner * CAP + rank] = x

    rank_rows(owners, counts, groups, visit)
    for layer in range(LAYERS_PER_BLOCK):
        saturs = []
        heads = []
        for level in range(layer * LEVELS_PER_LAYER, (layer + 1) * LEVELS_PER_LAYER):
            head = h[level]
            alpha = a[level]
            half_n = 0.5 * n[level]
            logx = half_n * jnp.log(alpha * alpha * (head * head + 0.01))
            softer = jnp.log(1.0 + jnp.exp(logx))
            saturs.append(jnp.exp(-expo_of(half_n) * softer))
            heads.append(head)
        means[layer] = (saturs[0] + saturs[1] + saturs[2] + saturs[3]) * 0.25
        means[LAYERS_PER_BLOCK + layer] = (heads[0] + heads[1] + heads[2] + heads[3]) * 0.25
    for j in range(groups):
        for c in range(CAP):
            row = slots[(me ^ j) * CAP + c]
            safe = jnp.maximum(row, 0)
            for q in range(8):
                value = means[q, pl.ds(safe, 1), :]
                y[j, pl.ds(c * 8 + q, 1), :] = jnp.where(row >= 0, value, -1.0)
    for j in range(count_gx):
        block = me_gx ^ j
        t[j] = jnp.zeros((8, COLS), jnp.float32)
        for c in range(CAP):
            t[j, pl.ds(2 * c, 1), :] = tr[pl.ds(block * CAP + c, 1), :]
            t[j, pl.ds(2 * c + 1, 1), :] = rt[pl.ds(block * CAP + c, 1), :].astype(jnp.float32)
    for level in range(LEVELS):
        planes[H0 + HALO + level] = h[level]
        alpha = a[level]
        planes[A0 + HALO - 1 + level] = alpha * alpha
        planes[N0 + HALO - 1 + level] = 0.5 * n[level]
        planes[S0 + HALO - 1 + level] = 0.5 * s[level]
        planes[P0 + HALO - 2 + level] = p[level]


def tile_values(count_gz, groups, owners, t, out, counts):
    me = place("gx") * count_gz + place("gz")
    out[0] = jnp.zeros((ROWS, COLS), jnp.float32)
    out[1] = jnp.ones((ROWS, COLS), jnp.float32)

    def visit(x, owner, rank):
        j = me ^ owner
        out[0, pl.ds(x, 1), :] = t[j, pl.ds(2 * rank, 1), :]
        out[1, pl.ds(x, 1), :] = t[j, pl.ds(2 * rank + 1, 1), :]

    rank_rows(owners, counts, groups, visit)


def x_faces(count_gx, planes_in, z_e, z_o, tile, planes, *sends):
    def take(got, low):
        for dist in (1, 2, 3):
            planes[H0 + (HALO - dist if low else HALO + LEVELS - 1 + dist)] = got[dist - 1]
        for dist in (1, 2):
            off = HALO - 1 - dist if low else HALO - 2 + LEVELS + dist
            planes[A0 + off] = got[2 + dist]
            planes[N0 + off] = got[4 + dist]
            planes[S0 + off] = got[6 + dist]
        planes[P0 + (0 if low else NP - 1)] = got[9]
        planes[K_LO if low else K_HI] = got[10]
        planes[M_LO if low else M_HI] = got[11]

    even_z = is_even("gz")

    @pl.when(even_z)
    def _():
        take(z_e, False)
        take(z_o, True)

    @pl.when(jnp.logical_not(even_z))
    def _():
        take(z_e, True)
        take(z_o, False)

    planes[TP] = tile[0]
    planes[RT] = tile[1]

    def put(send, last):
        start = ROWS - HALO if last else 0
        for p in range(PLANES):
            send[p, pl.ds(0, HALO), :] = planes[p, pl.ds(start, HALO), :]

    even_x = is_even("gx")

    @pl.when(even_x)
    def _():
        put(sends[0], True)
        if count_gx > 2:
            put(sends[1], False)

    @pl.when(jnp.logical_not(even_x))
    def _():
        put(sends[0], False)
        if count_gx > 2:
            put(sends[1], True)


def y_faces(count_gx, *refs):
    planes = refs[0]
    if count_gx > 2:
        got_e, got_o = refs[1], refs[2]
    else:
        got_e, got_o = refs[1], None
    edge, strips, send_e, send_o = refs[-4:]

    def take(high, low):
        for p in range(PLANES):
            edge[p] = planes[p, ROWS - EDGE : ROWS]
            if high is not None:
                edge[p, pl.ds(0, HALO), :] = high[p, pl.ds(0, HALO), :]
            if low is not None:
                edge[p, pl.ds(EDGE - HALO, HALO), :] = low[p, pl.ds(0, HALO), :]

    even_x = is_even("gx")

    @pl.when(even_x)
    def _():
        take(got_e, got_o)

    @pl.when(jnp.logical_not(even_x))
    def _():
        take(got_o, got_e)

    lane_group = lax.broadcasted_iota(jnp.int32, (WIDE, COLS), 1) // SIDE

    def pack(t, carry):
        acc = jnp.zeros((WIDE, COLS), jnp.float32)
        for j in range(8):
            p = jnp.minimum(t * 8 + j, PLANES - 1)
            value = jnp.concatenate([planes[p], edge[p]], axis=0)
            acc = jnp.where(lane_group == j, pltpu.roll(value, SIDE * j + 8, 1), acc)
        full = jnp.concatenate([acc] + [acc[ROWS:WIDE]] * ((COLS - WIDE) // EDGE), axis=0)
        strips[pl.ds(pl.multiple_of(t * COLS, COLS), COLS), :] = full.T
        return carry

    lax.fori_loop(0, PACKS, pack, 0)

    def put(send, last):
        start = 5 if last else 8
        for p in range(PLANES):
            send[pl.ds(p * HALO, HALO), :] = strips[pl.ds(p * SIDE + start, HALO), :]
        rest = Y_SEND - PLANES * HALO
        if rest:
            send[pl.ds(PLANES * HALO, rest), :] = jnp.zeros((rest, COLS), jnp.float32)

    even_y = is_even("role")

    @pl.when(even_y)
    def _():
        put(send_e, True)
        put(send_o, False)

    @pl.when(jnp.logical_not(even_y))
    def _():
        put(send_e, False)
        put(send_o, True)


def uptake_of(tpot, roots, head, layers, base_exp, first):
    total = jnp.zeros_like(tpot)
    for layer in range(layers):
        total = total + jnp.where(roots > float(layer), math.exp(-layer / 4.0), 0.0)
    share = tpot * base_exp / total
    result = []
    for q in range(LAYERS_PER_BLOCK + 2):
        depth = (first + (q - 1)).astype(jnp.float32)
        weight = jnp.where(depth < roots, math.exp(-(q - 1) / 4.0) * share, 0.0)
        result.append(weight / (1.0 + head[q] * head[q] * (1.0 / 2.25)))
    return result


def sweeps(count_role, count_gx, count_gz, planes, edge, strips_in, y_e, y_o, out,
           strips, ha, hb, kc, mm, th, wd, sk, xmask,
           sa, sb, sc, ks, sm, sth, swd, ssk, turn):
    me_role, me_gx, me_gz = place("role"), place("gx"), place("gz")
    layers = LAYERS_PER_BLOCK * count_gz
    first = me_gz * LAYERS_PER_BLOCK
    f32 = jnp.float32
    z_top = jnp.where(me_gz == 0, 0.0, 1.0).astype(f32)
    z_bottom = jnp.where(me_gz == count_gz - 1, 0.0, 1.0).astype(f32)
    x_first = jnp.where(me_gx == 0, 0.0, 1.0).astype(f32)
    x_last = jnp.where(me_gx == count_gx - 1, 0.0, 1.0).astype(f32)
    y_first = jnp.where(me_role == 0, 0.0, 1.0).astype(f32)
    y_last = jnp.where(me_role == count_role - 1, 0.0, 1.0).astype(f32)
    exp_first = jnp.exp(jnp.zeros((8, COLS), f32) - me_gz.astype(f32))

    strips[...] = strips_in[...]

    def take(high, low):
        for p in range(PLANES):
            strips[pl.ds(p * SIDE, HALO), :] = high[pl.ds(p * HALO, HALO), :]
            strips[pl.ds(p * SIDE + SIDE - HALO, HALO), :] = low[pl.ds(p * HALO, HALO), :]

    even_y = is_even("role")

    @pl.when(even_y)
    def _():
        take(y_e, y_o)

    @pl.when(jnp.logical_not(even_y))
    def _():
        take(y_o, y_e)

    def wide(p):
        return jnp.concatenate([planes[p], edge[p]], axis=0)

    def put(ref, i, value):
        ref[i, 8 : 8 + WIDE] = value
        ref[i, 0:8] = value[ROWS:WIDE]
        ref[i, 8 + WIDE : 16 + WIDE] = value[0:8]

    row = lax.broadcasted_iota(jnp.int32, (WIDE, COLS), 0)
    xmask[0] = jnp.where(row == 0, x_first, 1.0)
    xmask[1] = jnp.where(row == ROWS - 1, x_last, 1.0)

    def fill(i, carry):
        put(ha, i, wide(H0 + i))
        return carry

    lax.fori_loop(0, NH, fill, 0)
    put(kc, 0, wide(K_LO))
    put(kc, NH - 1, wide(K_HI))

    def mean4(ref, i):
        return (ref[i, 8 : 8 + WIDE] + ref[i + 1, 8 : 8 + WIDE] + ref[i + 2, 8 : 8 + WIDE] + ref[i + 3, 8 : 8 + WIDE]) * 0.25

    heads = [wide(M_LO)] + [mean4(ha, HALO + 4 * q) for q in range(LAYERS_PER_BLOCK)] + [wide(M_HI)]
    base = jnp.concatenate([exp_first] * (WIDE // 8), axis=0)
    for q, value in enumerate(uptake_of(wide(TP), wide(RT), heads, layers, base, first)):
        sk[q] = value

    def strip(p, count=1):
        return strips[p * SIDE : (p + count) * SIDE, :]

    heads = [strip(M_LO)]
    for q in range(LAYERS_PER_BLOCK):
        at = H0 + HALO + 4 * q
        heads.append((strip(at) + strip(at + 1) + strip(at + 2) + strip(at + 3)) * 0.25)
    heads.append(strip(M_HI))
    base = jnp.concatenate([exp_first] * 2, axis=0)
    for q, value in enumerate(uptake_of(strip(TP), strip(RT), heads, layers, base, first)):
        ssk[q * SIDE : (q + 1) * SIDE, :] = value

    def first_curves(j, theta):
        i = j + 1
        half_n = wide(N0 + j)
        expo = expo_of(half_n)
        mm[j] = expo
        satur, cond = curves(ha[i, 8 : 8 + WIDE], wide(A0 + j), half_n, wide(S0 + j), expo)
        put(kc, i, cond)
        if theta:
            th[j - 1] = wide(P0 + j - 1) * satur

    def later_curves(src, j, water):
        i = j + 1
        satur, cond = curves(src[i, 8 : 8 + WIDE], wide(A0 + j), wide(N0 + j), wide(S0 + j), mm[j])
        put(kc, i, cond)
        if water:
            wd[j - 1] = wide(P0 + j - 1) * satur - th[j - 1]

    def stencil(src, i, sweep):
        here = pl.ds(8, WIDE)
        head, cond = src[i, here, :], kc[i, here, :]
        mask_up = jnp.where(i == HALO, z_top, 1.0)
        mask_down = jnp.where(i == HALO + LEVELS - 1, z_bottom, 1.0)
        kf_up = (cond + kc[i - 1, here, :]) * mask_up
        kf_down = (cond + kc[i + 1, here, :]) * mask_down
        kf_xm = (cond + kc[i, pl.ds(7, WIDE), :]) * xmask[0]
        kf_xp = (cond + kc[i, pl.ds(9, WIDE), :]) * xmask[1]
        kf_ym = cond + pltpu.roll(cond, 1, 1)
        kf_yp = cond + pltpu.roll(cond, COLS - 1, 1)
        flux = kf_up * (head - src[i - 1, here, :]) + kf_down * (head - src[i + 1, here, :])
        flux = flux + kf_xm * (head - src[i, pl.ds(7, WIDE), :]) + kf_xp * (head - src[i, pl.ds(9, WIDE), :])
        flux = flux + kf_ym * (head - pltpu.roll(head, 1, 1)) + kf_yp * (head - pltpu.roll(head, COLS - 1, 1))
        resid = flux + (kf_down - kf_up) + sk[(i + 1) // LEVELS_PER_LAYER]
        if sweep > 0:
            resid = resid + wd[i - 2]
        diag = 1.0 + (kf_up + kf_down + kf_xm + kf_xp + kf_ym + kf_yp)
        return head - omega(sweep) * resid / diag

    def loop(lo, hi, body):
        def step(i, carry):
            body(i)
            return carry

        lax.fori_loop(lo, hi, step, 0)

    first_curves(0, False)
    loop(1, NC - 1, lambda j: first_curves(j, True))
    first_curves(NC - 1, False)
    loop(1, NH - 1, lambda i: put(hb, i, stencil(ha, i, 0)))

    lane = lax.broadcasted_iota(jnp.int32, (SIDE, COLS), 1)
    srow = lax.broadcasted_iota(jnp.int32, (SIDE, COLS), 0)
    s_xm = jnp.where(lane == 0, x_first, 1.0)
    s_xp = jnp.where(lane == ROWS - 1, x_last, 1.0)
    side_mask = jnp.where(srow < 8, y_last, y_first)
    s_ym = jnp.where(srow % 8 == 0, side_mask, 1.0)
    s_yp = jnp.where(srow % 8 == 7, side_mask, 1.0)

    def tiled(mask, count):
        return jnp.concatenate([mask] * count, axis=0)

    def y_shift(value, by):
        parts = value.reshape(value.shape[0] // 8, 8, COLS)
        return pltpu.roll(parts, by, 1).reshape(value.shape)

    def rows_of(i, count):
        return slice(i * SIDE, (i + count) * SIDE)

    def strip_curves(src, lo, hi, sweep):
        i = lo
        while i < hi:
            count = min(5, hi - i)
            j = i - 1
            here = rows_of(i, count)
            half_n = strip(N0 + j, count)
            if sweep == 0:
                expo = expo_of(half_n)
                sm[rows_of(j, count), :] = expo
            else:
                expo = sm[rows_of(j, count), :]
            satur, cond = curves(src[here, :], strip(A0 + j, count), half_n, strip(S0 + j, count), expo)
            ks[here, :] = cond
            start, stop = max(i, 2), min(i + count, NH - 2)
            if stop > start:
                part = satur[(start - i) * SIDE : (stop - i) * SIDE]
                water = strip(P0 + start - 2, stop - start) * part
                at = rows_of(start - 2, stop - start)
                if sweep == 0:
                    sth[at, :] = water
                else:
                    swd[at, :] = water - sth[at, :]
            i += count

    def strip_stencil(src, dst, lo, hi, sweep):
        i = lo
        while i < hi:
            count = min(5, hi - i)
            here = rows_of(i, count)
            above, below = rows_of(i - 1, count), rows_of(i + 1, count)
            head, cond = src[here, :], ks[here, :]
            kf_up = cond + ks[above, :]
            kf_down = cond + ks[below, :]
            if i <= HALO < i + count:
                level = lax.broadcasted_iota(jnp.int32, kf_up.shape, 0) // SIDE
                kf_up = jnp.where(level == HALO - i, kf_up * z_top, kf_up)
            if i <= HALO + LEVELS - 1 < i + count:
                level = lax.broadcasted_iota(jnp.int32, kf_up.shape, 0) // SIDE
                kf_down = jnp.where(level == HALO + LEVELS - 1 - i, kf_down * z_bottom, kf_down)
            kf_xm = (cond + pltpu.roll(cond, 1, 1)) * tiled(s_xm, count)
            kf_xp = (cond + pltpu.roll(cond, COLS - 1, 1)) * tiled(s_xp, count)
            kf_ym = (cond + y_shift(cond, 1)) * tiled(s_ym, count)
            kf_yp = (cond + y_shift(cond, 7)) * tiled(s_yp, count)
            flux = kf_up * (head - src[above, :]) + kf_down * (head - src[below, :])
            flux = flux + kf_xm * (head - pltpu.roll(head, 1, 1)) + kf_xp * (head - pltpu.roll(head, COLS - 1, 1))
            flux = flux + kf_ym * (head - y_shift(head, 1)) + kf_yp * (head - y_shift(head, 7))
            sink = jnp.concatenate([ssk[rows_of((k + 1) // LEVELS_PER_LAYER, 1), :] for k in range(i, i + count)], axis=0)
            resid = flux + (kf_down - kf_up) + sink
            if sweep > 0:
                resid = resid + swd[rows_of(i - 2, count), :]
            diag = 1.0 + (kf_up + kf_down + kf_xm + kf_xp + kf_ym + kf_yp)
            dst[here, :] = head - omega(sweep) * resid / diag
            i += count

    ks[rows_of(0, 1), :] = strip(K_LO)
    ks[rows_of(NH - 1, 1), :] = strip(K_HI)
    strip_curves(strips, 1, NH - 1, 0)
    strip_stencil(strips, sa, 1, NH - 1, 0)
    strip_curves(sa, 1, NH - 1, 1)
    strip_stencil(sa, sb, 2, NH - 2, 1)
    strip_curves(sb, 2, NH - 2, 2)
    strip_stencil(sb, sc, 3, NH - 3, 2)

    lane_wide = lax.broadcasted_iota(jnp.int32, (WIDE, COLS), 1)
    low_rows = lax.broadcasted_iota(jnp.int32, (EDGE, COLS), 0) >= EDGE - HALO

    def turned(pieces):
        rows = sum(piece.shape[0] for piece in pieces)
        full = jnp.concatenate(pieces + [jnp.zeros((COLS - rows, COLS), f32)], axis=0).T
        last = jnp.where(low_rows, full[COLS - EDGE : COLS], full[ROWS:WIDE])
        return jnp.concatenate([full[0:ROWS], last], axis=0)

    turn[...] = turned([sa[i * SIDE + 7 : i * SIDE + 9, :] for i in range(1, NH - 1)])
    outer = (lane_wide == 0) | (lane_wide == COLS - 1)
    for i in range(1, NH - 1):
        moved = pltpu.roll(turn[...], (COLS - 1 - 2 * (i - 1)) % COLS, 1)
        put(hb, i, jnp.where(outer, moved, hb[i, 8 : 8 + WIDE]))

    loop(0, 1, lambda j: later_curves(hb, j, False))
    loop(1, NC - 1, lambda j: later_curves(hb, j, True))
    loop(NC - 1, NC, lambda j: later_curves(hb, j, False))
    loop(2, NH - 2, lambda i: put(ha, i, stencil(hb, i, 1)))
    loop(1, NC - 1, lambda j: later_curves(ha, j, True))

    turn[...] = turned([sc[i * SIDE + 6 : i * SIDE + 10, :] for i in range(HALO, HALO + LEVELS)])
    outer = ((lane_wide < 2) | (lane_wide >= COLS - 2))[0:ROWS]
    loop(HALO, HALO + LEVELS, lambda i: put(hb, i, stencil(ha, i, 2)))
    for level in range(LEVELS):
        moved = pltpu.roll(turn[0:ROWS], (COLS - 2 - 4 * level) % COLS, 1)
        out[level] = jnp.where(outer, moved, hb[HALO + level, 8 : 8 + ROWS])


def heat(count_gx, count_gz, y, temp, tr, air, rt, out, sat, head):
    me = place("gx") * count_gz + place("gz")
    layers = LAYERS_PER_BLOCK * count_gz
    for gx in range(count_gx):
        for gz in range(count_gz):
            j = me ^ (gx * count_gz + gz)
            for c in range(CAP):
                tile = y[j, c * 8 : c * 8 + 8]
                at = pl.ds(gz * LAYERS_PER_BLOCK, LAYERS_PER_BLOCK)
                sat[gx * CAP + c, at, :] = tile[0:LAYERS_PER_BLOCK]
                head[gx * CAP + c, at, :] = tile[LAYERS_PER_BLOCK : 2 * LAYERS_PER_BLOCK]
    layer = lax.broadcasted_iota(jnp.int32, (layers, COLS), 0)
    decay = jnp.exp(layer.astype(jnp.float32) * -0.25)
    for slot in range(count_gx * CAP):
        roots = jnp.broadcast_to(rt[pl.ds(slot, 1), :], (layers, COLS))
        weight = jnp.where(layer < roots, decay, 0.0)
        weight = weight / jnp.sum(weight, axis=0, keepdims=True)
        stress = 1.0 / (1.0 + head[slot] * head[slot] * (1.0 / 2.25))
        uptake = tr[pl.ds(slot, 1), :] * weight * stress
        kappa = 0.25 + 0.9 * sat[slot]
        top = jnp.broadcast_to(air[pl.ds(slot, 1), :], (layers, COLS))
        k_above = jnp.where(layer == 0, kappa, 0.5 * (kappa + pltpu.roll(kappa, 1, 0)))
        k_below = jnp.where(layer == layers - 1, 0.0, 0.5 * (kappa + pltpu.roll(kappa, layers - 1, 0)))
        old = temp[slot]
        new = old
        for _ in range(HEAT_STEPS):
            above = jnp.where(layer == 0, top, pltpu.roll(new, 1, 0))
            below = pltpu.roll(new, layers - 1, 0)
            new = new + 0.2 * (k_above * (above - new) + k_below * (below - new)) - 0.3 * uptake
        out[slot] = jnp.where(sat[slot] >= 0.0, new, old)


def call(body, outs, ins, scratch=(), aliases=None):
    return pl.pallas_call(
        body,
        out_shape=[jax.ShapeDtypeStruct(shape, jnp.float32) for shape in outs],
        in_specs=ins,
        out_specs=[VMEM] * len(outs),
        scratch_shapes=list(scratch),
        input_output_aliases=aliases or {},
        compiler_params=PARAMS,
    )


def local(h, a, n, s, p, tile_owner, land_temp, tr, air, rt):
    sizes = tuple(lax.axis_size(axis) for axis in AXES)
    count_role, count_gx, count_gz = sizes
    groups = count_gx * count_gz
    slots = count_gx * CAP
    f32 = jnp.float32

    def swap(value, axis, odd):
        return lax.ppermute(value, AXES, pairing(sizes, axis, odd))

    owners = lax.dynamic_slice(tile_owner, (place("gx") * ROWS, place("role")), (ROWS, 1))[:, 0]
    land_temp, tr, air, rt = land_temp[0, 0], tr[0, 0], air[0, 0], rt[0, 0]

    z_send_e, z_send_o = call(
        z_faces,
        [(Z_SEND, ROWS, COLS)] * 2,
        [ANY] * 5,
        [
            pltpu.VMEM((2, 4, ROWS, COLS), f32),
            pltpu.VMEM((2, 3, ROWS, COLS), f32),
            pltpu.VMEM((2, 3, ROWS, COLS), f32),
            pltpu.VMEM((2, 3, ROWS, COLS), f32),
            pltpu.VMEM((2, 1, ROWS, COLS), f32),
            pltpu.SemaphoreType.DMA((10,)),
        ],
    )(h, a, n, s, p)
    z_e = swap(z_send_e, "gz", False)
    z_o = swap(z_send_o, "gz", True) if count_gz > 2 else z_e

    y, t, planes = call(
        functools.partial(land_pack, count_gx, count_gz),
        [(groups, 8 * CAP, COLS), (count_gx, 8, COLS), (PLANES, ROWS, COLS)],
        [SMEM] + [VMEM] * 7,
        [
            pltpu.VMEM((2 * LAYERS_PER_BLOCK, ROWS, COLS), f32),
            pltpu.SMEM((groups,), jnp.int32),
            pltpu.SMEM((groups * CAP,), jnp.int32),
        ],
    )(owners, h, a, n, s, p, tr, rt)

    pieces = [y[j] for j in range(groups)]
    values = {j * count_gz: t[j] for j in range(count_gx)}
    bit = groups // 2
    while bit:
        axis, step = ("gx", bit // count_gz) if bit >= count_gz else ("gz", bit)
        moving = [j for j in range(groups) if j & bit]
        if axis == "gx":
            t_moving = [j for j in values if j & bit]
        else:
            t_moving = sorted(values)
        sent = jnp.concatenate([pieces[j] for j in moving] + [values[j] for j in t_moving], axis=0)
        got = lax.ppermute(sent, AXES, xor_pairs(sizes, axis, step))
        at = 0
        for j in moving:
            pieces[j] = got[at : at + 8 * CAP]
            at += 8 * CAP
        for j in t_moving:
            values[j | bit] = got[at : at + 8]
            at += 8
        bit //= 2
    y = jnp.stack(pieces)
    t = jnp.stack([values[j] for j in range(groups)])

    (tile,) = call(
        functools.partial(tile_values, count_gz, groups),
        [(2, ROWS, COLS)],
        [SMEM, VMEM],
        [pltpu.SMEM((groups,), jnp.int32)],
    )(owners, t)

    x_count = 1 if count_gx == 2 else 2
    planes, *x_sends = call(
        functools.partial(x_faces, count_gx),
        [(PLANES, ROWS, COLS)] + [(PLANES, 4, COLS)] * x_count,
        [VMEM] * 4,
        aliases={0: 0},
    )(planes, z_e, z_o, tile)
    x_got = [swap(value, "gx", bool(k)) for k, value in enumerate(x_sends)]

    edge, strips, y_send_e, y_send_o = call(
        functools.partial(y_faces, count_gx),
        [(PLANES, EDGE, COLS), (PACKS * COLS, COLS), (Y_SEND, COLS), (Y_SEND, COLS)],
        [VMEM] * (1 + x_count),
    )(planes, *x_got)
    y_e = swap(y_send_e, "role", False)
    y_o = swap(y_send_o, "role", True) if count_role > 2 else y_e

    (land_new,) = call(
        functools.partial(heat, count_gx, count_gz),
        [(slots, LAYERS_PER_BLOCK * count_gz, COLS)],
        [VMEM] * 5,
        [pltpu.VMEM((slots, LAYERS_PER_BLOCK * count_gz, COLS), f32)] * 2,
    )(y, land_temp, tr, air, rt)

    deep = WIDE + 16
    (head,) = call(
        functools.partial(sweeps, count_role, count_gx, count_gz),
        [(LEVELS, ROWS, COLS)],
        [VMEM] * 5,
        [
            pltpu.VMEM((PACKS * COLS, COLS), f32),
            pltpu.VMEM((NH, deep, COLS), f32),
            pltpu.VMEM((NH, deep, COLS), f32),
            pltpu.VMEM((NH, deep, COLS), f32),
            pltpu.VMEM((NC, WIDE, COLS), f32),
            pltpu.VMEM((NP, WIDE, COLS), f32),
            pltpu.VMEM((NP, WIDE, COLS), f32),
            pltpu.VMEM((LAYERS_PER_BLOCK + 2, WIDE, COLS), f32),
            pltpu.VMEM((2, WIDE, COLS), f32),
            pltpu.VMEM((NH * SIDE, COLS), f32),
            pltpu.VMEM((NH * SIDE, COLS), f32),
            pltpu.VMEM((NH * SIDE, COLS), f32),
            pltpu.VMEM((NH * SIDE, COLS), f32),
            pltpu.VMEM((NC * SIDE, COLS), f32),
            pltpu.VMEM((NP * SIDE, COLS), f32),
            pltpu.VMEM((NP * SIDE, COLS), f32),
            pltpu.VMEM(((LAYERS_PER_BLOCK + 2) * SIDE, COLS), f32),
            pltpu.VMEM((WIDE, COLS), f32),
        ],
    )(planes, edge, strips, y_e, y_o)
    return (head, land_new[None, None])


def solution(mesh):
    in_specs = (
        P("gz", "gx", "role"),
        P("gz", "gx", "role"),
        P("gz", "gx", "role"),
        P("gz", "gx", "role"),
        P("gz", "gx", "role"),
        P(),
        P("role", ("gx", "gz"), None, None, None),
        P("role", ("gx", "gz"), None, None),
        P("role", ("gx", "gz"), None, None),
        P("role", ("gx", "gz"), None, None),
    )
    out_specs = (P("gz", "gx", "role"), P("role", ("gx", "gz"), None, None, None))
    return jax.shard_map(local, mesh=mesh, in_specs=in_specs, out_specs=out_specs, check_vma=False)
```

```python
import functools
import math

import jax
import jax.numpy as jnp
from jax import lax
from jax.experimental import pallas as pl
from jax.experimental.pallas import tpu as pltpu
from jax.sharding import PartitionSpec as P

LAYERS_PER_BLOCK = 4
LEVELS_PER_LAYER = 4
CAP = 3
SWEEPS = 3
HEAT_STEPS = 4
HALO = SWEEPS
AXES = ("role", "gx", "gz")
VMEM = pl.BlockSpec(memory_space=pltpu.VMEM)
SMEM = pl.BlockSpec(memory_space=pltpu.SMEM)
HBM = pl.BlockSpec(memory_space=pltpu.HBM)
MIB = 1024 * 1024

LEVELS = 16
ROWS = 64
COLS = 128
EDGE = 8
WIDE = ROWS + EDGE
H0 = 0
NH = LEVELS + 2 * HALO
A0 = H0 + NH
NC = LEVELS + 2 * HALO - 2
N0 = A0 + NC
S0 = N0 + NC
K_LO = S0 + NC
K_HI = K_LO + 1
P0 = K_HI + 1
NP = LEVELS + 2 * HALO - 4
M_LO = P0 + NP
M_HI = M_LO + 1
TP = M_HI + 1
RT = TP + 1
PLANES = RT + 1
PACKS = (PLANES + 7) // 8
SIDE = 16
Z_SEND = 12
PIECE = 8 * CAP
Y_SEND = (PLANES * HALO + 7) // 8 * 8


def omega(sweep):
    return 1.0 / (1.0 + 0.6 * math.cos(math.pi * (2 * sweep + 1) / (2 * SWEEPS)))


def place(axis):
    return lax.axis_index(axis)


def is_even(axis):
    return lax.rem(place(axis), 2) == 0


def pairing(sizes, axis, odd):
    pairs = []
    which = AXES.index(axis)
    for index in range(math.prod(sizes)):
        at = [index // (sizes[1] * sizes[2]), index // sizes[2] % sizes[1], index % sizes[2]]
        count = sizes[which]
        there = list(at)
        if not odd:
            there[which] = at[which] ^ 1
        else:
            there[which] = at[which] + (1 if at[which] % 2 else -1)
            if not 0 <= there[which] < count:
                there = list(at)
                if axis == "gx":
                    there[1] = count - 1 - at[1]
                else:
                    there[1] = at[1] ^ 1
        pairs.append((index, (there[0] * sizes[1] + there[1]) * sizes[2] + there[2]))
    return pairs


def xor_pairs(sizes, axis, bit):
    pairs = []
    which = AXES.index(axis)
    for index in range(math.prod(sizes)):
        at = [index // (sizes[1] * sizes[2]), index // sizes[2] % sizes[1], index % sizes[2]]
        at[which] ^= bit
        pairs.append((index, (at[0] * sizes[1] + at[1]) * sizes[2] + at[2]))
    return pairs


def curves(head, alpha2, half_n, half_ks, expo):
    logx = half_n * jnp.log(alpha2 * (head * head + 0.01))
    softer = jnp.log(1.0 + jnp.exp(logx))
    root = jnp.exp(-0.5 * expo * softer)
    gap = 1.0 - jnp.exp(expo * (logx - softer))
    return root * root, half_ks * root * (gap * gap)


def inverse(value):
    guess = pl.reciprocal(value, approx=True)
    return guess * (2.0 - value * guess)


def expo_of(half_n):
    return 1.0 - 0.5 * inverse(half_n)


def relax(head, inflow, diag, sweep):
    step = omega(sweep)
    return (1.0 - step) * head + (step * (head + inflow)) * inverse(diag)


def z_faces(h, a, n, s, p, out_e, out_o, hb, ab, nb, sb, pb, sem):
    copies = []
    for side in range(2):
        for src, dst, count in ((h, hb, 4), (a, ab, 3), (n, nb, 3), (s, sb, 3), (p, pb, 1)):
            start = 0 if side == 0 else LEVELS - count
            copy = pltpu.make_async_copy(src.at[pl.ds(start, count)], dst.at[side], sem.at[len(copies)])
            copy.start()
            copies.append(copy)
    for copy in copies:
        copy.wait()

    def put(out, side):
        def level(buf, count, dist):
            return buf[side, dist - 1 if side == 0 else count - dist]

        for dist in (1, 2, 3):
            out[dist - 1] = level(hb, 4, dist)
        for dist in (1, 2):
            alpha = level(ab, 3, dist)
            out[2 + dist] = alpha * alpha
            out[4 + dist] = 0.5 * level(nb, 3, dist)
            out[6 + dist] = 0.5 * level(sb, 3, dist)
        out[9] = level(pb, 1, 1)
        alpha = level(ab, 3, 3)
        half_n = 0.5 * level(nb, 3, 3)
        out[10] = curves(level(hb, 4, 3), alpha * alpha, half_n, 0.5 * level(sb, 3, 3), expo_of(half_n))[1]
        out[11] = (hb[side, 0] + hb[side, 1] + hb[side, 2] + hb[side, 3]) * 0.25

    even = is_even("gz")

    @pl.when(even)
    def _():
        put(out_e, 1)
        put(out_o, 0)

    @pl.when(jnp.logical_not(even))
    def _():
        put(out_e, 0)
        put(out_o, 1)


def land_pack(count_gx, count_gz, owners, h_in, a_in, n_in, tr_in, rt_in, send, keep, hot,
              means, counts, slots, h, a, n, tr, rt, sem):
    groups = count_gx * count_gz
    me_role, me_gx = place("role"), place("gx")
    me = me_gx * count_gz + place("gz")
    copies = []
    for src, dst in ((h_in, h), (a_in, a), (n_in, n), (tr_in, tr), (rt_in, rt)):
        copy = pltpu.make_async_copy(src, dst, sem.at[len(copies)])
        copy.start()
        copies.append(copy)

    def clear_slot(i, carry):
        slots[i] = -1
        return carry

    def clear_count(i, carry):
        counts[i] = 0
        return carry

    lax.fori_loop(0, groups * CAP, clear_slot, 0)
    lax.fori_loop(0, groups, clear_count, 0)
    lane = lax.broadcasted_iota(jnp.int32, (1, groups * 8), 1)

    def step(x, carry):
        owner = owners[me_role, me_gx * ROWS + x]
        safe = jnp.maximum(owner, 0)
        rank = counts[safe]
        at = jnp.where(owner >= 0, (me ^ owner) * 8 + 2 * rank, -1)
        hot[pl.ds(x, 1), :] = jnp.where(lane == at, 1.0, 0.0)

        @pl.when(owner >= 0)
        def _():
            counts[owner] = rank + 1
            slots[owner * CAP + rank] = x

        return carry

    lax.fori_loop(0, ROWS, step, 0)
    for copy in copies:
        copy.wait()
    for layer in range(LAYERS_PER_BLOCK):
        saturs = []
        heads = []
        for level in range(layer * LEVELS_PER_LAYER, (layer + 1) * LEVELS_PER_LAYER):
            head = h[level]
            alpha = a[level]
            half_n = 0.5 * n[level]
            logx = half_n * jnp.log(alpha * alpha * (head * head + 0.01))
            softer = jnp.log(1.0 + jnp.exp(logx))
            saturs.append(jnp.exp(-expo_of(half_n) * softer))
            heads.append(head)
        means[layer] = (saturs[0] + saturs[1] + saturs[2] + saturs[3]) * 0.25
        means[LAYERS_PER_BLOCK + layer] = (heads[0] + heads[1] + heads[2] + heads[3]) * 0.25
    half = groups // 2
    for j in range(groups):
        out, k = (keep, j) if j < half else (send, j - half)
        for c in range(CAP):
            row = slots[(me ^ j) * CAP + c]
            safe = jnp.maximum(row, 0)
            for q in range(8):
                value = means[q, pl.ds(safe, 1), :]
                out[pl.ds(k * PIECE + c * 8 + q, 1), :] = jnp.where(row >= 0, value, -1.0)
    blocks = count_gx // 2
    for j in range(count_gx):
        block = me_gx ^ j
        out, k = (keep, j) if j < blocks else (send, j - blocks)
        base = half * PIECE + k * 8
        out[pl.ds(base, 8), :] = jnp.zeros((8, COLS), jnp.float32)
        for c in range(CAP):
            out[pl.ds(base + 2 * c, 1), :] = tr[block * CAP + c]
            out[pl.ds(base + 2 * c + 1, 1), :] = rt[block * CAP + c].astype(jnp.float32)


def land_sort(count_gx, count_gz, keep, got, *outs):
    half, blocks = count_gx * count_gz // 2, count_gx // 2
    for gx in range(count_gx):
        src, k = (keep, gx) if gx < blocks else (got, gx - blocks)
        for dist in range(count_gz):
            at = (k * count_gz + dist) * PIECE
            outs[dist][gx * PIECE : (gx + 1) * PIECE] = src[at : at + PIECE]
            base = count_gx * PIECE + gx * 8
            outs[dist][base : base + 8] = src[half * PIECE + k * 8 : half * PIECE + k * 8 + 8]


def tile_values(count_gx, count_gz, hot, *refs):
    parts, out = refs[:count_gz], refs[count_gz]
    values = []
    for gx in range(count_gx):
        for dist in range(count_gz):
            base = count_gx * PIECE + gx * 8
            values.append(parts[dist][base : base + 8])
    t = jnp.concatenate(values, axis=0)
    out[0] = exact_dot(hot[...], t)
    out[1] = jnp.maximum(exact_dot(hot[...], pltpu.roll(t, t.shape[0] - 1, 0)), 1.0)


def exact_dot(hot, values):
    total = None
    rest = values
    left = hot.astype(jnp.bfloat16)
    for _ in range(3):
        part = rest.astype(jnp.bfloat16)
        rest = rest - part.astype(jnp.float32)
        term = jnp.dot(left, part, preferred_element_type=jnp.float32)
        total = term if total is None else total + term
    return total


def z_places(low):
    places = [H0 + (HALO - dist if low else HALO + LEVELS - 1 + dist) for dist in (1, 2, 3)]
    for first in (A0, N0, S0):
        places += [first + (HALO - 1 - dist if low else HALO - 2 + LEVELS + dist) for dist in (1, 2)]
    return places + [P0 + (0 if low else NP - 1), K_LO if low else K_HI, M_LO if low else M_HI]


def by_parity(axis, action, first, second):
    even = is_even(axis)

    @pl.when(even)
    def _():
        action(first, second)

    @pl.when(jnp.logical_not(even))
    def _():
        action(second, first)


OWN = (H0 + HALO, A0 + HALO - 1, N0 + HALO - 1, S0 + HALO - 1, P0 + HALO - 2)


def scaled(k, value):
    return (value, value * value, 0.5 * value, 0.5 * value, value)[k]


def own_edges(count_gx, *refs):
    arrays, outs, buf, sem = refs[:5], refs[5:-2], refs[-2], refs[-1]
    copies = []
    for k, src in enumerate(arrays):
        for side in range(2):
            start = 0 if side == 0 else ROWS - 8
            copy = pltpu.make_async_copy(src.at[:, pl.ds(start, 8), :], buf.at[side, k], sem.at[len(copies)])
            copy.start()
            copies.append(copy)
    for copy in copies:
        copy.wait()

    def put(high, low):
        for k, first in enumerate(OWN):
            for level in range(LEVELS):
                if high is not None:
                    value = buf[1, k, level, pl.ds(8 - HALO, HALO), :]
                    high[first + level, pl.ds(0, HALO), :] = scaled(k, value)
                if low is not None:
                    value = buf[0, k, level, pl.ds(0, HALO), :]
                    low[first + level, pl.ds(0, HALO), :] = scaled(k, value)

    by_parity("gx", put, outs[0], outs[1] if count_gx > 2 else None)


def x_faces(count_gx, *refs):
    z_e, z_o, tile = refs[:3]
    sends = refs[-1:] if count_gx == 2 else refs[-2:]

    def put_all(high, low):
        def put(upper, lower):
            for got, places in ((upper, z_places(False)), (lower, z_places(True))):
                for k, p in enumerate(places):
                    if high is not None:
                        high[p, pl.ds(0, HALO), :] = got[k, pl.ds(ROWS - HALO, HALO), :]
                    if low is not None:
                        low[p, pl.ds(0, HALO), :] = got[k, pl.ds(0, HALO), :]

        by_parity("gz", put, z_e, z_o)
        for k in range(2):
            if high is not None:
                high[TP + k, pl.ds(0, HALO), :] = tile[k, pl.ds(ROWS - HALO, HALO), :]
            if low is not None:
                low[TP + k, pl.ds(0, HALO), :] = tile[k, pl.ds(0, HALO), :]

    by_parity("gx", put_all, sends[0], sends[1] if count_gx > 2 else None)


def all_planes(h, a, n, s, p, z_e, z_o, tile, planes, sem):
    copies = []
    for k, src in enumerate((h, a, n, s, p)):
        copy = pltpu.make_async_copy(src, planes.at[pl.ds(OWN[k], LEVELS)], sem.at[k])
        copy.start()
        copies.append(copy)

    def put(upper, lower):
        for got, places in ((upper, z_places(False)), (lower, z_places(True))):
            for k, p in enumerate(places):
                planes[p] = got[k]

    by_parity("gz", put, z_e, z_o)
    planes[TP] = tile[0]
    planes[RT] = tile[1]
    for copy in copies:
        copy.wait()
    for k in (1, 2, 3):
        for level in range(LEVELS):
            planes[OWN[k] + level] = scaled(k, planes[OWN[k] + level])


def y_faces(count_gx, *refs):
    planes = refs[0]
    if count_gx > 2:
        got_e, got_o = refs[1], refs[2]
    else:
        got_e, got_o = refs[1], None
    edge, strips, send_e, send_o = refs[-4:]

    def take(high, low):
        for p in range(PLANES):
            edge[p] = planes[p, ROWS - EDGE : ROWS]
            if high is not None:
                edge[p, pl.ds(0, HALO), :] = high[p, pl.ds(0, HALO), :]
            if low is not None:
                edge[p, pl.ds(EDGE - HALO, HALO), :] = low[p, pl.ds(0, HALO), :]

    even_x = is_even("gx")

    @pl.when(even_x)
    def _():
        take(got_e, got_o)

    @pl.when(jnp.logical_not(even_x))
    def _():
        take(got_o, got_e)

    lane_group = lax.broadcasted_iota(jnp.int32, (WIDE, COLS), 1) // SIDE

    def pack(t, carry):
        acc = jnp.zeros((WIDE, COLS), jnp.float32)
        for j in range(8):
            p = jnp.minimum(t * 8 + j, PLANES - 1)
            value = jnp.concatenate([planes[p], edge[p]], axis=0)
            acc = jnp.where(lane_group == j, pltpu.roll(value, SIDE * j + 8, 1), acc)
        full = jnp.concatenate([acc] + [acc[ROWS:WIDE]] * ((COLS - WIDE) // EDGE), axis=0)
        strips[pl.ds(pl.multiple_of(t * COLS, COLS), COLS), :] = full.T
        return carry

    lax.fori_loop(0, PACKS, pack, 0)

    def put(send, last):
        start = 5 if last else 8
        for p in range(PLANES):
            send[pl.ds(p * HALO, HALO), :] = strips[pl.ds(p * SIDE + start, HALO), :]
        rest = Y_SEND - PLANES * HALO
        if rest:
            send[pl.ds(PLANES * HALO, rest), :] = jnp.zeros((rest, COLS), jnp.float32)

    even_y = is_even("role")

    @pl.when(even_y)
    def _():
        put(send_e, True)
        put(send_o, False)

    @pl.when(jnp.logical_not(even_y))
    def _():
        put(send_e, False)
        put(send_o, True)


def uptake_of(tpot, roots, head, layers, base_exp, first):
    total = jnp.zeros_like(tpot)
    for layer in range(layers):
        total = total + jnp.where(roots > float(layer), math.exp(-layer / 4.0), 0.0)
    share = tpot * base_exp / total
    result = []
    for q in range(LAYERS_PER_BLOCK + 2):
        depth = (first + (q - 1)).astype(jnp.float32)
        weight = jnp.where(depth < roots, math.exp(-(q - 1) / 4.0) * share, 0.0)
        result.append(weight / (1.0 + head[q] * head[q] * (1.0 / 2.25)))
    return result


def sweeps(count_role, count_gx, count_gz, planes, edge, strips_in, y_e, y_o, out,
           strips, ha, hb, kc, mm, th, wd, sk,
           sa, sb, sc, ks, sm, sth, swd, ssk, turn):
    me_role, me_gx, me_gz = place("role"), place("gx"), place("gz")
    layers = LAYERS_PER_BLOCK * count_gz
    first = me_gz * LAYERS_PER_BLOCK
    f32 = jnp.float32
    z_top = jnp.where(me_gz == 0, 0.0, 1.0).astype(f32)
    z_bottom = jnp.where(me_gz == count_gz - 1, 0.0, 1.0).astype(f32)
    x_first = jnp.where(me_gx == 0, 0.0, 1.0).astype(f32)
    x_last = jnp.where(me_gx == count_gx - 1, 0.0, 1.0).astype(f32)
    y_first = jnp.where(me_role == 0, 0.0, 1.0).astype(f32)
    y_last = jnp.where(me_role == count_role - 1, 0.0, 1.0).astype(f32)
    exp_first = jnp.exp(jnp.zeros((8, COLS), f32) - me_gz.astype(f32))

    strips[...] = strips_in[...]

    def take(high, low):
        for p in range(PLANES):
            strips[pl.ds(p * SIDE, HALO), :] = high[pl.ds(p * HALO, HALO), :]
            strips[pl.ds(p * SIDE + SIDE - HALO, HALO), :] = low[pl.ds(p * HALO, HALO), :]

    even_y = is_even("role")

    @pl.when(even_y)
    def _():
        take(y_e, y_o)

    @pl.when(jnp.logical_not(even_y))
    def _():
        take(y_o, y_e)

    def wide(p):
        return jnp.concatenate([planes[p], edge[p]], axis=0)

    def put(ref, i, value):
        ref[i, 8 : 8 + WIDE] = value
        ref[i, 0:8] = value[ROWS:WIDE]
        ref[i, 8 + WIDE : 16 + WIDE] = value[0:8]

    row = lax.broadcasted_iota(jnp.int32, (8, COLS), 0)
    x_low = jnp.where(row == 0, x_first, 1.0)
    x_high = jnp.where(row == 7, x_last, 1.0)

    def fill(i, carry):
        put(ha, i, wide(H0 + i))
        return carry

    lax.fori_loop(0, NH, fill, 0)
    put(kc, 0, wide(K_LO))
    put(kc, NH - 1, wide(K_HI))

    def mean4(ref, i):
        return (ref[i, 8 : 8 + WIDE] + ref[i + 1, 8 : 8 + WIDE] + ref[i + 2, 8 : 8 + WIDE] + ref[i + 3, 8 : 8 + WIDE]) * 0.25

    heads = [wide(M_LO)] + [mean4(ha, HALO + 4 * q) for q in range(LAYERS_PER_BLOCK)] + [wide(M_HI)]
    base = jnp.concatenate([exp_first] * (WIDE // 8), axis=0)
    for q, value in enumerate(uptake_of(wide(TP), wide(RT), heads, layers, base, first)):
        sk[q] = value

    def strip(p, count=1):
        return strips[p * SIDE : (p + count) * SIDE, :]

    heads = [strip(M_LO)]
    for q in range(LAYERS_PER_BLOCK):
        at = H0 + HALO + 4 * q
        heads.append((strip(at) + strip(at + 1) + strip(at + 2) + strip(at + 3)) * 0.25)
    heads.append(strip(M_HI))
    base = jnp.concatenate([exp_first] * 2, axis=0)
    for q, value in enumerate(uptake_of(strip(TP), strip(RT), heads, layers, base, first)):
        ssk[q * SIDE : (q + 1) * SIDE, :] = value

    def first_curves(j, theta):
        i = j + 1
        half_n = wide(N0 + j)
        expo = expo_of(half_n)
        mm[j] = expo
        satur, cond = curves(ha[i, 8 : 8 + WIDE], wide(A0 + j), half_n, wide(S0 + j), expo)
        put(kc, i, cond)
        if theta:
            th[j - 1] = wide(P0 + j - 1) * satur

    def later_curves(src, j, water):
        i = j + 1
        satur, cond = curves(src[i, 8 : 8 + WIDE], wide(A0 + j), wide(N0 + j), wide(S0 + j), mm[j])
        put(kc, i, cond)
        if water:
            wd[j - 1] = wide(P0 + j - 1) * satur - th[j - 1] + sk[(i + 1) // LEVELS_PER_LAYER]

    def stencil(src, i0, count, sweep, store):
        here = pl.ds(8, WIDE)
        conds = [kc[i0 + g - 1, here, :] for g in range(count + 2)]
        heads = [src[i0 + g - 1, here, :] for g in range(count + 2)]
        faces = [conds[g] + conds[g + 1] for g in range(count + 1)]
        faces[0] = faces[0] * jnp.where(i0 == HALO, z_top, jnp.where(i0 == HALO + LEVELS, z_bottom, 1.0))
        end = i0 + count
        faces[count] = faces[count] * jnp.where(
            end == HALO, z_top, jnp.where(end == HALO + LEVELS, z_bottom, 1.0)
        )
        for g in range(count):
            i = i0 + g
            head, cond = heads[g + 1], conds[g + 1]
            kf_up, kf_down = faces[g], faces[g + 1]
            kf_xm = cond + kc[i, pl.ds(7, WIDE), :]
            kf_xm = jnp.concatenate([kf_xm[0:8] * x_low, kf_xm[8:]], axis=0)
            kf_xp = cond + kc[i, pl.ds(9, WIDE), :]
            kf_xp = jnp.concatenate([kf_xp[: ROWS - 8], kf_xp[ROWS - 8 : ROWS] * x_high, kf_xp[ROWS:]], axis=0)
            kf_ym = cond + pltpu.roll(cond, 1, 1)
            kf_yp = cond + pltpu.roll(cond, COLS - 1, 1)
            inflow = kf_up * (heads[g] + 1.0) + kf_down * (heads[g + 2] - 1.0)
            inflow = inflow + (kf_xm * src[i, pl.ds(7, WIDE), :] + kf_xp * src[i, pl.ds(9, WIDE), :])
            inflow = inflow + (kf_ym * pltpu.roll(head, 1, 1) + kf_yp * pltpu.roll(head, COLS - 1, 1))
            lost = wd[i - 2] if sweep > 0 else sk[(i + 1) // LEVELS_PER_LAYER]
            diag = (1.0 + kf_up) + (kf_down + kf_xm) + (kf_xp + kf_ym) + kf_yp
            store(i, relax(head, inflow - lost, diag, sweep))

    def loop(lo, hi, body, unroll=1):
        def step(i, carry):
            body(i)
            return carry

        lax.fori_loop(lo, hi, step, 0, unroll=unroll)

    def levels_of(src, sweep, store):
        extra = SWEEPS - 1 - sweep
        if extra:
            stencil(src, HALO - extra, extra, sweep, store)
        loop(0, LEVELS // 4, lambda k: stencil(src, HALO + 4 * k, 4, sweep, store))
        if extra:
            stencil(src, HALO + LEVELS, extra, sweep, store)

    first_curves(0, False)
    loop(1, NC - 1, lambda j: first_curves(j, True), 3)
    first_curves(NC - 1, False)
    levels_of(ha, 0, lambda i, value: put(hb, i, value))

    lane = lax.broadcasted_iota(jnp.int32, (SIDE, COLS), 1)
    srow = lax.broadcasted_iota(jnp.int32, (SIDE, COLS), 0)
    s_xm = jnp.where(lane == 0, x_first, 1.0)
    s_xp = jnp.where(lane == ROWS - 1, x_last, 1.0)
    side_mask = jnp.where(srow < 8, y_last, y_first)
    s_ym = jnp.where(srow % 8 == 0, side_mask, 1.0)
    s_yp = jnp.where(srow % 8 == 7, side_mask, 1.0)

    def tiled(mask, count):
        return jnp.concatenate([mask] * count, axis=0)

    def y_shift(value, by):
        parts = value.reshape(value.shape[0] // 8, 8, COLS)
        return pltpu.roll(parts, by, 1).reshape(value.shape)

    def rows_of(i, count):
        return slice(i * SIDE, (i + count) * SIDE)

    def strip_curves(src, lo, hi, sweep):
        i = lo
        while i < hi:
            count = min(5, hi - i)
            j = i - 1
            here = rows_of(i, count)
            half_n = strip(N0 + j, count)
            if sweep == 0:
                expo = expo_of(half_n)
                sm[rows_of(j, count), :] = expo
            else:
                expo = sm[rows_of(j, count), :]
            satur, cond = curves(src[here, :], strip(A0 + j, count), half_n, strip(S0 + j, count), expo)
            ks[here, :] = cond
            start, stop = max(i, 2), min(i + count, NH - 2)
            if stop > start:
                part = satur[(start - i) * SIDE : (stop - i) * SIDE]
                water = strip(P0 + start - 2, stop - start) * part
                at = rows_of(start - 2, stop - start)
                if sweep == 0:
                    sth[at, :] = water
                else:
                    swd[at, :] = water - sth[at, :]
            i += count

    def strip_stencil(src, dst, lo, hi, sweep):
        i = lo
        while i < hi:
            count = min(5, hi - i)
            here = rows_of(i, count)
            above, below = rows_of(i - 1, count), rows_of(i + 1, count)
            head, cond = src[here, :], ks[here, :]
            kf_up = cond + ks[above, :]
            kf_down = cond + ks[below, :]
            if i <= HALO < i + count:
                level = lax.broadcasted_iota(jnp.int32, kf_up.shape, 0) // SIDE
                kf_up = jnp.where(level == HALO - i, kf_up * z_top, kf_up)
            if i <= HALO + LEVELS - 1 < i + count:
                level = lax.broadcasted_iota(jnp.int32, kf_up.shape, 0) // SIDE
                kf_down = jnp.where(level == HALO + LEVELS - 1 - i, kf_down * z_bottom, kf_down)
            kf_xm = (cond + pltpu.roll(cond, 1, 1)) * tiled(s_xm, count)
            kf_xp = (cond + pltpu.roll(cond, COLS - 1, 1)) * tiled(s_xp, count)
            kf_ym = (cond + y_shift(cond, 1)) * tiled(s_ym, count)
            kf_yp = (cond + y_shift(cond, 7)) * tiled(s_yp, count)
            inflow = kf_up * (src[above, :] + 1.0) + kf_down * (src[below, :] - 1.0)
            inflow = inflow + (kf_xm * pltpu.roll(head, 1, 1) + kf_xp * pltpu.roll(head, COLS - 1, 1))
            inflow = inflow + (kf_ym * y_shift(head, 1) + kf_yp * y_shift(head, 7))
            lost = jnp.concatenate([ssk[rows_of((k + 1) // LEVELS_PER_LAYER, 1), :] for k in range(i, i + count)], axis=0)
            if sweep > 0:
                lost = lost + swd[rows_of(i - 2, count), :]
            diag = (1.0 + kf_up) + (kf_down + kf_xm) + (kf_xp + kf_ym) + kf_yp
            dst[here, :] = relax(head, inflow - lost, diag, sweep)
            i += count

    ks[rows_of(0, 1), :] = strip(K_LO)
    ks[rows_of(NH - 1, 1), :] = strip(K_HI)
    strip_curves(strips, 1, NH - 1, 0)
    strip_stencil(strips, sa, 1, NH - 1, 0)
    strip_curves(sa, 1, NH - 1, 1)
    strip_stencil(sa, sb, 2, NH - 2, 1)
    strip_curves(sb, 2, NH - 2, 2)
    strip_stencil(sb, sc, 3, NH - 3, 2)

    lane_wide = lax.broadcasted_iota(jnp.int32, (WIDE, COLS), 1)
    low_rows = lax.broadcasted_iota(jnp.int32, (EDGE, COLS), 0) >= EDGE - HALO

    def turned(pieces):
        rows = sum(piece.shape[0] for piece in pieces)
        full = jnp.concatenate(pieces + [jnp.zeros((COLS - rows, COLS), f32)], axis=0).T
        last = jnp.where(low_rows, full[COLS - EDGE : COLS], full[ROWS:WIDE])
        return jnp.concatenate([full[0:ROWS], last], axis=0)

    turn[...] = turned([sa[i * SIDE + 7 : i * SIDE + 9, :] for i in range(1, NH - 1)])
    outer = (lane_wide == 0) | (lane_wide == COLS - 1)
    for i in range(1, NH - 1):
        moved = pltpu.roll(turn[...], (COLS - 1 - 2 * (i - 1)) % COLS, 1)
        put(hb, i, jnp.where(outer, moved, hb[i, 8 : 8 + WIDE]))

    later_curves(hb, 0, False)
    loop(1, NC - 1, lambda j: later_curves(hb, j, True), 3)
    later_curves(hb, NC - 1, False)
    levels_of(hb, 1, lambda i, value: put(ha, i, value))
    loop(1, NC - 1, lambda j: later_curves(ha, j, True), 3)

    turn[...] = turned([sc[i * SIDE + 6 : i * SIDE + 10, :] for i in range(HALO, HALO + LEVELS)])
    outer = ((lane_wide < 2) | (lane_wide >= COLS - 2))[0:ROWS]
    levels_of(ha, 2, lambda i, value: put(hb, i, value))
    for level in range(LEVELS):
        moved = pltpu.roll(turn[0:ROWS], (COLS - 2 - 4 * level) % COLS, 1)
        out[level] = jnp.where(outer, moved, hb[HALO + level, 8 : 8 + ROWS])


def heat(count_gx, count_gz, *refs):
    parts, refs = refs[:count_gz], refs[count_gz:]
    temp_in, tr_in, air_in, rt_in, out, sat, head, temp, tr, air, rt, y, sem = refs
    copies = []
    for dist, part in enumerate(parts):
        for gx in range(count_gx):
            copy = pltpu.make_async_copy(
                part.at[pl.ds(gx * PIECE, PIECE)], y.at[gx * count_gz + dist], sem.at[len(copies)]
            )
            copy.start()
            copies.append(copy)
    for src, dst in ((temp_in, temp), (tr_in, tr), (air_in, air), (rt_in, rt)):
        copy = pltpu.make_async_copy(src, dst, sem.at[len(copies)])
        copy.start()
        copies.append(copy)
    me = place("gx") * count_gz + place("gz")
    layers = LAYERS_PER_BLOCK * count_gz
    for copy in copies:
        copy.wait()
    for gx in range(count_gx):
        for gz in range(count_gz):
            j = me ^ (gx * count_gz + gz)
            for c in range(CAP):
                tile = y[j, c * 8 : c * 8 + 8]
                at = pl.ds(gz * LAYERS_PER_BLOCK, LAYERS_PER_BLOCK)
                sat[gx * CAP + c, at, :] = tile[0:LAYERS_PER_BLOCK]
                head[gx * CAP + c, at, :] = tile[LAYERS_PER_BLOCK : 2 * LAYERS_PER_BLOCK]
    layer = lax.broadcasted_iota(jnp.int32, (layers, COLS), 0)
    decay = jnp.exp(layer.astype(jnp.float32) * -0.25)
    for slot in range(count_gx * CAP):
        roots = jnp.broadcast_to(rt[slot], (layers, COLS))
        weight = jnp.where(layer < roots, decay, 0.0)
        weight = weight / jnp.sum(weight, axis=0, keepdims=True)
        stress = 1.0 / (1.0 + head[slot] * head[slot] * (1.0 / 2.25))
        uptake = tr[slot] * weight * stress
        kappa = 0.25 + 0.9 * sat[slot]
        top = jnp.broadcast_to(air[slot], (layers, COLS))
        k_above = jnp.where(layer == 0, kappa, 0.5 * (kappa + pltpu.roll(kappa, 1, 0)))
        k_below = jnp.where(layer == layers - 1, 0.0, 0.5 * (kappa + pltpu.roll(kappa, layers - 1, 0)))
        old = temp[slot]
        new = old
        for _ in range(HEAT_STEPS):
            above = jnp.where(layer == 0, top, pltpu.roll(new, 1, 0))
            below = pltpu.roll(new, layers - 1, 0)
            new = new + 0.2 * (k_above * (above - new) + k_below * (below - new)) - 0.3 * uptake
        out[slot] = jnp.where(sat[slot] >= 0.0, new, old)


def call(body, outs, ins, scratch=(), aliases=None, limit=40 * MIB, kept=True, work=0):
    return pl.pallas_call(
        body,
        out_shape=[pltpu.VMEM(shape, jnp.float32) if kept else jax.ShapeDtypeStruct(shape, jnp.float32) for shape in outs],
        in_specs=ins,
        out_specs=[VMEM] * len(outs),
        scratch_shapes=list(scratch),
        input_output_aliases=aliases or {},
        compiler_params=pltpu.CompilerParams(vmem_limit_bytes=limit),
        cost_estimate=pl.CostEstimate(flops=work, bytes_accessed=work, transcendentals=0) if work else None,
    )


def sweep_call(count_role, count_gx, count_gz):
    f32 = jnp.float32
    deep = WIDE + 16
    return call(
        functools.partial(sweeps, count_role, count_gx, count_gz),
        [(LEVELS, ROWS, COLS)],
        [VMEM] * 5,
        [
            pltpu.VMEM((PACKS * COLS, COLS), f32),
            pltpu.VMEM((NH, deep, COLS), f32),
            pltpu.VMEM((NH, deep, COLS), f32),
            pltpu.VMEM((NH, deep, COLS), f32),
            pltpu.VMEM((NC, WIDE, COLS), f32),
            pltpu.VMEM((NP, WIDE, COLS), f32),
            pltpu.VMEM((NP, WIDE, COLS), f32),
            pltpu.VMEM((LAYERS_PER_BLOCK + 2, WIDE, COLS), f32),
            pltpu.VMEM((NH * SIDE, COLS), f32),
            pltpu.VMEM((NH * SIDE, COLS), f32),
            pltpu.VMEM((NH * SIDE, COLS), f32),
            pltpu.VMEM((NH * SIDE, COLS), f32),
            pltpu.VMEM((NC * SIDE, COLS), f32),
            pltpu.VMEM((NP * SIDE, COLS), f32),
            pltpu.VMEM((NP * SIDE, COLS), f32),
            pltpu.VMEM(((LAYERS_PER_BLOCK + 2) * SIDE, COLS), f32),
            pltpu.VMEM((WIDE, COLS), f32),
        ],
        kept=False,
    )


def local(h, a, n, s, p, tile_owner, land_temp, tr, air, rt):
    sizes = tuple(lax.axis_size(axis) for axis in AXES)
    count_role, count_gx, count_gz = sizes
    groups = count_gx * count_gz
    slots = count_gx * CAP
    f32 = jnp.float32

    def swap(value, axis, odd):
        return lax.ppermute(value, AXES, pairing(sizes, axis, odd))

    owners = tile_owner.T
    land = (land_temp[0, 0], tr[0, 0, :, None], air[0, 0, :, None], rt[0, 0, :, None])
    h, a, n, s, p = (pltpu.with_memory_space_constraint(x, pltpu.HBM) for x in (h, a, n, s, p))
    land_temp, tr, air, rt = (pltpu.with_memory_space_constraint(x, pltpu.HBM) for x in land)

    z_send_e, z_send_o = call(
        z_faces,
        [(Z_SEND, ROWS, COLS)] * 2,
        [HBM] * 5,
        [
            pltpu.VMEM((2, 4, ROWS, COLS), f32),
            pltpu.VMEM((2, 3, ROWS, COLS), f32),
            pltpu.VMEM((2, 3, ROWS, COLS), f32),
            pltpu.VMEM((2, 3, ROWS, COLS), f32),
            pltpu.VMEM((2, 1, ROWS, COLS), f32),
            pltpu.SemaphoreType.DMA((10,)),
        ],
    )(h, a, n, s, p)
    z_e = swap(z_send_e, "gz", False)
    z_o = swap(z_send_o, "gz", True) if count_gz > 2 else z_e

    half = groups // 2
    blocks = count_gx // 2
    packed = half * 8 * CAP + blocks * 8
    def land_stage():
        send, keep, hot = call(
            functools.partial(land_pack, count_gx, count_gz),
            [(packed, COLS), (packed, COLS), (ROWS, groups * 8)],
            [SMEM] + [HBM] * 5,
            [
                pltpu.VMEM((2 * LAYERS_PER_BLOCK, ROWS, COLS), f32),
                pltpu.SMEM((groups,), jnp.int32),
                pltpu.SMEM((groups * CAP,), jnp.int32),
                pltpu.VMEM((LEVELS, ROWS, COLS), f32),
                pltpu.VMEM((LEVELS, ROWS, COLS), f32),
                pltpu.VMEM((LEVELS, ROWS, COLS), f32),
                pltpu.VMEM((slots, 1, COLS), f32),
                pltpu.VMEM((slots, 1, COLS), jnp.int32),
                pltpu.SemaphoreType.DMA((5,)),
            ],
        )(owners, h, a, n, tr, rt)

        got = lax.ppermute(send, AXES, xor_pairs(sizes, "gx", blocks))
        bit = blocks // 2
        if bit:
            pieces = [part[j * PIECE : (j + 1) * PIECE] for part in (keep, got) for j in range(half)]
            base = half * PIECE
            values = [part[base + j * 8 : base + (j + 1) * 8] for part in (keep, got) for j in range(blocks)]
            while bit:
                moving = [j for j in range(groups) if (j // count_gz) & bit]
                t_moving = [j for j in range(count_gx) if j & bit]
                sent = jnp.concatenate([pieces[j] for j in moving] + [values[j] for j in t_moving], axis=0)
                got = lax.ppermute(sent, AXES, xor_pairs(sizes, "gx", bit))
                for k, j in enumerate(moving):
                    pieces[j] = got[k * PIECE : (k + 1) * PIECE]
                for k, j in enumerate(t_moving):
                    base = len(moving) * PIECE + k * 8
                    values[j] = got[base : base + 8]
                bit //= 2
            keep = jnp.concatenate(pieces[:half] + values[:blocks], axis=0)
            got = jnp.concatenate(pieces[half:] + values[blocks:], axis=0)
        parts = call(
            functools.partial(land_sort, count_gx, count_gz),
            [(count_gx * (PIECE + 8), COLS)] * count_gz,
            [VMEM] * 2,
        )(keep, got)
        parts = [parts[0]] + [
            lax.ppermute(parts[dist], AXES, xor_pairs(sizes, "gz", dist)) for dist in range(1, count_gz)
        ]
        (tile,) = call(
            functools.partial(tile_values, count_gx, count_gz),
            [(2, ROWS, COLS)],
            [VMEM] * (1 + count_gz),
        )(hot, *parts)
        return [tile] + parts

    def no_land_stage():
        shapes = [(2, ROWS, COLS)] + [(count_gx * (PIECE + 8), COLS)] * count_gz
        return [jnp.zeros(shape, f32) for shape in shapes]

    ahead = lax.optimization_barrier(jnp.bool_(True))
    tile, *parts = lax.cond(ahead, land_stage, no_land_stage)
    parts = [pltpu.with_memory_space_constraint(x, pltpu.HBM) for x in parts]

    x_count = 1 if count_gx == 2 else 2
    x_shape = (PLANES, 4, COLS)
    edges = call(
        functools.partial(own_edges, count_gx),
        [x_shape] * x_count,
        [HBM] * 5,
        [pltpu.VMEM((2, 5, LEVELS, 8, COLS), f32), pltpu.SemaphoreType.DMA((10,))],
    )(h, a, n, s, p)
    x_sends = call(
        functools.partial(x_faces, count_gx),
        [x_shape] * x_count,
        [VMEM] * (3 + x_count),
        aliases={3 + k: k for k in range(x_count)},
    )(z_e, z_o, tile, *edges)
    (planes,) = call(
        all_planes,
        [(PLANES, ROWS, COLS)],
        [HBM] * 5 + [VMEM] * 3,
        [pltpu.SemaphoreType.DMA((5,))],
    )(h, a, n, s, p, z_e, z_o, tile)
    x_got = [swap(value, "gx", bool(k)) for k, value in enumerate(x_sends)]

    edge, strips, y_send_e, y_send_o = call(
        functools.partial(y_faces, count_gx),
        [(PLANES, EDGE, COLS), (PACKS * COLS, COLS), (Y_SEND, COLS), (Y_SEND, COLS)],
        [VMEM] * (1 + x_count),
    )(planes, *x_got)
    y_e = swap(y_send_e, "role", False)
    y_o = swap(y_send_o, "role", True) if count_role > 2 else y_e

    land_shape = (slots, LAYERS_PER_BLOCK * count_gz, COLS)
    (land_new,) = call(
        functools.partial(heat, count_gx, count_gz),
        [land_shape],
        [HBM] * (count_gz + 4),
        [
            pltpu.VMEM(land_shape, f32),
            pltpu.VMEM(land_shape, f32),
            pltpu.VMEM(land_shape, f32),
            pltpu.VMEM((slots, 1, COLS), f32),
            pltpu.VMEM((slots, 1, COLS), f32),
            pltpu.VMEM((slots, 1, COLS), jnp.int32),
            pltpu.VMEM((groups, PIECE, COLS), f32),
            pltpu.SemaphoreType.DMA((4 + groups,)),
        ],
        kept=False,
    )(*parts, land_temp, tr, air, rt)

    (head,) = sweep_call(count_role, count_gx, count_gz)(planes, edge, strips, y_e, y_o)
    return (head, land_new[None, None])


def solution(mesh):
    in_specs = (
        P("gz", "gx", "role"),
        P("gz", "gx", "role"),
        P("gz", "gx", "role"),
        P("gz", "gx", "role"),
        P("gz", "gx", "role"),
        P(),
        P("role", ("gx", "gz"), None, None, None),
        P("role", ("gx", "gz"), None, None),
        P("role", ("gx", "gz"), None, None),
        P("role", ("gx", "gz"), None, None),
    )
    out_specs = (P("gz", "gx", "role"), P("role", ("gx", "gz"), None, None, None))
    return jax.shard_map(local, mesh=mesh, in_specs=in_specs, out_specs=out_specs, check_vma=False)
```

```python
import functools
import math

import jax
import jax.numpy as jnp
from jax import lax
from jax.experimental import pallas as pl
from jax.experimental.pallas import tpu as pltpu
from jax.sharding import PartitionSpec as P

LAYERS_PER_BLOCK = 4
LEVELS_PER_LAYER = 4
CAP = 3
SWEEPS = 3
HEAT_STEPS = 4
HALO = SWEEPS
AXES = ("role", "gx", "gz")
VMEM = pl.BlockSpec(memory_space=pltpu.VMEM)
SMEM = pl.BlockSpec(memory_space=pltpu.SMEM)
HBM = pl.BlockSpec(memory_space=pltpu.HBM)
MIB = 1024 * 1024

LEVELS = 16
ROWS = 64
COLS = 128
EDGE = 8
WIDE = ROWS + EDGE
H0 = 0
NH = LEVELS + 2 * HALO
A0 = H0 + NH
NC = LEVELS + 2 * HALO - 2
N0 = A0 + NC
S0 = N0 + NC
K_LO = S0 + NC
K_HI = K_LO + 1
P0 = K_HI + 1
NP = LEVELS + 2 * HALO - 4
M_LO = P0 + NP
M_HI = M_LO + 1
TP = M_HI + 1
RT = TP + 1
PLANES = RT + 1
PACKS = (PLANES + 7) // 8
SIDE = 16
NEAR = 4
Z_SEND = 12
PIECE = 8 * CAP
Y_SEND = (PLANES * HALO + 7) // 8 * 8


def omega(sweep):
    return 1.0 / (1.0 + 0.6 * math.cos(math.pi * (2 * sweep + 1) / (2 * SWEEPS)))


def place(axis):
    return lax.axis_index(axis)


def is_even(axis):
    return lax.rem(place(axis), 2) == 0


def pairing(sizes, axis, odd):
    pairs = []
    which = AXES.index(axis)
    for index in range(math.prod(sizes)):
        at = [index // (sizes[1] * sizes[2]), index // sizes[2] % sizes[1], index % sizes[2]]
        count = sizes[which]
        there = list(at)
        if not odd:
            there[which] = at[which] ^ 1
        else:
            there[which] = at[which] + (1 if at[which] % 2 else -1)
            if not 0 <= there[which] < count:
                there = list(at)
                if axis == "gx":
                    there[1] = count - 1 - at[1]
                else:
                    there[1] = at[1] ^ 1
        pairs.append((index, (there[0] * sizes[1] + there[1]) * sizes[2] + there[2]))
    return pairs


def xor_pairs(sizes, axis, bit):
    pairs = []
    which = AXES.index(axis)
    for index in range(math.prod(sizes)):
        at = [index // (sizes[1] * sizes[2]), index // sizes[2] % sizes[1], index % sizes[2]]
        at[which] ^= bit
        pairs.append((index, (at[0] * sizes[1] + at[1]) * sizes[2] + at[2]))
    return pairs


def curves(head, alpha2, half_n, half_ks, expo):
    logx = half_n * jnp.log(alpha2 * (head * head + 0.01))
    softer = jnp.log(1.0 + jnp.exp(logx))
    root = jnp.exp(-0.5 * expo * softer)
    gap = 1.0 - jnp.exp(expo * (logx - softer))
    return root * root, half_ks * root * (gap * gap)


def inverse(value):
    guess = pl.reciprocal(value, approx=True)
    return guess * (2.0 - value * guess)


def expo_of(half_n):
    return 1.0 - 0.5 * inverse(half_n)


def relax(head, inflow, diag, sweep):
    step = omega(sweep)
    return (1.0 - step) * head + (step * (head + inflow)) * inverse(diag)


def z_faces(h, a, n, s, p, out_e, out_o, hb, ab, nb, sb, pb, sem):
    copies = []
    for side in range(2):
        for src, dst, count in ((h, hb, 4), (a, ab, 3), (n, nb, 3), (s, sb, 3), (p, pb, 1)):
            start = 0 if side == 0 else LEVELS - count
            copy = pltpu.make_async_copy(src.at[pl.ds(start, count)], dst.at[side], sem.at[len(copies)])
            copy.start()
            copies.append(copy)
    for copy in copies:
        copy.wait()

    def put(out, side):
        def level(buf, count, dist):
            return buf[side, dist - 1 if side == 0 else count - dist]

        for dist in (1, 2, 3):
            out[dist - 1] = level(hb, 4, dist)
        for dist in (1, 2):
            alpha = level(ab, 3, dist)
            out[2 + dist] = alpha * alpha
            out[4 + dist] = 0.5 * level(nb, 3, dist)
            out[6 + dist] = 0.5 * level(sb, 3, dist)
        out[9] = level(pb, 1, 1)
        alpha = level(ab, 3, 3)
        half_n = 0.5 * level(nb, 3, 3)
        out[10] = curves(level(hb, 4, 3), alpha * alpha, half_n, 0.5 * level(sb, 3, 3), expo_of(half_n))[1]
        out[11] = (hb[side, 0] + hb[side, 1] + hb[side, 2] + hb[side, 3]) * 0.25

    even = is_even("gz")

    @pl.when(even)
    def _():
        put(out_e, 1)
        put(out_o, 0)

    @pl.when(jnp.logical_not(even))
    def _():
        put(out_e, 0)
        put(out_o, 1)


def land_pack(count_gx, count_gz, owners, h_in, a_in, n_in, tr_in, rt_in, send, keep, hot,
              means, counts, slots, h, a, n, tr, rt, sem):
    groups = count_gx * count_gz
    me_role, me_gx = place("role"), place("gx")
    me = me_gx * count_gz + place("gz")
    copies = []
    for src, dst in ((h_in, h), (a_in, a), (n_in, n), (tr_in, tr), (rt_in, rt)):
        copy = pltpu.make_async_copy(src, dst, sem.at[len(copies)])
        copy.start()
        copies.append(copy)

    def clear_slot(i, carry):
        slots[i] = -1
        return carry

    def clear_count(i, carry):
        counts[i] = 0
        return carry

    lax.fori_loop(0, groups * CAP, clear_slot, 0)
    lax.fori_loop(0, groups, clear_count, 0)
    lane = lax.broadcasted_iota(jnp.int32, (1, groups * 8), 1)

    def step(x, carry):
        owner = owners[me_role, me_gx * ROWS + x]
        safe = jnp.maximum(owner, 0)
        rank = counts[safe]
        at = jnp.where(owner >= 0, (me ^ owner) * 8 + 2 * rank, -1)
        hot[pl.ds(x, 1), :] = jnp.where(lane == at, 1.0, 0.0)

        @pl.when(owner >= 0)
        def _():
            counts[owner] = rank + 1
            slots[owner * CAP + rank] = x

        return carry

    lax.fori_loop(0, ROWS, step, 0)
    for copy in copies:
        copy.wait()
    for layer in range(LAYERS_PER_BLOCK):
        saturs = []
        heads = []
        for level in range(layer * LEVELS_PER_LAYER, (layer + 1) * LEVELS_PER_LAYER):
            head = h[level]
            alpha = a[level]
            half_n = 0.5 * n[level]
            logx = half_n * jnp.log(alpha * alpha * (head * head + 0.01))
            softer = jnp.log(1.0 + jnp.exp(logx))
            saturs.append(jnp.exp(-expo_of(half_n) * softer))
            heads.append(head)
        means[layer] = (saturs[0] + saturs[1] + saturs[2] + saturs[3]) * 0.25
        means[LAYERS_PER_BLOCK + layer] = (heads[0] + heads[1] + heads[2] + heads[3]) * 0.25
    half = groups // 2
    for j in range(groups):
        out, k = (keep, j) if j < half else (send, j - half)
        for c in range(CAP):
            row = slots[(me ^ j) * CAP + c]
            safe = jnp.maximum(row, 0)
            for q in range(8):
                value = means[q, pl.ds(safe, 1), :]
                out[pl.ds(k * PIECE + c * 8 + q, 1), :] = jnp.where(row >= 0, value, -1.0)
    blocks = count_gx // 2
    for j in range(count_gx):
        block = me_gx ^ j
        out, k = (keep, j) if j < blocks else (send, j - blocks)
        base = half * PIECE + k * 8
        out[pl.ds(base, 8), :] = jnp.zeros((8, COLS), jnp.float32)
        for c in range(CAP):
            out[pl.ds(base + 2 * c, 1), :] = tr[block * CAP + c]
            out[pl.ds(base + 2 * c + 1, 1), :] = rt[block * CAP + c].astype(jnp.float32)


def land_sort(count_gx, count_gz, keep, got, *outs):
    half, blocks = count_gx * count_gz // 2, count_gx // 2
    for gx in range(count_gx):
        src, k = (keep, gx) if gx < blocks else (got, gx - blocks)
        for dist in range(count_gz):
            at = (k * count_gz + dist) * PIECE
            outs[dist][gx * PIECE : (gx + 1) * PIECE] = src[at : at + PIECE]
            base = count_gx * PIECE + gx * 8
            outs[dist][base : base + 8] = src[half * PIECE + k * 8 : half * PIECE + k * 8 + 8]


def tile_values(count_gx, count_gz, hot, *refs):
    parts, out = refs[:count_gz], refs[count_gz]
    values = []
    for gx in range(count_gx):
        for dist in range(count_gz):
            base = count_gx * PIECE + gx * 8
            values.append(parts[dist][base : base + 8])
    t = jnp.concatenate(values, axis=0)
    out[0] = exact_dot(hot[...], t)
    out[1] = jnp.maximum(exact_dot(hot[...], pltpu.roll(t, t.shape[0] - 1, 0)), 1.0)


def exact_dot(hot, values):
    total = None
    rest = values
    left = hot.astype(jnp.bfloat16)
    for _ in range(3):
        part = rest.astype(jnp.bfloat16)
        rest = rest - part.astype(jnp.float32)
        term = jnp.dot(left, part, preferred_element_type=jnp.float32)
        total = term if total is None else total + term
    return total


def z_places(low):
    places = [H0 + (HALO - dist if low else HALO + LEVELS - 1 + dist) for dist in (1, 2, 3)]
    for first in (A0, N0, S0):
        places += [first + (HALO - 1 - dist if low else HALO - 2 + LEVELS + dist) for dist in (1, 2)]
    return places + [P0 + (0 if low else NP - 1), K_LO if low else K_HI, M_LO if low else M_HI]


def by_parity(axis, action, first, second):
    even = is_even(axis)

    @pl.when(even)
    def _():
        action(first, second)

    @pl.when(jnp.logical_not(even))
    def _():
        action(second, first)


OWN = (H0 + HALO, A0 + HALO - 1, N0 + HALO - 1, S0 + HALO - 1, P0 + HALO - 2)


def scaled(k, value):
    return (value, value * value, 0.5 * value, 0.5 * value, value)[k]


def own_edges(count_gx, *refs):
    arrays, outs, buf, sem = refs[:5], refs[5:-2], refs[-2], refs[-1]
    copies = []
    for k, src in enumerate(arrays):
        for side in range(2):
            start = 0 if side == 0 else ROWS - 8
            copy = pltpu.make_async_copy(src.at[:, pl.ds(start, 8), :], buf.at[side, k], sem.at[len(copies)])
            copy.start()
            copies.append(copy)
    for copy in copies:
        copy.wait()

    def put(high, low):
        for k, first in enumerate(OWN):
            for level in range(LEVELS):
                if high is not None:
                    value = buf[1, k, level, pl.ds(8 - HALO, HALO), :]
                    high[first + level, pl.ds(0, HALO), :] = scaled(k, value)
                if low is not None:
                    value = buf[0, k, level, pl.ds(0, HALO), :]
                    low[first + level, pl.ds(0, HALO), :] = scaled(k, value)

    by_parity("gx", put, outs[0], outs[1] if count_gx > 2 else None)


def x_faces(count_gx, *refs):
    z_e, z_o, tile = refs[:3]
    sends = refs[-1:] if count_gx == 2 else refs[-2:]

    def put_all(high, low):
        def put(upper, lower):
            for got, places in ((upper, z_places(False)), (lower, z_places(True))):
                for k, p in enumerate(places):
                    if high is not None:
                        high[p, pl.ds(0, HALO), :] = got[k, pl.ds(ROWS - HALO, HALO), :]
                    if low is not None:
                        low[p, pl.ds(0, HALO), :] = got[k, pl.ds(0, HALO), :]

        by_parity("gz", put, z_e, z_o)
        for k in range(2):
            if high is not None:
                high[TP + k, pl.ds(0, HALO), :] = tile[k, pl.ds(ROWS - HALO, HALO), :]
            if low is not None:
                low[TP + k, pl.ds(0, HALO), :] = tile[k, pl.ds(0, HALO), :]

    by_parity("gx", put_all, sends[0], sends[1] if count_gx > 2 else None)


def all_planes(h, a, n, s, p, z_e, z_o, tile, planes, sem):
    copies = []
    for k, src in enumerate((h, a, n, s, p)):
        copy = pltpu.make_async_copy(src, planes.at[pl.ds(OWN[k], LEVELS)], sem.at[k])
        copy.start()
        copies.append(copy)

    def put(upper, lower):
        for got, places in ((upper, z_places(False)), (lower, z_places(True))):
            for k, p in enumerate(places):
                planes[p] = got[k]

    by_parity("gz", put, z_e, z_o)
    planes[TP] = tile[0]
    planes[RT] = tile[1]
    for copy in copies:
        copy.wait()
    for k in (1, 2, 3):
        for level in range(LEVELS):
            planes[OWN[k] + level] = scaled(k, planes[OWN[k] + level])


def y_faces(count_gx, *refs):
    planes = refs[0]
    if count_gx > 2:
        got_e, got_o = refs[1], refs[2]
    else:
        got_e, got_o = refs[1], None
    edge, strips, send_e, send_o = refs[-4:]

    def take(high, low):
        for p in range(PLANES):
            edge[p] = planes[p, ROWS - EDGE : ROWS]
            if high is not None:
                edge[p, pl.ds(0, HALO), :] = high[p, pl.ds(0, HALO), :]
            if low is not None:
                edge[p, pl.ds(EDGE - HALO, HALO), :] = low[p, pl.ds(0, HALO), :]

    even_x = is_even("gx")

    @pl.when(even_x)
    def _():
        take(got_e, got_o)

    @pl.when(jnp.logical_not(even_x))
    def _():
        take(got_o, got_e)

    lane_group = lax.broadcasted_iota(jnp.int32, (WIDE, COLS), 1) // SIDE

    def pack(t, carry):
        acc = jnp.zeros((WIDE, COLS), jnp.float32)
        for j in range(8):
            p = jnp.minimum(t * 8 + j, PLANES - 1)
            value = jnp.concatenate([planes[p], edge[p]], axis=0)
            acc = jnp.where(lane_group == j, pltpu.roll(value, SIDE * j + 8, 1), acc)
        full = jnp.concatenate([acc] + [acc[ROWS:WIDE]] * ((COLS - WIDE) // EDGE), axis=0)
        strips[pl.ds(pl.multiple_of(t * COLS, COLS), COLS), :] = full.T
        return carry

    lax.fori_loop(0, PACKS, pack, 0)

    def put(send, last):
        start = 5 if last else 8
        for p in range(PLANES):
            send[pl.ds(p * HALO, HALO), :] = strips[pl.ds(p * SIDE + start, HALO), :]
        rest = Y_SEND - PLANES * HALO
        if rest:
            send[pl.ds(PLANES * HALO, rest), :] = jnp.zeros((rest, COLS), jnp.float32)

    even_y = is_even("role")

    @pl.when(even_y)
    def _():
        put(send_e, True)
        put(send_o, False)

    @pl.when(jnp.logical_not(even_y))
    def _():
        put(send_e, False)
        put(send_o, True)


def uptake_of(tpot, roots, head, layers, base_exp, first):
    total = jnp.zeros_like(tpot)
    for layer in range(layers):
        total = total + jnp.where(roots > float(layer), math.exp(-layer / 4.0), 0.0)
    share = tpot * base_exp / total
    result = []
    for q in range(LAYERS_PER_BLOCK + 2):
        depth = (first + (q - 1)).astype(jnp.float32)
        weight = jnp.where(depth < roots, math.exp(-(q - 1) / 4.0) * share, 0.0)
        result.append(weight / (1.0 + head[q] * head[q] * (1.0 / 2.25)))
    return result


def inner_lane(k):
    return k // 9 * 18 + k % 9


class Where:
    def __init__(self, count_role, count_gx, count_gz):
        me_role, me_gx, me_gz = place("role"), place("gx"), place("gz")
        f32 = jnp.float32
        self.layers = LAYERS_PER_BLOCK * count_gz
        self.first = me_gz * LAYERS_PER_BLOCK
        self.z_top = jnp.where(me_gz == 0, 0.0, 1.0).astype(f32)
        self.z_bottom = jnp.where(me_gz == count_gz - 1, 0.0, 1.0).astype(f32)
        self.x_first = jnp.where(me_gx == 0, 0.0, 1.0).astype(f32)
        self.x_last = jnp.where(me_gx == count_gx - 1, 0.0, 1.0).astype(f32)
        self.y_first = jnp.where(me_role == 0, 0.0, 1.0).astype(f32)
        self.y_last = jnp.where(me_role == count_role - 1, 0.0, 1.0).astype(f32)
        self.exp_first = jnp.exp(jnp.zeros((8, COLS), f32) - me_gz.astype(f32))


def widened(value):
    return jnp.concatenate([value] + [value[ROWS:WIDE]] * ((COLS - WIDE) // EDGE), axis=0)


def main_region(count_role, count_gx, count_gz, planes, edge, *refs):
    land_in, refs = refs[: count_gz + 4], refs[count_gz + 4 :]
    out, inner, land_out, ha, hb, kc, mm, th, wd, sk = refs[:10]
    heat_finish = heat(count_gx, count_gz, *land_in, land_out, *refs[10:])
    spot = Where(count_role, count_gx, count_gz)
    z_top, z_bottom = spot.z_top, spot.z_bottom

    def wide(p):
        return jnp.concatenate([planes[p], edge[p]], axis=0)

    def put(ref, i, value):
        ref[i, 8 : 8 + WIDE] = value
        ref[i, 0:8] = value[ROWS:WIDE]
        ref[i, 8 + WIDE : 16 + WIDE] = value[0:8]

    row = lax.broadcasted_iota(jnp.int32, (8, COLS), 0)
    x_low = jnp.where(row == 0, spot.x_first, 1.0)
    x_high = jnp.where(row == 7, spot.x_last, 1.0)

    def fill(i, carry):
        put(ha, i, wide(H0 + i))
        return carry

    lax.fori_loop(0, NH, fill, 0)
    put(kc, 0, wide(K_LO))
    put(kc, NH - 1, wide(K_HI))

    def mean4(ref, i):
        return (ref[i, 8 : 8 + WIDE] + ref[i + 1, 8 : 8 + WIDE] + ref[i + 2, 8 : 8 + WIDE] + ref[i + 3, 8 : 8 + WIDE]) * 0.25

    heads = [wide(M_LO)] + [mean4(ha, HALO + 4 * q) for q in range(LAYERS_PER_BLOCK)] + [wide(M_HI)]
    base = jnp.concatenate([spot.exp_first] * (WIDE // 8), axis=0)
    for q, value in enumerate(uptake_of(wide(TP), wide(RT), heads, spot.layers, base, spot.first)):
        sk[q] = value

    def first_curves(j, theta):
        i = j + 1
        half_n = wide(N0 + j)
        expo = expo_of(half_n)
        mm[j] = expo
        satur, cond = curves(ha[i, 8 : 8 + WIDE], wide(A0 + j), half_n, wide(S0 + j), expo)
        put(kc, i, cond)
        if theta:
            th[j - 1] = wide(P0 + j - 1) * satur

    def later_curves(src, j, water):
        i = j + 1
        satur, cond = curves(src[i, 8 : 8 + WIDE], wide(A0 + j), wide(N0 + j), wide(S0 + j), mm[j])
        put(kc, i, cond)
        if water:
            wd[j - 1] = wide(P0 + j - 1) * satur - th[j - 1] + sk[(i + 1) // LEVELS_PER_LAYER]

    def stencil(src, i0, count, sweep, store):
        here = pl.ds(8, WIDE)
        conds = [kc[i0 + g - 1, here, :] for g in range(count + 2)]
        heads = [src[i0 + g - 1, here, :] for g in range(count + 2)]
        faces = [conds[g] + conds[g + 1] for g in range(count + 1)]
        faces[0] = faces[0] * jnp.where(i0 == HALO, z_top, jnp.where(i0 == HALO + LEVELS, z_bottom, 1.0))
        end = i0 + count
        faces[count] = faces[count] * jnp.where(
            end == HALO, z_top, jnp.where(end == HALO + LEVELS, z_bottom, 1.0)
        )
        for g in range(count):
            i = i0 + g
            head, cond = heads[g + 1], conds[g + 1]
            kf_up, kf_down = faces[g], faces[g + 1]
            kf_xm = cond + kc[i, pl.ds(7, WIDE), :]
            kf_xm = jnp.concatenate([kf_xm[0:8] * x_low, kf_xm[8:]], axis=0)
            kf_xp = cond + kc[i, pl.ds(9, WIDE), :]
            kf_xp = jnp.concatenate([kf_xp[: ROWS - 8], kf_xp[ROWS - 8 : ROWS] * x_high, kf_xp[ROWS:]], axis=0)
            kf_ym = cond + pltpu.roll(cond, 1, 1)
            kf_yp = cond + pltpu.roll(cond, COLS - 1, 1)
            inflow = kf_up * (heads[g] + 1.0) + kf_down * (heads[g + 2] - 1.0)
            inflow = inflow + (kf_xm * src[i, pl.ds(7, WIDE), :] + kf_xp * src[i, pl.ds(9, WIDE), :])
            inflow = inflow + (kf_ym * pltpu.roll(head, 1, 1) + kf_yp * pltpu.roll(head, COLS - 1, 1))
            lost = wd[i - 2] if sweep > 0 else sk[(i + 1) // LEVELS_PER_LAYER]
            diag = (1.0 + kf_up) + (kf_down + kf_xm) + (kf_xp + kf_ym) + kf_yp
            store(i, relax(head, inflow - lost, diag, sweep))

    def loop(lo, hi, body, unroll=1):
        def step(i, carry):
            body(i)
            return carry

        lax.fori_loop(lo, hi, step, 0, unroll=unroll)

    def levels_of(src, sweep, store):
        extra = SWEEPS - 1 - sweep
        if extra:
            stencil(src, HALO - extra, extra, sweep, store)
        loop(0, LEVELS // 4, lambda k: stencil(src, HALO + 4 * k, 4, sweep, store))
        if extra:
            stencil(src, HALO + LEVELS, extra, sweep, store)

    first_curves(0, False)
    loop(1, NC - 1, lambda j: first_curves(j, True), 3)
    first_curves(NC - 1, False)
    levels_of(ha, 0, lambda i, value: put(hb, i, value))

    lane_wide = lax.broadcasted_iota(jnp.int32, (WIDE, COLS), 1)
    acc = jnp.zeros((WIDE, COLS), jnp.float32)
    for k in range(NC):
        lane = inner_lane(k)
        pick = (lane_wide == lane) | (lane_wide == lane + 9)
        acc = jnp.where(pick, pltpu.roll(hb[k + 1, 8 : 8 + WIDE], (lane - (COLS - 1 - NEAR)) % COLS, 1), acc)
    inner[...] = widened(acc).T

    later_curves(hb, 0, False)
    loop(1, NC - 1, lambda j: later_curves(hb, j, True), 3)
    later_curves(hb, NC - 1, False)
    levels_of(hb, 1, lambda i, value: put(ha, i, value))
    loop(1, NC - 1, lambda j: later_curves(ha, j, True), 3)

    def keep(i, value):
        out[i - HALO] = value[0:ROWS]

    levels_of(ha, 2, keep)
    heat_finish()


def edge_strips(count_role, count_gx, count_gz, main, inner, strips_in, y_e, y_o, out,
                strips, sa, sb, sc, ks, sm, sth, swd, ssk, turn, done, sem):
    spot = Where(count_role, count_gx, count_gz)
    z_top, z_bottom = spot.z_top, spot.z_bottom
    f32 = jnp.float32
    strips[...] = strips_in[...]

    def take(high, low):
        for p in range(PLANES):
            strips[pl.ds(p * SIDE, HALO), :] = high[pl.ds(p * HALO, HALO), :]
            strips[pl.ds(p * SIDE + SIDE - HALO, HALO), :] = low[pl.ds(p * HALO, HALO), :]

    by_parity("role", take, y_e, y_o)

    def strip(p, count=1):
        return strips[p * SIDE : (p + count) * SIDE, :]

    heads = [strip(M_LO)]
    for q in range(LAYERS_PER_BLOCK):
        at = H0 + HALO + 4 * q
        heads.append((strip(at) + strip(at + 1) + strip(at + 2) + strip(at + 3)) * 0.25)
    heads.append(strip(M_HI))
    base = jnp.concatenate([spot.exp_first] * 2, axis=0)
    for q, value in enumerate(uptake_of(strip(TP), strip(RT), heads, spot.layers, base, spot.first)):
        ssk[q * SIDE : (q + 1) * SIDE, :] = value

    lane = lax.broadcasted_iota(jnp.int32, (SIDE, COLS), 1)
    srow = lax.broadcasted_iota(jnp.int32, (SIDE, COLS), 0)
    s_xm = jnp.where(lane == 0, spot.x_first, 1.0)
    s_xp = jnp.where(lane == ROWS - 1, spot.x_last, 1.0)
    side_mask = jnp.where(srow < 8, spot.y_last, spot.y_first)
    s_ym = jnp.where(srow % 8 == 0, side_mask, 1.0)
    s_yp = jnp.where(srow % 8 == 7, side_mask, 1.0)

    def tiled(mask, count):
        return jnp.concatenate([mask] * count, axis=0)

    def y_shift(value, by):
        parts = value.reshape(value.shape[0] // 8, 8, COLS)
        return pltpu.roll(parts, by, 1).reshape(value.shape)

    def rows_of(i, count):
        return slice(i * SIDE, (i + count) * SIDE)

    def strip_curves(src, lo, hi, sweep):
        i = lo
        while i < hi:
            count = min(5, hi - i)
            j = i - 1
            here = rows_of(i, count)
            half_n = strip(N0 + j, count)
            if sweep == 0:
                expo = expo_of(half_n)
                sm[rows_of(j, count), :] = expo
            else:
                expo = sm[rows_of(j, count), :]
            satur, cond = curves(src[here, :], strip(A0 + j, count), half_n, strip(S0 + j, count), expo)
            ks[here, :] = cond
            start, stop = max(i, 2), min(i + count, NH - 2)
            if stop > start:
                part = satur[(start - i) * SIDE : (stop - i) * SIDE]
                water = strip(P0 + start - 2, stop - start) * part
                at = rows_of(start - 2, stop - start)
                if sweep == 0:
                    sth[at, :] = water
                else:
                    swd[at, :] = water - sth[at, :]
            i += count

    def strip_stencil(src, dst, lo, hi, sweep):
        i = lo
        while i < hi:
            count = min(5, hi - i)
            here = rows_of(i, count)
            above, below = rows_of(i - 1, count), rows_of(i + 1, count)
            head, cond = src[here, :], ks[here, :]
            kf_up = cond + ks[above, :]
            kf_down = cond + ks[below, :]
            if i <= HALO < i + count:
                level = lax.broadcasted_iota(jnp.int32, kf_up.shape, 0) // SIDE
                kf_up = jnp.where(level == HALO - i, kf_up * z_top, kf_up)
            if i <= HALO + LEVELS - 1 < i + count:
                level = lax.broadcasted_iota(jnp.int32, kf_up.shape, 0) // SIDE
                kf_down = jnp.where(level == HALO + LEVELS - 1 - i, kf_down * z_bottom, kf_down)
            kf_xm = (cond + pltpu.roll(cond, 1, 1)) * tiled(s_xm, count)
            kf_xp = (cond + pltpu.roll(cond, COLS - 1, 1)) * tiled(s_xp, count)
            kf_ym = (cond + y_shift(cond, 1)) * tiled(s_ym, count)
            kf_yp = (cond + y_shift(cond, 7)) * tiled(s_yp, count)
            inflow = kf_up * (src[above, :] + 1.0) + kf_down * (src[below, :] - 1.0)
            inflow = inflow + (kf_xm * pltpu.roll(head, 1, 1) + kf_xp * pltpu.roll(head, COLS - 1, 1))
            inflow = inflow + (kf_ym * y_shift(head, 1) + kf_yp * y_shift(head, 7))
            lost = jnp.concatenate([ssk[rows_of((k + 1) // LEVELS_PER_LAYER, 1), :] for k in range(i, i + count)], axis=0)
            if sweep > 0:
                lost = lost + swd[rows_of(i - 2, count), :]
            diag = (1.0 + kf_up) + (kf_down + kf_xm) + (kf_xp + kf_ym) + kf_yp
            dst[here, :] = relax(head, inflow - lost, diag, sweep)
            i += count

    ks[rows_of(0, 1), :] = strip(K_LO)
    ks[rows_of(NH - 1, 1), :] = strip(K_HI)
    strip_curves(strips, 1, NH - 1, 0)
    strip_stencil(strips, sa, 1, NH - 1, 0)
    for k in range(NC):
        lane = inner_lane(k)
        sa[pl.ds((k + 1) * SIDE + 3, 1), :] = inner[pl.ds(lane, 1), :]
        sa[pl.ds((k + 1) * SIDE + 8 + NEAR, 1), :] = inner[pl.ds(lane + 9, 1), :]
    strip_curves(sa, 1, NH - 1, 1)
    strip_stencil(sa, sb, 2, NH - 2, 1)
    strip_curves(sb, 2, NH - 2, 2)
    strip_stencil(sb, sc, 3, NH - 3, 2)

    pieces = [sc[i * SIDE + 8 - HALO : i * SIDE + 8 + HALO, :] for i in range(HALO, HALO + LEVELS)]
    pieces.append(jnp.zeros((COLS - 2 * HALO * LEVELS, COLS), f32))
    turn[...] = jnp.concatenate(pieces, axis=0).T[0:ROWS]
    lane_rows = lax.broadcasted_iota(jnp.int32, (ROWS, COLS), 1)
    outer = (lane_rows < HALO) | (lane_rows >= COLS - HALO)
    copies = []
    for level in range(LEVELS):
        moved = pltpu.roll(turn[...], (COLS - HALO - 2 * HALO * level) % COLS, 1)
        done[level] = jnp.where(outer, moved, main[level])
        copy = pltpu.make_async_copy(done.at[level], out.at[level], sem.at[level])
        copy.start()
        copies.append(copy)
    for copy in copies:
        copy.wait()


def heat(count_gx, count_gz, *refs):
    parts, refs = refs[:count_gz], refs[count_gz:]
    temp_in, tr_in, air_in, rt_in, out, sat, head, temp, tr, air, rt, y, sem = refs
    copies = []
    for dist, part in enumerate(parts):
        for gx in range(count_gx):
            copy = pltpu.make_async_copy(
                part.at[pl.ds(gx * PIECE, PIECE)], y.at[gx * count_gz + dist], sem.at[len(copies)]
            )
            copy.start()
            copies.append(copy)
    for src, dst in ((temp_in, temp), (tr_in, tr), (air_in, air), (rt_in, rt)):
        copy = pltpu.make_async_copy(src, dst, sem.at[len(copies)])
        copy.start()
        copies.append(copy)
    def finish():
        me = place("gx") * count_gz + place("gz")
        layers = LAYERS_PER_BLOCK * count_gz
        for copy in copies:
            copy.wait()
        for gx in range(count_gx):
            for gz in range(count_gz):
                j = me ^ (gx * count_gz + gz)
                for c in range(CAP):
                    tile = y[j, c * 8 : c * 8 + 8]
                    at = pl.ds(gz * LAYERS_PER_BLOCK, LAYERS_PER_BLOCK)
                    sat[gx * CAP + c, at, :] = tile[0:LAYERS_PER_BLOCK]
                    head[gx * CAP + c, at, :] = tile[LAYERS_PER_BLOCK : 2 * LAYERS_PER_BLOCK]
        layer = lax.broadcasted_iota(jnp.int32, (layers, COLS), 0)
        decay = jnp.exp(layer.astype(jnp.float32) * -0.25)
        for slot in range(count_gx * CAP):
            roots = jnp.broadcast_to(rt[slot], (layers, COLS))
            weight = jnp.where(layer < roots, decay, 0.0)
            weight = weight / jnp.sum(weight, axis=0, keepdims=True)
            stress = 1.0 / (1.0 + head[slot] * head[slot] * (1.0 / 2.25))
            uptake = tr[slot] * weight * stress
            kappa = 0.25 + 0.9 * sat[slot]
            top = jnp.broadcast_to(air[slot], (layers, COLS))
            k_above = jnp.where(layer == 0, kappa, 0.5 * (kappa + pltpu.roll(kappa, 1, 0)))
            k_below = jnp.where(layer == layers - 1, 0.0, 0.5 * (kappa + pltpu.roll(kappa, layers - 1, 0)))
            old = temp[slot]
            new = old
            for _ in range(HEAT_STEPS):
                above = jnp.where(layer == 0, top, pltpu.roll(new, 1, 0))
                below = pltpu.roll(new, layers - 1, 0)
                new = new + 0.2 * (k_above * (above - new) + k_below * (below - new)) - 0.3 * uptake
            out[slot] = jnp.where(sat[slot] >= 0.0, new, old)

    return finish


def call(body, outs, ins, scratch=(), aliases=None, limit=40 * MIB, kept=True, work=0):
    return pl.pallas_call(
        body,
        out_shape=[pltpu.VMEM(shape, jnp.float32) if kept else jax.ShapeDtypeStruct(shape, jnp.float32) for shape in outs],
        in_specs=ins,
        out_specs=[VMEM] * len(outs),
        scratch_shapes=list(scratch),
        input_output_aliases=aliases or {},
        compiler_params=pltpu.CompilerParams(vmem_limit_bytes=limit),
        cost_estimate=pl.CostEstimate(flops=work, bytes_accessed=work, transcendentals=0) if work else None,
    )


def main_call(count_role, count_gx, count_gz):
    f32 = jnp.float32
    deep = WIDE + 16
    slots = count_gx * CAP
    land_shape = (slots, LAYERS_PER_BLOCK * count_gz, COLS)
    groups = count_gx * count_gz
    return pl.pallas_call(
        functools.partial(main_region, count_role, count_gx, count_gz),
        out_shape=[
            pltpu.VMEM((LEVELS, ROWS, COLS), f32),
            pltpu.VMEM((COLS, COLS), f32),
            jax.ShapeDtypeStruct(land_shape, f32),
        ],
        in_specs=[VMEM] * 2 + [HBM] * (count_gz + 4),
        out_specs=[VMEM] * 3,
        scratch_shapes=[
            pltpu.VMEM((NH, deep, COLS), f32),
            pltpu.VMEM((NH, deep, COLS), f32),
            pltpu.VMEM((NH, deep, COLS), f32),
            pltpu.VMEM((NC, WIDE, COLS), f32),
            pltpu.VMEM((NP, WIDE, COLS), f32),
            pltpu.VMEM((NP, WIDE, COLS), f32),
            pltpu.VMEM((LAYERS_PER_BLOCK + 2, WIDE, COLS), f32),
            pltpu.VMEM(land_shape, f32),
            pltpu.VMEM(land_shape, f32),
            pltpu.VMEM(land_shape, f32),
            pltpu.VMEM((slots, 1, COLS), f32),
            pltpu.VMEM((slots, 1, COLS), f32),
            pltpu.VMEM((slots, 1, COLS), jnp.int32),
            pltpu.VMEM((groups, PIECE, COLS), f32),
            pltpu.SemaphoreType.DMA((4 + groups,)),
        ],
        compiler_params=pltpu.CompilerParams(vmem_limit_bytes=40 * MIB),
    )


def strip_call(count_role, count_gx, count_gz):
    f32 = jnp.float32
    return pl.pallas_call(
        functools.partial(edge_strips, count_role, count_gx, count_gz),
        out_shape=jax.ShapeDtypeStruct((LEVELS, ROWS, COLS), f32),
        in_specs=[VMEM] * 5,
        out_specs=HBM,
        scratch_shapes=[
            pltpu.VMEM((PACKS * COLS, COLS), f32),
            pltpu.VMEM((NH * SIDE, COLS), f32),
            pltpu.VMEM((NH * SIDE, COLS), f32),
            pltpu.VMEM((NH * SIDE, COLS), f32),
            pltpu.VMEM((NH * SIDE, COLS), f32),
            pltpu.VMEM((NC * SIDE, COLS), f32),
            pltpu.VMEM((NP * SIDE, COLS), f32),
            pltpu.VMEM((NP * SIDE, COLS), f32),
            pltpu.VMEM(((LAYERS_PER_BLOCK + 2) * SIDE, COLS), f32),
            pltpu.VMEM((ROWS, COLS), f32),
            pltpu.VMEM((LEVELS, ROWS, COLS), f32),
            pltpu.SemaphoreType.DMA((LEVELS,)),
        ],
        compiler_params=pltpu.CompilerParams(vmem_limit_bytes=40 * MIB),
    )


def local(h, a, n, s, p, tile_owner, land_temp, tr, air, rt):
    sizes = tuple(lax.axis_size(axis) for axis in AXES)
    count_role, count_gx, count_gz = sizes
    groups = count_gx * count_gz
    slots = count_gx * CAP
    f32 = jnp.float32

    def swap(value, axis, odd):
        return lax.ppermute(value, AXES, pairing(sizes, axis, odd))

    owners = tile_owner.T
    land = (land_temp[0, 0], tr[0, 0, :, None], air[0, 0, :, None], rt[0, 0, :, None])
    h, a, n, s, p = (pltpu.with_memory_space_constraint(x, pltpu.HBM) for x in (h, a, n, s, p))
    land_temp, tr, air, rt = (pltpu.with_memory_space_constraint(x, pltpu.HBM) for x in land)

    z_send_e, z_send_o = call(
        z_faces,
        [(Z_SEND, ROWS, COLS)] * 2,
        [HBM] * 5,
        [
            pltpu.VMEM((2, 4, ROWS, COLS), f32),
            pltpu.VMEM((2, 3, ROWS, COLS), f32),
            pltpu.VMEM((2, 3, ROWS, COLS), f32),
            pltpu.VMEM((2, 3, ROWS, COLS), f32),
            pltpu.VMEM((2, 1, ROWS, COLS), f32),
            pltpu.SemaphoreType.DMA((10,)),
        ],
    )(h, a, n, s, p)
    z_e = swap(z_send_e, "gz", False)
    z_o = swap(z_send_o, "gz", True) if count_gz > 2 else z_e

    half = groups // 2
    blocks = count_gx // 2
    packed = half * 8 * CAP + blocks * 8
    def land_stage():
        send, keep, hot = call(
            functools.partial(land_pack, count_gx, count_gz),
            [(packed, COLS), (packed, COLS), (ROWS, groups * 8)],
            [SMEM] + [HBM] * 5,
            [
                pltpu.VMEM((2 * LAYERS_PER_BLOCK, ROWS, COLS), f32),
                pltpu.SMEM((groups,), jnp.int32),
                pltpu.SMEM((groups * CAP,), jnp.int32),
                pltpu.VMEM((LEVELS, ROWS, COLS), f32),
                pltpu.VMEM((LEVELS, ROWS, COLS), f32),
                pltpu.VMEM((LEVELS, ROWS, COLS), f32),
                pltpu.VMEM((slots, 1, COLS), f32),
                pltpu.VMEM((slots, 1, COLS), jnp.int32),
                pltpu.SemaphoreType.DMA((5,)),
            ],
        )(owners, h, a, n, tr, rt)

        got = lax.ppermute(send, AXES, xor_pairs(sizes, "gx", blocks))
        bit = blocks // 2
        if bit:
            pieces = [part[j * PIECE : (j + 1) * PIECE] for part in (keep, got) for j in range(half)]
            base = half * PIECE
            values = [part[base + j * 8 : base + (j + 1) * 8] for part in (keep, got) for j in range(blocks)]
            while bit:
                moving = [j for j in range(groups) if (j // count_gz) & bit]
                t_moving = [j for j in range(count_gx) if j & bit]
                sent = jnp.concatenate([pieces[j] for j in moving] + [values[j] for j in t_moving], axis=0)
                got = lax.ppermute(sent, AXES, xor_pairs(sizes, "gx", bit))
                for k, j in enumerate(moving):
                    pieces[j] = got[k * PIECE : (k + 1) * PIECE]
                for k, j in enumerate(t_moving):
                    base = len(moving) * PIECE + k * 8
                    values[j] = got[base : base + 8]
                bit //= 2
            keep = jnp.concatenate(pieces[:half] + values[:blocks], axis=0)
            got = jnp.concatenate(pieces[half:] + values[blocks:], axis=0)
        parts = call(
            functools.partial(land_sort, count_gx, count_gz),
            [(count_gx * (PIECE + 8), COLS)] * count_gz,
            [VMEM] * 2,
        )(keep, got)
        parts = [parts[0]] + [
            lax.ppermute(parts[dist], AXES, xor_pairs(sizes, "gz", dist)) for dist in range(1, count_gz)
        ]
        (tile,) = call(
            functools.partial(tile_values, count_gx, count_gz),
            [(2, ROWS, COLS)],
            [VMEM] * (1 + count_gz),
        )(hot, *parts)
        return [tile] + parts

    def no_land_stage():
        shapes = [(2, ROWS, COLS)] + [(count_gx * (PIECE + 8), COLS)] * count_gz
        return [jnp.zeros(shape, f32) for shape in shapes]

    ahead = lax.optimization_barrier(jnp.bool_(True))
    tile, *parts = lax.cond(ahead, land_stage, no_land_stage)
    parts = [pltpu.with_memory_space_constraint(x, pltpu.HBM) for x in parts]

    x_count = 1 if count_gx == 2 else 2
    x_shape = (PLANES, 4, COLS)
    edges = call(
        functools.partial(own_edges, count_gx),
        [x_shape] * x_count,
        [HBM] * 5,
        [pltpu.VMEM((2, 5, LEVELS, 8, COLS), f32), pltpu.SemaphoreType.DMA((10,))],
    )(h, a, n, s, p)
    x_sends = call(
        functools.partial(x_faces, count_gx),
        [x_shape] * x_count,
        [VMEM] * (3 + x_count),
        aliases={3 + k: k for k in range(x_count)},
    )(z_e, z_o, tile, *edges)
    (planes,) = call(
        all_planes,
        [(PLANES, ROWS, COLS)],
        [HBM] * 5 + [VMEM] * 3,
        [pltpu.SemaphoreType.DMA((5,))],
    )(h, a, n, s, p, z_e, z_o, tile)
    x_got = [swap(value, "gx", bool(k)) for k, value in enumerate(x_sends)]

    edge, strips, y_send_e, y_send_o = call(
        functools.partial(y_faces, count_gx),
        [(PLANES, EDGE, COLS), (PACKS * COLS, COLS), (Y_SEND, COLS), (Y_SEND, COLS)],
        [VMEM] * (1 + x_count),
    )(planes, *x_got)
    y_e = swap(y_send_e, "role", False)
    y_o = swap(y_send_o, "role", True) if count_role > 2 else y_e

    main, inner, land_new = main_call(*sizes)(planes, edge, *parts, land_temp, tr, air, rt)
    head = strip_call(*sizes)(main, inner, strips, y_e, y_o)
    return (head, land_new[None, None])


def solution(mesh):
    in_specs = (
        P("gz", "gx", "role"),
        P("gz", "gx", "role"),
        P("gz", "gx", "role"),
        P("gz", "gx", "role"),
        P("gz", "gx", "role"),
        P(),
        P("role", ("gx", "gz"), None, None, None),
        P("role", ("gx", "gz"), None, None),
        P("role", ("gx", "gz"), None, None),
        P("role", ("gx", "gz"), None, None),
    )
    out_specs = (P("gz", "gx", "role"), P("role", ("gx", "gz"), None, None, None))
    return jax.shard_map(local, mesh=mesh, in_specs=in_specs, out_specs=out_specs, check_vma=False)
```

```python
import functools
import math

import jax
import jax.numpy as jnp
from jax import lax
from jax.experimental import pallas as pl
from jax.experimental.pallas import tpu as pltpu
from jax.sharding import PartitionSpec as P

LAYERS_PER_BLOCK = 4
LEVELS_PER_LAYER = 4
CAP = 3
SWEEPS = 3
HEAT_STEPS = 4
HALO = SWEEPS
AXES = ("role", "gx", "gz")
VMEM = pl.BlockSpec(memory_space=pltpu.VMEM)
SMEM = pl.BlockSpec(memory_space=pltpu.SMEM)
HBM = pl.BlockSpec(memory_space=pltpu.HBM)
ANY = pl.BlockSpec(memory_space=pl.ANY)
MIB = 1024 * 1024

LEVELS = 16
ROWS = 64
COLS = 128
EDGE = 8
WIDE = ROWS + EDGE
H0 = 0
NH = LEVELS + 2 * HALO
A0 = H0 + NH
NC = LEVELS + 2 * HALO - 2
N0 = A0 + NC
S0 = N0 + NC
K_LO = S0 + NC
K_HI = K_LO + 1
P0 = K_HI + 1
NP = LEVELS + 2 * HALO - 4
M_LO = P0 + NP
M_HI = M_LO + 1
TP = M_HI + 1
RT = TP + 1
PLANES = RT + 1
PACKS = (PLANES + 7) // 8
SIDE = 16
NEAR = 4
Z_SEND = 12
PIECE = 8 * CAP
Y_SEND = (PLANES * HALO + 7) // 8 * 8


def omega(sweep):
    return 1.0 / (1.0 + 0.6 * math.cos(math.pi * (2 * sweep + 1) / (2 * SWEEPS)))


def place(axis):
    return lax.axis_index(axis)


def is_even(axis):
    return lax.rem(place(axis), 2) == 0


def pairing(sizes, axis, odd):
    pairs = []
    which = AXES.index(axis)
    for index in range(math.prod(sizes)):
        at = [index // (sizes[1] * sizes[2]), index // sizes[2] % sizes[1], index % sizes[2]]
        count = sizes[which]
        there = list(at)
        if not odd:
            there[which] = at[which] ^ 1
        else:
            there[which] = at[which] + (1 if at[which] % 2 else -1)
            if not 0 <= there[which] < count:
                there = list(at)
                if axis == "gx":
                    there[1] = count - 1 - at[1]
                else:
                    there[1] = at[1] ^ 1
        pairs.append((index, (there[0] * sizes[1] + there[1]) * sizes[2] + there[2]))
    return pairs


def xor_pairs(sizes, axis, bit):
    pairs = []
    which = AXES.index(axis)
    for index in range(math.prod(sizes)):
        at = [index // (sizes[1] * sizes[2]), index // sizes[2] % sizes[1], index % sizes[2]]
        at[which] ^= bit
        pairs.append((index, (at[0] * sizes[1] + at[1]) * sizes[2] + at[2]))
    return pairs


def curves(head, alpha2, half_n, half_ks, expo):
    logx = half_n * jnp.log(alpha2 * (head * head + 0.01))
    softer = jnp.log(1.0 + jnp.exp(logx))
    root = jnp.exp(-0.5 * expo * softer)
    gap = 1.0 - jnp.exp(expo * (logx - softer))
    return root * root, half_ks * root * (gap * gap)


def inverse(value):
    guess = pl.reciprocal(value, approx=True)
    return guess * (2.0 - value * guess)


def expo_of(half_n):
    return 1.0 - 0.5 * inverse(half_n)


def relax(head, inflow, diag, sweep):
    step = omega(sweep)
    return (1.0 - step) * head + (step * (head + inflow)) * inverse(diag)


def z_faces(h, a, n, s, p, out_e, out_o, hb, ab, nb, sb, pb, sem):
    copies = []
    for side in range(2):
        for src, dst, count in ((h, hb, 4), (a, ab, 3), (n, nb, 3), (s, sb, 3), (p, pb, 1)):
            start = 0 if side == 0 else LEVELS - count
            copy = pltpu.make_async_copy(src.at[pl.ds(start, count)], dst.at[side], sem.at[len(copies)])
            copy.start()
            copies.append(copy)
    for copy in copies:
        copy.wait()

    def put(out, side):
        def level(buf, count, dist):
            return buf[side, dist - 1 if side == 0 else count - dist]

        for dist in (1, 2, 3):
            out[dist - 1] = level(hb, 4, dist)
        for dist in (1, 2):
            alpha = level(ab, 3, dist)
            out[2 + dist] = alpha * alpha
            out[4 + dist] = 0.5 * level(nb, 3, dist)
            out[6 + dist] = 0.5 * level(sb, 3, dist)
        out[9] = level(pb, 1, 1)
        alpha = level(ab, 3, 3)
        half_n = 0.5 * level(nb, 3, 3)
        out[10] = curves(level(hb, 4, 3), alpha * alpha, half_n, 0.5 * level(sb, 3, 3), expo_of(half_n))[1]
        out[11] = (hb[side, 0] + hb[side, 1] + hb[side, 2] + hb[side, 3]) * 0.25

    even = is_even("gz")

    @pl.when(even)
    def _():
        put(out_e, 1)
        put(out_o, 0)

    @pl.when(jnp.logical_not(even))
    def _():
        put(out_e, 0)
        put(out_o, 1)


def land_pack(count_gx, count_gz, owners, h_in, a_in, n_in, tr_in, rt_in, send, keep, hot,
              means, counts, slots, h, a, n, tr, rt, sem):
    groups = count_gx * count_gz
    me_role, me_gx = place("role"), place("gx")
    me = me_gx * count_gz + place("gz")
    copies = []
    for layer in range(LAYERS_PER_BLOCK):
        some = pl.ds(layer * LEVELS_PER_LAYER, LEVELS_PER_LAYER)
        for src, dst in ((h_in, h), (a_in, a), (n_in, n)):
            copies.append(pltpu.make_async_copy(src.at[some], dst.at[some], sem.at[len(copies)]))
    for src, dst in ((tr_in, tr), (rt_in, rt)):
        copies.append(pltpu.make_async_copy(src, dst, sem.at[len(copies)]))
    for copy in copies:
        copy.start()

    def clear_slot(i, carry):
        slots[i] = -1
        return carry

    def clear_count(i, carry):
        counts[i] = 0
        return carry

    lax.fori_loop(0, groups * CAP, clear_slot, 0)
    lax.fori_loop(0, groups, clear_count, 0)
    lane = lax.broadcasted_iota(jnp.int32, (1, groups * 8), 1)

    def step(x, carry):
        owner = owners[me_role, me_gx * ROWS + x]
        safe = jnp.maximum(owner, 0)
        rank = counts[safe]
        at = jnp.where(owner >= 0, (me ^ owner) * 8 + 2 * rank, -1)
        hot[pl.ds(x, 1), :] = jnp.where(lane == at, 1.0, 0.0)

        @pl.when(owner >= 0)
        def _():
            counts[owner] = rank + 1
            slots[owner * CAP + rank] = x

        return carry

    lax.fori_loop(0, ROWS, step, 0)
    for layer in range(LAYERS_PER_BLOCK):
        for copy in copies[3 * layer : 3 * layer + 3]:
            copy.wait()
        saturs = []
        heads = []
        for level in range(layer * LEVELS_PER_LAYER, (layer + 1) * LEVELS_PER_LAYER):
            head = h[level]
            alpha = a[level]
            half_n = 0.5 * n[level]
            logx = half_n * jnp.log(alpha * alpha * (head * head + 0.01))
            softer = jnp.log(1.0 + jnp.exp(logx))
            saturs.append(jnp.exp(-expo_of(half_n) * softer))
            heads.append(head)
        means[layer] = (saturs[0] + saturs[1] + saturs[2] + saturs[3]) * 0.25
        means[LAYERS_PER_BLOCK + layer] = (heads[0] + heads[1] + heads[2] + heads[3]) * 0.25
    for copy in copies[3 * LAYERS_PER_BLOCK :]:
        copy.wait()
    half = groups // 2
    for j in range(groups):
        out, k = (keep, j) if j < half else (send, j - half)
        for c in range(CAP):
            row = slots[(me ^ j) * CAP + c]
            safe = jnp.maximum(row, 0)
            for q in range(8):
                value = means[q, pl.ds(safe, 1), :]
                out[pl.ds(k * PIECE + c * 8 + q, 1), :] = jnp.where(row >= 0, value, -1.0)
    blocks = count_gx // 2
    for j in range(count_gx):
        block = me_gx ^ j
        out, k = (keep, j) if j < blocks else (send, j - blocks)
        base = half * PIECE + k * 8
        out[pl.ds(base, 8), :] = jnp.zeros((8, COLS), jnp.float32)
        for c in range(CAP):
            out[pl.ds(base + 2 * c, 1), :] = tr[block * CAP + c]
            out[pl.ds(base + 2 * c + 1, 1), :] = rt[block * CAP + c].astype(jnp.float32)


def land_sort(count_gx, count_gz, keep, got, *outs):
    half, blocks = count_gx * count_gz // 2, count_gx // 2
    for gx in range(count_gx):
        src, k = (keep, gx) if gx < blocks else (got, gx - blocks)
        for dist in range(count_gz):
            at = (k * count_gz + dist) * PIECE
            outs[dist][gx * PIECE : (gx + 1) * PIECE] = src[at : at + PIECE]
            base = count_gx * PIECE + gx * 8
            outs[dist][base : base + 8] = src[half * PIECE + k * 8 : half * PIECE + k * 8 + 8]


def tile_values(count_gx, count_gz, hot, *refs):
    parts, out, y = refs[:count_gz], refs[count_gz], refs[count_gz + 1]
    values = []
    for gx in range(count_gx):
        for dist in range(count_gz):
            base = count_gx * PIECE + gx * 8
            values.append(parts[dist][base : base + 8])
            y[gx * count_gz + dist] = parts[dist][gx * PIECE : (gx + 1) * PIECE]
    t = jnp.concatenate(values, axis=0)
    out[0] = exact_dot(hot[...], t)
    out[1] = jnp.maximum(exact_dot(hot[...], pltpu.roll(t, t.shape[0] - 1, 0)), 1.0)


def exact_dot(hot, values):
    total = None
    rest = values
    left = hot.astype(jnp.bfloat16)
    for _ in range(3):
        part = rest.astype(jnp.bfloat16)
        rest = rest - part.astype(jnp.float32)
        term = jnp.dot(left, part, preferred_element_type=jnp.float32)
        total = term if total is None else total + term
    return total


def z_places(low):
    places = [H0 + (HALO - dist if low else HALO + LEVELS - 1 + dist) for dist in (1, 2, 3)]
    for first in (A0, N0, S0):
        places += [first + (HALO - 1 - dist if low else HALO - 2 + LEVELS + dist) for dist in (1, 2)]
    return places + [P0 + (0 if low else NP - 1), K_LO if low else K_HI, M_LO if low else M_HI]


def by_parity(axis, action, first, second):
    even = is_even(axis)

    @pl.when(even)
    def _():
        action(first, second)

    @pl.when(jnp.logical_not(even))
    def _():
        action(second, first)


OWN = (H0 + HALO, A0 + HALO - 1, N0 + HALO - 1, S0 + HALO - 1, P0 + HALO - 2)


def scaled(k, value):
    return (value, value * value, 0.5 * value, 0.5 * value, value)[k]


def packed_tile(tile, rows_of, count):
    lane_group = lax.broadcasted_iota(jnp.int32, (count, COLS), 1) // SIDE
    acc = jnp.zeros((count, COLS), jnp.float32)
    for j in range(8):
        p = tile * 8 + j
        value = rows_of(p) if p < PLANES else None
        if value is not None:
            acc = jnp.where(lane_group == j, pltpu.roll(value, SIDE * j + 8, 1), acc)
    return acc


OWN_AT = {first + level: k * LEVELS + level for k, first in enumerate(OWN) for level in range(LEVELS)}
EXT_AT = {p: k for k, p in enumerate(p for p in range(PLANES) if p not in OWN_AT)}


def own_planes(*refs):
    arrays, own, sem = refs[:5], refs[5], refs[6]
    copies = []
    for k, src in enumerate(arrays):
        copy = pltpu.make_async_copy(src, own.at[pl.ds(k * LEVELS, LEVELS)], sem.at[k])
        copy.start()
        copies.append(copy)
    for k, copy in enumerate(copies):
        copy.wait()
        if 0 < k < 4:
            for level in range(LEVELS):
                own[k * LEVELS + level] = scaled(k, own[k * LEVELS + level])


def own_part(*refs):
    arrays, rim, pack, own, sem = refs[:5], refs[5], refs[6], refs[7], refs[8]
    own_planes(*arrays, own, sem)
    for k in range(len(OWN_AT)):
        rim[k, 0:8] = own[k, 0:8]
        rim[k, 8:16] = own[k, ROWS - 8 : ROWS]
    for t in range(PACKS):
        pack[t] = packed_tile(t, lambda p: own[OWN_AT[p]] if p in OWN_AT else None, ROWS)


def x_faces(count_gx, rim, z_e, z_o, tile, ext, *sends):
    def take(upper, lower):
        for got, places in ((upper, z_places(False)), (lower, z_places(True))):
            for k, p in enumerate(places):
                ext[EXT_AT[p]] = got[k]

    by_parity("gz", take, z_e, z_o)
    ext[EXT_AT[TP]] = tile[0]
    ext[EXT_AT[RT]] = tile[1]

    def put(high, low):
        for p in range(PLANES):
            src, k, rows = (rim, OWN_AT[p], 16) if p in OWN_AT else (ext, EXT_AT[p], ROWS)
            if high is not None:
                high[p, pl.ds(0, HALO), :] = src[k, pl.ds(rows - HALO, HALO), :]
            if low is not None:
                low[p, pl.ds(0, HALO), :] = src[k, pl.ds(0, HALO), :]

    by_parity("gx", put, sends[0], sends[1] if count_gx > 2 else None)


def y_faces(count_gx, *refs):
    rim, own_pack, ext = refs[:3]
    if count_gx > 2:
        got_e, got_o = refs[4], refs[5]
    else:
        got_e, got_o = refs[4], None
    edge, strips, send_e, send_o = refs[-4:]

    def take(high, low):
        for p in range(PLANES):
            edge[p] = rim[OWN_AT[p], 8:16] if p in OWN_AT else ext[EXT_AT[p], ROWS - EDGE : ROWS]
            if high is not None:
                edge[p, pl.ds(0, HALO), :] = high[p, pl.ds(0, HALO), :]
            if low is not None:
                edge[p, pl.ds(EDGE - HALO, HALO), :] = low[p, pl.ds(0, HALO), :]

    even_x = is_even("gx")

    @pl.when(even_x)
    def _():
        take(got_e, got_o)

    @pl.when(jnp.logical_not(even_x))
    def _():
        take(got_o, got_e)

    group = lax.broadcasted_iota(jnp.int32, (ROWS, COLS), 1) // SIDE
    for t in range(PACKS):
        rows = own_pack[t]
        for j in range(8):
            p = t * 8 + j
            if p in EXT_AT:
                rows = jnp.where(group == j, pltpu.roll(ext[EXT_AT[p]], SIDE * j + 8, 1), rows)
        last = packed_tile(t, lambda p: edge[p], EDGE)
        full = widened(jnp.concatenate([rows, last], axis=0))
        strips[t * COLS : (t + 1) * COLS, :] = full.T

    def put(send, last):
        start = 5 if last else 8
        for p in range(PLANES):
            send[pl.ds(p * HALO, HALO), :] = strips[pl.ds(p * SIDE + start, HALO), :]
        rest = Y_SEND - PLANES * HALO
        if rest:
            send[pl.ds(PLANES * HALO, rest), :] = jnp.zeros((rest, COLS), jnp.float32)

    even_y = is_even("role")

    @pl.when(even_y)
    def _():
        put(send_e, True)
        put(send_o, False)

    @pl.when(jnp.logical_not(even_y))
    def _():
        put(send_e, False)
        put(send_o, True)


def uptake_of(tpot, roots, head, layers, base_exp, first):
    total = jnp.zeros_like(tpot)
    for layer in range(layers):
        total = total + jnp.where(roots > float(layer), math.exp(-layer / 4.0), 0.0)
    share = tpot * base_exp / total
    result = []
    for q in range(LAYERS_PER_BLOCK + 2):
        depth = (first + (q - 1)).astype(jnp.float32)
        weight = jnp.where(depth < roots, math.exp(-(q - 1) / 4.0) * share, 0.0)
        result.append(weight / (1.0 + head[q] * head[q] * (1.0 / 2.25)))
    return result


def inner_lane(k):
    return k // 9 * 18 + k % 9


class Where:
    def __init__(self, count_role, count_gx, count_gz):
        me_role, me_gx, me_gz = place("role"), place("gx"), place("gz")
        f32 = jnp.float32
        self.layers = LAYERS_PER_BLOCK * count_gz
        self.first = me_gz * LAYERS_PER_BLOCK
        self.z_top = jnp.where(me_gz == 0, 0.0, 1.0).astype(f32)
        self.z_bottom = jnp.where(me_gz == count_gz - 1, 0.0, 1.0).astype(f32)
        self.x_first = jnp.where(me_gx == 0, 0.0, 1.0).astype(f32)
        self.x_last = jnp.where(me_gx == count_gx - 1, 0.0, 1.0).astype(f32)
        self.y_first = jnp.where(me_role == 0, 0.0, 1.0).astype(f32)
        self.y_last = jnp.where(me_role == count_role - 1, 0.0, 1.0).astype(f32)
        self.exp_first = jnp.exp(jnp.zeros((8, COLS), f32) - me_gz.astype(f32))


def widened(value):
    return jnp.concatenate([value] + [value[ROWS:WIDE]] * ((COLS - WIDE) // EDGE), axis=0)


def main_region(count_role, count_gx, count_gz, own, ext, edge, *refs):
    land_in, refs = refs[:5], refs[5:]
    out, inner, land_out, ha, hb, kc, mm, th, wd, sk = refs[:10]
    heat_finish = heat(count_gx, count_gz, *land_in, land_out, *refs[10:])
    spot = Where(count_role, count_gx, count_gz)
    z_top, z_bottom = spot.z_top, spot.z_bottom

    def wide(p):
        rows = own[OWN_AT[p]] if p in OWN_AT else ext[EXT_AT[p]]
        return jnp.concatenate([rows, edge[p]], axis=0)

    def wide_own(k, level):
        return jnp.concatenate([own[k * LEVELS + level], edge[OWN[k] + level]], axis=0)

    def inputs(j):
        if isinstance(j, int):
            return [wide(A0 + j), wide(N0 + j), wide(S0 + j)] + ([wide(P0 + j - 1)] if 0 < j < NC - 1 else [])
        return [wide_own(k, j - (HALO - 1)) for k in (1, 2, 3, 4)]

    def put(ref, i, value):
        ref[i, 8 : 8 + WIDE] = value
        ref[i, 0:8] = value[ROWS:WIDE]
        ref[i, 8 + WIDE : 16 + WIDE] = value[0:8]

    row = lax.broadcasted_iota(jnp.int32, (8, COLS), 0)
    x_low = jnp.where(row == 0, spot.x_first, 1.0)
    x_high = jnp.where(row == 7, spot.x_last, 1.0)

    def fill(level, carry):
        put(ha, HALO + level, wide_own(0, level))
        return carry

    lax.fori_loop(0, LEVELS, fill, 0, unroll=4)
    for i in range(HALO):
        put(ha, i, wide(H0 + i))
        put(ha, HALO + LEVELS + i, wide(H0 + HALO + LEVELS + i))
    put(kc, 0, wide(K_LO))
    put(kc, NH - 1, wide(K_HI))

    def mean4(ref, i):
        return (ref[i, 8 : 8 + WIDE] + ref[i + 1, 8 : 8 + WIDE] + ref[i + 2, 8 : 8 + WIDE] + ref[i + 3, 8 : 8 + WIDE]) * 0.25

    heads = [wide(M_LO)] + [mean4(ha, HALO + 4 * q) for q in range(LAYERS_PER_BLOCK)] + [wide(M_HI)]
    base = jnp.concatenate([spot.exp_first] * (WIDE // 8), axis=0)
    for q, value in enumerate(uptake_of(wide(TP), wide(RT), heads, spot.layers, base, spot.first)):
        sk[q] = value

    def first_curves(j):
        i = j + 1
        alpha2, half_n, half_ks, *poros = inputs(j)
        expo = expo_of(half_n)
        mm[j] = expo
        satur, cond = curves(ha[i, 8 : 8 + WIDE], alpha2, half_n, half_ks, expo)
        put(kc, i, cond)
        if poros:
            th[j - 1] = poros[0] * satur

    def later_curves(src, j):
        i = j + 1
        alpha2, half_n, half_ks, *poros = inputs(j)
        satur, cond = curves(src[i, 8 : 8 + WIDE], alpha2, half_n, half_ks, mm[j])
        put(kc, i, cond)
        if poros:
            wd[j - 1] = poros[0] * satur - th[j - 1] + sk[(i + 1) // LEVELS_PER_LAYER]

    def curves_of(body, extra):
        for j in range(HALO - 1 - extra, HALO - 1):
            body(j)
        loop(HALO - 1, HALO - 1 + LEVELS, body, 4)
        for j in range(HALO - 1 + LEVELS, HALO - 1 + LEVELS + extra):
            body(j)

    def stencil(src, i0, count, sweep, store):
        here = pl.ds(8, WIDE)
        conds = [kc[i0 + g - 1, here, :] for g in range(count + 2)]
        heads = [src[i0 + g - 1, here, :] for g in range(count + 2)]
        faces = [conds[g] + conds[g + 1] for g in range(count + 1)]
        faces[0] = faces[0] * jnp.where(i0 == HALO, z_top, jnp.where(i0 == HALO + LEVELS, z_bottom, 1.0))
        end = i0 + count
        faces[count] = faces[count] * jnp.where(
            end == HALO, z_top, jnp.where(end == HALO + LEVELS, z_bottom, 1.0)
        )
        for g in range(count):
            i = i0 + g
            head, cond = heads[g + 1], conds[g + 1]
            kf_up, kf_down = faces[g], faces[g + 1]
            kf_xm = cond + kc[i, pl.ds(7, WIDE), :]
            kf_xm = jnp.concatenate([kf_xm[0:8] * x_low, kf_xm[8:]], axis=0)
            kf_xp = cond + kc[i, pl.ds(9, WIDE), :]
            kf_xp = jnp.concatenate([kf_xp[: ROWS - 8], kf_xp[ROWS - 8 : ROWS] * x_high, kf_xp[ROWS:]], axis=0)
            kf_ym = cond + pltpu.roll(cond, 1, 1)
            kf_yp = cond + pltpu.roll(cond, COLS - 1, 1)
            inflow = kf_up * (heads[g] + 1.0) + kf_down * (heads[g + 2] - 1.0)
            inflow = inflow + (kf_xm * src[i, pl.ds(7, WIDE), :] + kf_xp * src[i, pl.ds(9, WIDE), :])
            inflow = inflow + (kf_ym * pltpu.roll(head, 1, 1) + kf_yp * pltpu.roll(head, COLS - 1, 1))
            lost = wd[i - 2] if sweep > 0 else sk[(i + 1) // LEVELS_PER_LAYER]
            diag = (1.0 + kf_up) + (kf_down + kf_xm) + (kf_xp + kf_ym) + kf_yp
            store(i, relax(head, inflow - lost, diag, sweep))

    def loop(lo, hi, body, unroll=1):
        def step(i, carry):
            body(i)
            return carry

        lax.fori_loop(lo, hi, step, 0, unroll=unroll)

    def levels_of(src, sweep, store):
        extra = SWEEPS - 1 - sweep
        if extra:
            stencil(src, HALO - extra, extra, sweep, store)
        loop(0, LEVELS // 4, lambda k: stencil(src, HALO + 4 * k, 4, sweep, store))
        if extra:
            stencil(src, HALO + LEVELS, extra, sweep, store)

    curves_of(first_curves, 2)
    levels_of(ha, 0, lambda i, value: put(hb, i, value))

    lane_wide = lax.broadcasted_iota(jnp.int32, (WIDE, COLS), 1)
    acc = jnp.zeros((WIDE, COLS), jnp.float32)
    for k in range(NC):
        lane = inner_lane(k)
        pick = (lane_wide == lane) | (lane_wide == lane + 9)
        acc = jnp.where(pick, pltpu.roll(hb[k + 1, 8 : 8 + WIDE], (lane - (COLS - 1 - NEAR)) % COLS, 1), acc)
    inner[...] = widened(acc).T

    curves_of(lambda j: later_curves(hb, j), 2)
    levels_of(hb, 1, lambda i, value: put(ha, i, value))
    curves_of(lambda j: later_curves(ha, j), 1)

    def keep(i, value):
        out[i - HALO] = value[0:ROWS]

    levels_of(ha, 2, keep)
    heat_finish()


def edge_strips(count_role, count_gx, count_gz, main, inner, strips_in, y_e, y_o, out,
                strips, sa, sb, sc, ks, sm, sth, swd, ssk, turn, done, sem):
    spot = Where(count_role, count_gx, count_gz)
    z_top, z_bottom = spot.z_top, spot.z_bottom
    f32 = jnp.float32
    strips[...] = strips_in[...]

    def take(high, low):
        for p in range(PLANES):
            strips[pl.ds(p * SIDE, HALO), :] = high[pl.ds(p * HALO, HALO), :]
            strips[pl.ds(p * SIDE + SIDE - HALO, HALO), :] = low[pl.ds(p * HALO, HALO), :]

    by_parity("role", take, y_e, y_o)

    def strip(p, count=1):
        return strips[p * SIDE : (p + count) * SIDE, :]

    heads = [strip(M_LO)]
    for q in range(LAYERS_PER_BLOCK):
        at = H0 + HALO + 4 * q
        heads.append((strip(at) + strip(at + 1) + strip(at + 2) + strip(at + 3)) * 0.25)
    heads.append(strip(M_HI))
    base = jnp.concatenate([spot.exp_first] * 2, axis=0)
    for q, value in enumerate(uptake_of(strip(TP), strip(RT), heads, spot.layers, base, spot.first)):
        ssk[q * SIDE : (q + 1) * SIDE, :] = value

    lane = lax.broadcasted_iota(jnp.int32, (SIDE, COLS), 1)
    srow = lax.broadcasted_iota(jnp.int32, (SIDE, COLS), 0)
    s_xm = jnp.where(lane == 0, spot.x_first, 1.0)
    s_xp = jnp.where(lane == ROWS - 1, spot.x_last, 1.0)
    side_mask = jnp.where(srow < 8, spot.y_last, spot.y_first)
    s_ym = jnp.where(srow % 8 == 0, side_mask, 1.0)
    s_yp = jnp.where(srow % 8 == 7, side_mask, 1.0)

    def tiled(mask, count):
        return jnp.concatenate([mask] * count, axis=0)

    def y_shift(value, by):
        parts = value.reshape(value.shape[0] // 8, 8, COLS)
        return pltpu.roll(parts, by, 1).reshape(value.shape)

    def rows_of(i, count):
        return slice(i * SIDE, (i + count) * SIDE)

    def strip_curves(src, lo, hi, sweep):
        i = lo
        while i < hi:
            count = min(5, hi - i)
            j = i - 1
            here = rows_of(i, count)
            half_n = strip(N0 + j, count)
            if sweep == 0:
                expo = expo_of(half_n)
                sm[rows_of(j, count), :] = expo
            else:
                expo = sm[rows_of(j, count), :]
            satur, cond = curves(src[here, :], strip(A0 + j, count), half_n, strip(S0 + j, count), expo)
            ks[here, :] = cond
            start, stop = max(i, 2), min(i + count, NH - 2)
            if stop > start:
                part = satur[(start - i) * SIDE : (stop - i) * SIDE]
                water = strip(P0 + start - 2, stop - start) * part
                at = rows_of(start - 2, stop - start)
                if sweep == 0:
                    sth[at, :] = water
                else:
                    swd[at, :] = water - sth[at, :]
            i += count

    def strip_stencil(src, dst, lo, hi, sweep):
        i = lo
        while i < hi:
            count = min(5, hi - i)
            here = rows_of(i, count)
            above, below = rows_of(i - 1, count), rows_of(i + 1, count)
            head, cond = src[here, :], ks[here, :]
            kf_up = cond + ks[above, :]
            kf_down = cond + ks[below, :]
            if i <= HALO < i + count:
                level = lax.broadcasted_iota(jnp.int32, kf_up.shape, 0) // SIDE
                kf_up = jnp.where(level == HALO - i, kf_up * z_top, kf_up)
            if i <= HALO + LEVELS - 1 < i + count:
                level = lax.broadcasted_iota(jnp.int32, kf_up.shape, 0) // SIDE
                kf_down = jnp.where(level == HALO + LEVELS - 1 - i, kf_down * z_bottom, kf_down)
            kf_xm = (cond + pltpu.roll(cond, 1, 1)) * tiled(s_xm, count)
            kf_xp = (cond + pltpu.roll(cond, COLS - 1, 1)) * tiled(s_xp, count)
            kf_ym = (cond + y_shift(cond, 1)) * tiled(s_ym, count)
            kf_yp = (cond + y_shift(cond, 7)) * tiled(s_yp, count)
            inflow = kf_up * (src[above, :] + 1.0) + kf_down * (src[below, :] - 1.0)
            inflow = inflow + (kf_xm * pltpu.roll(head, 1, 1) + kf_xp * pltpu.roll(head, COLS - 1, 1))
            inflow = inflow + (kf_ym * y_shift(head, 1) + kf_yp * y_shift(head, 7))
            lost = jnp.concatenate([ssk[rows_of((k + 1) // LEVELS_PER_LAYER, 1), :] for k in range(i, i + count)], axis=0)
            if sweep > 0:
                lost = lost + swd[rows_of(i - 2, count), :]
            diag = (1.0 + kf_up) + (kf_down + kf_xm) + (kf_xp + kf_ym) + kf_yp
            dst[here, :] = relax(head, inflow - lost, diag, sweep)
            i += count

    ks[rows_of(0, 1), :] = strip(K_LO)
    ks[rows_of(NH - 1, 1), :] = strip(K_HI)
    strip_curves(strips, 1, NH - 1, 0)
    strip_stencil(strips, sa, 1, NH - 1, 0)
    for k in range(NC):
        lane = inner_lane(k)
        sa[pl.ds((k + 1) * SIDE + 3, 1), :] = inner[pl.ds(lane, 1), :]
        sa[pl.ds((k + 1) * SIDE + 8 + NEAR, 1), :] = inner[pl.ds(lane + 9, 1), :]
    strip_curves(sa, 1, NH - 1, 1)
    strip_stencil(sa, sb, 2, NH - 2, 1)
    strip_curves(sb, 2, NH - 2, 2)
    strip_stencil(sb, sc, 3, NH - 3, 2)

    pieces = [sc[i * SIDE + 8 - HALO : i * SIDE + 8 + HALO, :] for i in range(HALO, HALO + LEVELS)]
    pieces.append(jnp.zeros((COLS - 2 * HALO * LEVELS, COLS), f32))
    turn[...] = jnp.concatenate(pieces, axis=0).T[0:ROWS]
    lane_rows = lax.broadcasted_iota(jnp.int32, (ROWS, COLS), 1)
    outer = (lane_rows < HALO) | (lane_rows >= COLS - HALO)
    copies = []
    for level in range(LEVELS):
        moved = pltpu.roll(turn[...], (COLS - HALO - 2 * HALO * level) % COLS, 1)
        done[level] = jnp.where(outer, moved, main[level])
        copy = pltpu.make_async_copy(done.at[level], out.at[level], sem.at[level])
        copy.start()
        copies.append(copy)
    for copy in copies:
        copy.wait()


def heat(count_gx, count_gz, y, temp_in, tr_in, air_in, rt_in, out, sat, head, temp, tr, air, rt, sem):
    copies = []
    for src, dst in ((temp_in, temp), (tr_in, tr), (air_in, air), (rt_in, rt)):
        copy = pltpu.make_async_copy(src, dst, sem.at[len(copies)])
        copy.start()
        copies.append(copy)
    def finish():
        me = place("gx") * count_gz + place("gz")
        layers = LAYERS_PER_BLOCK * count_gz
        for copy in copies:
            copy.wait()
        for gx in range(count_gx):
            for gz in range(count_gz):
                j = me ^ (gx * count_gz + gz)
                for c in range(CAP):
                    tile = y[j, c * 8 : c * 8 + 8]
                    at = pl.ds(gz * LAYERS_PER_BLOCK, LAYERS_PER_BLOCK)
                    sat[gx * CAP + c, at, :] = tile[0:LAYERS_PER_BLOCK]
                    head[gx * CAP + c, at, :] = tile[LAYERS_PER_BLOCK : 2 * LAYERS_PER_BLOCK]
        layer = lax.broadcasted_iota(jnp.int32, (layers, COLS), 0)
        decay = jnp.exp(layer.astype(jnp.float32) * -0.25)
        for slot in range(count_gx * CAP):
            roots = jnp.broadcast_to(rt[slot], (layers, COLS))
            weight = jnp.where(layer < roots, decay, 0.0)
            weight = weight / jnp.sum(weight, axis=0, keepdims=True)
            stress = 1.0 / (1.0 + head[slot] * head[slot] * (1.0 / 2.25))
            uptake = tr[slot] * weight * stress
            kappa = 0.25 + 0.9 * sat[slot]
            top = jnp.broadcast_to(air[slot], (layers, COLS))
            k_above = jnp.where(layer == 0, kappa, 0.5 * (kappa + pltpu.roll(kappa, 1, 0)))
            k_below = jnp.where(layer == layers - 1, 0.0, 0.5 * (kappa + pltpu.roll(kappa, layers - 1, 0)))
            old = temp[slot]
            new = old
            for _ in range(HEAT_STEPS):
                above = jnp.where(layer == 0, top, pltpu.roll(new, 1, 0))
                below = pltpu.roll(new, layers - 1, 0)
                new = new + 0.2 * (k_above * (above - new) + k_below * (below - new)) - 0.3 * uptake
            out[slot] = jnp.where(sat[slot] >= 0.0, new, old)

    return finish


def call(body, outs, ins, scratch=(), aliases=None, limit=16 * MIB, kept=True, work=0):
    return pl.pallas_call(
        body,
        out_shape=[pltpu.VMEM(shape, jnp.float32) if kept else jax.ShapeDtypeStruct(shape, jnp.float32) for shape in outs],
        in_specs=ins,
        out_specs=[VMEM] * len(outs),
        scratch_shapes=list(scratch),
        input_output_aliases=aliases or {},
        compiler_params=pltpu.CompilerParams(vmem_limit_bytes=limit),
        cost_estimate=pl.CostEstimate(flops=work, bytes_accessed=work, transcendentals=0) if work else None,
    )


def main_call(count_role, count_gx, count_gz):
    f32 = jnp.float32
    deep = WIDE + 16
    slots = count_gx * CAP
    land_shape = (slots, LAYERS_PER_BLOCK * count_gz, COLS)
    return pl.pallas_call(
        functools.partial(main_region, count_role, count_gx, count_gz),
        out_shape=[
            pltpu.VMEM((LEVELS, ROWS, COLS), f32),
            pltpu.VMEM((COLS, COLS), f32),
            jax.ShapeDtypeStruct(land_shape, f32),
        ],
        in_specs=[VMEM] * 4 + [HBM] * 4,
        out_specs=[VMEM] * 3,
        scratch_shapes=[
            pltpu.VMEM((NH, deep, COLS), f32),
            pltpu.VMEM((NH, deep, COLS), f32),
            pltpu.VMEM((NH, deep, COLS), f32),
            pltpu.VMEM((NC, WIDE, COLS), f32),
            pltpu.VMEM((NP, WIDE, COLS), f32),
            pltpu.VMEM((NP, WIDE, COLS), f32),
            pltpu.VMEM((LAYERS_PER_BLOCK + 2, WIDE, COLS), f32),
            pltpu.VMEM(land_shape, f32),
            pltpu.VMEM(land_shape, f32),
            pltpu.VMEM(land_shape, f32),
            pltpu.VMEM((slots, 1, COLS), f32),
            pltpu.VMEM((slots, 1, COLS), f32),
            pltpu.VMEM((slots, 1, COLS), jnp.int32),
            pltpu.SemaphoreType.DMA((4,)),
        ],
        compiler_params=pltpu.CompilerParams(vmem_limit_bytes=16 * MIB),
    )


def strip_call(count_role, count_gx, count_gz):
    f32 = jnp.float32
    return pl.pallas_call(
        functools.partial(edge_strips, count_role, count_gx, count_gz),
        out_shape=jax.ShapeDtypeStruct((LEVELS, ROWS, COLS), f32),
        in_specs=[VMEM] * 5,
        out_specs=HBM,
        scratch_shapes=[
            pltpu.VMEM((PACKS * COLS, COLS), f32),
            pltpu.VMEM((NH * SIDE, COLS), f32),
            pltpu.VMEM((NH * SIDE, COLS), f32),
            pltpu.VMEM((NH * SIDE, COLS), f32),
            pltpu.VMEM((NH * SIDE, COLS), f32),
            pltpu.VMEM((NC * SIDE, COLS), f32),
            pltpu.VMEM((NP * SIDE, COLS), f32),
            pltpu.VMEM((NP * SIDE, COLS), f32),
            pltpu.VMEM(((LAYERS_PER_BLOCK + 2) * SIDE, COLS), f32),
            pltpu.VMEM((ROWS, COLS), f32),
            pltpu.VMEM((LEVELS, ROWS, COLS), f32),
            pltpu.SemaphoreType.DMA((LEVELS,)),
        ],
        compiler_params=pltpu.CompilerParams(vmem_limit_bytes=16 * MIB),
    )


def local(h, a, n, s, p, tile_owner, land_temp, tr, air, rt):
    sizes = tuple(lax.axis_size(axis) for axis in AXES)
    count_role, count_gx, count_gz = sizes
    groups = count_gx * count_gz
    slots = count_gx * CAP
    f32 = jnp.float32

    def swap(value, axis, odd):
        return lax.ppermute(value, AXES, pairing(sizes, axis, odd))

    owners = tile_owner.T
    land = (land_temp[0, 0], tr[0, 0, :, None], air[0, 0, :, None], rt[0, 0, :, None])
    h, a, n, s, p = (pltpu.with_memory_space_constraint(x, pltpu.HBM) for x in (h, a, n, s, p))
    land_temp, tr, air, rt = (pltpu.with_memory_space_constraint(x, pltpu.HBM) for x in land)

    z_send_e, z_send_o = call(
        z_faces,
        [(Z_SEND, ROWS, COLS)] * 2,
        [HBM] * 5,
        [
            pltpu.VMEM((2, 4, ROWS, COLS), f32),
            pltpu.VMEM((2, 3, ROWS, COLS), f32),
            pltpu.VMEM((2, 3, ROWS, COLS), f32),
            pltpu.VMEM((2, 3, ROWS, COLS), f32),
            pltpu.VMEM((2, 1, ROWS, COLS), f32),
            pltpu.SemaphoreType.DMA((10,)),
        ],
    )(h, a, n, s, p)
    z_e = swap(z_send_e, "gz", False)
    z_o = swap(z_send_o, "gz", True) if count_gz > 2 else z_e

    half = groups // 2
    blocks = count_gx // 2
    packed = half * 8 * CAP + blocks * 8
    x_count = 1 if count_gx == 2 else 2
    x_shape = (PLANES, 4, COLS)
    own_shapes = [(len(OWN_AT), 16, COLS), (PACKS, ROWS, COLS)]

    def land_stage():
        send, keep, hot = call(
            functools.partial(land_pack, count_gx, count_gz),
            [(packed, COLS), (packed, COLS), (ROWS, groups * 8)],
            [SMEM] + [HBM] * 5,
            [
                pltpu.VMEM((2 * LAYERS_PER_BLOCK, ROWS, COLS), f32),
                pltpu.SMEM((groups,), jnp.int32),
                pltpu.SMEM((groups * CAP,), jnp.int32),
                pltpu.VMEM((LEVELS, ROWS, COLS), f32),
                pltpu.VMEM((LEVELS, ROWS, COLS), f32),
                pltpu.VMEM((LEVELS, ROWS, COLS), f32),
                pltpu.VMEM((slots, 1, COLS), f32),
                pltpu.VMEM((slots, 1, COLS), jnp.int32),
                pltpu.SemaphoreType.DMA((3 * LAYERS_PER_BLOCK + 2,)),
            ],
        )(owners, h, a, n, tr, rt)

        got = lax.ppermute(send, AXES, xor_pairs(sizes, "gx", blocks))
        bit = blocks // 2
        if bit:
            pieces = [part[j * PIECE : (j + 1) * PIECE] for part in (keep, got) for j in range(half)]
            base = half * PIECE
            values = [part[base + j * 8 : base + (j + 1) * 8] for part in (keep, got) for j in range(blocks)]
            while bit:
                moving = [j for j in range(groups) if (j // count_gz) & bit]
                t_moving = [j for j in range(count_gx) if j & bit]
                sent = jnp.concatenate([pieces[j] for j in moving] + [values[j] for j in t_moving], axis=0)
                got = lax.ppermute(sent, AXES, xor_pairs(sizes, "gx", bit))
                for k, j in enumerate(moving):
                    pieces[j] = got[k * PIECE : (k + 1) * PIECE]
                for k, j in enumerate(t_moving):
                    base = len(moving) * PIECE + k * 8
                    values[j] = got[base : base + 8]
                bit //= 2
            keep = jnp.concatenate(pieces[:half] + values[:blocks], axis=0)
            got = jnp.concatenate(pieces[half:] + values[blocks:], axis=0)
        rim, pack = call(
            own_part,
            own_shapes,
            [HBM] * 5,
            [pltpu.VMEM((len(OWN_AT), ROWS, COLS), f32), pltpu.SemaphoreType.DMA((5,))],
        )(h, a, n, s, p)
        parts = call(
            functools.partial(land_sort, count_gx, count_gz),
            [(count_gx * (PIECE + 8), COLS)] * count_gz,
            [VMEM] * 2,
        )(keep, got)
        parts = [parts[0]] + [
            lax.ppermute(parts[dist], AXES, xor_pairs(sizes, "gz", dist)) for dist in range(1, count_gz)
        ]
        tile, y = call(
            functools.partial(tile_values, count_gx, count_gz),
            [(2, ROWS, COLS), (groups, PIECE, COLS)],
            [VMEM] * (1 + count_gz),
        )(hot, *parts)
        return [rim, pack, tile, y]

    def no_land_stage():
        shapes = own_shapes + [(2, ROWS, COLS), (groups, PIECE, COLS)]
        return [jnp.zeros(shape, f32) for shape in shapes]

    ahead = lax.optimization_barrier(jnp.bool_(True))
    rim, pack, tile, y = lax.cond(ahead, land_stage, no_land_stage)

    ext, *x_sends = call(
        functools.partial(x_faces, count_gx),
        [(len(EXT_AT), ROWS, COLS)] + [x_shape] * x_count,
        [VMEM] * 4,
    )(rim, z_e, z_o, tile)
    (own,) = call(
        own_planes,
        [(len(OWN_AT), ROWS, COLS)],
        [HBM] * 5,
        [pltpu.SemaphoreType.DMA((5,))],
    )(h, a, n, s, p)
    x_got = [swap(value, "gx", bool(k)) for k, value in enumerate(x_sends)]

    edge, strips, y_send_e, y_send_o = call(
        functools.partial(y_faces, count_gx),
        [(PLANES, EDGE, COLS), (PACKS * COLS, COLS), (Y_SEND, COLS), (Y_SEND, COLS)],
        [VMEM] * 3 + [ANY] + [VMEM] * x_count,
    )(rim, pack, ext, own, *x_got)
    y_e = swap(y_send_e, "role", False)
    y_o = swap(y_send_o, "role", True) if count_role > 2 else y_e

    main, inner, land_new = main_call(*sizes)(own, ext, edge, y, land_temp, tr, air, rt)
    head = strip_call(*sizes)(main, inner, strips, y_e, y_o)
    return (head, land_new[None, None])


def solution(mesh):
    in_specs = (
        P("gz", "gx", "role"),
        P("gz", "gx", "role"),
        P("gz", "gx", "role"),
        P("gz", "gx", "role"),
        P("gz", "gx", "role"),
        P(),
        P("role", ("gx", "gz"), None, None, None),
        P("role", ("gx", "gz"), None, None),
        P("role", ("gx", "gz"), None, None),
        P("role", ("gx", "gz"), None, None),
    )
    out_specs = (P("gz", "gx", "role"), P("role", ("gx", "gz"), None, None, None))
    return jax.shard_map(local, mesh=mesh, in_specs=in_specs, out_specs=out_specs, check_vma=False)
```

```python
import functools
import math

import jax
import jax.numpy as jnp
from jax import lax
from jax.experimental import pallas as pl
from jax.experimental.pallas import tpu as pltpu
from jax.sharding import PartitionSpec as P

LAYERS_PER_BLOCK = 4
LEVELS_PER_LAYER = 4
CAP = 3
SWEEPS = 3
HEAT_STEPS = 4
HALO = SWEEPS
AXES = ("role", "gx", "gz")
VMEM = pl.BlockSpec(memory_space=pltpu.VMEM)
SMEM = pl.BlockSpec(memory_space=pltpu.SMEM)
HBM = pl.BlockSpec(memory_space=pltpu.HBM)
ANY = pl.BlockSpec(memory_space=pl.ANY)
MIB = 1024 * 1024

LEVELS = 16
ROWS = 64
COLS = 128
EDGE = 8
WIDE = ROWS + EDGE
H0 = 0
NH = LEVELS + 2 * HALO
A0 = H0 + NH
NC = LEVELS + 2 * HALO - 2
N0 = A0 + NC
S0 = N0 + NC
K_LO = S0 + NC
K_HI = K_LO + 1
P0 = K_HI + 1
NP = LEVELS + 2 * HALO - 4
M_LO = P0 + NP
M_HI = M_LO + 1
TP = M_HI + 1
RT = TP + 1
PLANES = RT + 1
PACKS = (PLANES + 7) // 8
SIDE = 16
NEAR = 4
Z_SEND = 12
PIECE = 8 * CAP


def columns_sent(p):
    for first, count, reach in ((H0, NH, HALO), (A0, NC, HALO), (N0, NC, HALO), (S0, NC, HALO), (P0, NP, 1)):
        if first <= p < first + count:
            out = (count - LEVELS) // 2
            level = p - first - out
            away = max(0, -level, level - LEVELS + 1)
            return max(0, reach - away)
    return {M_LO: 1, M_HI: 1, TP: 2, RT: 2}.get(p, 0)


Y_ROWS = 256
Y_EXTRA = Y_ROWS // (ROWS // EDGE)
Y_SEND = Y_ROWS // 2 + Y_EXTRA


def omega(sweep):
    return 1.0 / (1.0 + 0.6 * math.cos(math.pi * (2 * sweep + 1) / (2 * SWEEPS)))


def place(axis):
    return lax.axis_index(axis)


def is_even(axis):
    return lax.rem(place(axis), 2) == 0


def pairing(sizes, axis, odd):
    pairs = []
    which = AXES.index(axis)
    for index in range(math.prod(sizes)):
        at = [index // (sizes[1] * sizes[2]), index // sizes[2] % sizes[1], index % sizes[2]]
        count = sizes[which]
        there = list(at)
        if not odd:
            there[which] = at[which] ^ 1
        else:
            there[which] = at[which] + (1 if at[which] % 2 else -1)
            if not 0 <= there[which] < count:
                there = list(at)
                if axis == "gx":
                    there[1] = count - 1 - at[1]
                else:
                    there[1] = at[1] ^ 1
        pairs.append((index, (there[0] * sizes[1] + there[1]) * sizes[2] + there[2]))
    return pairs


def xor_pairs(sizes, axis, bit):
    pairs = []
    which = AXES.index(axis)
    for index in range(math.prod(sizes)):
        at = [index // (sizes[1] * sizes[2]), index // sizes[2] % sizes[1], index % sizes[2]]
        at[which] ^= bit
        pairs.append((index, (at[0] * sizes[1] + at[1]) * sizes[2] + at[2]))
    return pairs


LOG2E = math.log2(math.e)
HALF_LOG2E = 0.5 * LOG2E


def saturation_of(head, alpha2, half_n, expo):
    logx = half_n * jnp.log(alpha2 * (head * head + 0.01))
    softer = LOG2E * jnp.log(1.0 + jnp.exp2(logx))
    return logx, softer, jnp.exp2(-0.5 * expo * softer)


def curves(head, alpha2, half_n, half_ks, expo):
    logx, softer, root = saturation_of(head, alpha2, half_n, expo)
    gap = 1.0 - jnp.exp2(expo * (logx - softer))
    return root * root, half_ks * root * (gap * gap)


def inverse(value):
    guess = pl.reciprocal(value, approx=True)
    return guess * (2.0 - value * guess)


def expo_of(half_n):
    return 1.0 - HALF_LOG2E * inverse(half_n)


def relax(head, inflow, diag, sweep):
    step = omega(sweep)
    return (1.0 - step) * head + (step * (head + inflow)) * inverse(diag)


def z_faces(h, a, n, s, p, out_e, out_o, hb, ab, nb, sb, pb, sem):
    copies = []
    for side in range(2):
        for src, dst, count in ((h, hb, 4), (a, ab, 3), (n, nb, 3), (s, sb, 3), (p, pb, 1)):
            start = 0 if side == 0 else LEVELS - count
            copy = pltpu.make_async_copy(src.at[pl.ds(start, count)], dst.at[side], sem.at[len(copies)])
            copy.start()
            copies.append(copy)
    for copy in copies:
        copy.wait()

    def put(out, side):
        def level(buf, count, dist):
            return buf[side, dist - 1 if side == 0 else count - dist]

        for dist in (1, 2, 3):
            out[dist - 1] = level(hb, 4, dist)
        for dist in (1, 2):
            alpha = level(ab, 3, dist)
            out[2 + dist] = alpha * alpha
            out[4 + dist] = HALF_LOG2E * level(nb, 3, dist)
            out[6 + dist] = 0.5 * level(sb, 3, dist)
        out[9] = level(pb, 1, 1)
        alpha = level(ab, 3, 3)
        half_n = HALF_LOG2E * level(nb, 3, 3)
        out[10] = curves(level(hb, 4, 3), alpha * alpha, half_n, 0.5 * level(sb, 3, 3), expo_of(half_n))[1]
        out[11] = (hb[side, 0] + hb[side, 1] + hb[side, 2] + hb[side, 3]) * 0.25

    even = is_even("gz")

    @pl.when(even)
    def _():
        put(out_e, 1)
        put(out_o, 0)

    @pl.when(jnp.logical_not(even))
    def _():
        put(out_e, 0)
        put(out_o, 1)


def land_pack(count_gx, count_gz, owners, h_in, a_in, n_in, tr_in, rt_in, send, keep, hot,
              means, counts, slots, h, a, n, tr, rt, sem):
    groups = count_gx * count_gz
    me_role, me_gx = place("role"), place("gx")
    me = me_gx * count_gz + place("gz")
    copies = []
    for layer in range(LAYERS_PER_BLOCK):
        some = pl.ds(layer * LEVELS_PER_LAYER, LEVELS_PER_LAYER)
        for src, dst in ((h_in, h), (a_in, a), (n_in, n)):
            copies.append(pltpu.make_async_copy(src.at[some], dst.at[some], sem.at[len(copies)]))
    for src, dst in ((tr_in, tr), (rt_in, rt)):
        copies.append(pltpu.make_async_copy(src, dst, sem.at[len(copies)]))
    for copy in copies:
        copy.start()

    def clear_slot(i, carry):
        slots[i] = -1
        return carry

    def clear_count(i, carry):
        counts[i] = 0
        return carry

    lax.fori_loop(0, groups * CAP, clear_slot, 0)
    lax.fori_loop(0, groups, clear_count, 0)
    lane = lax.broadcasted_iota(jnp.int32, (1, groups * 8), 1)

    def step(x, carry):
        owner = owners[me_role, me_gx * ROWS + x]
        safe = jnp.maximum(owner, 0)
        rank = counts[safe]
        at = jnp.where(owner >= 0, (me ^ owner) * 8 + 2 * rank, -1)
        hot[pl.ds(x, 1), :] = jnp.where(lane == at, 1.0, 0.0)

        @pl.when(owner >= 0)
        def _():
            counts[owner] = rank + 1
            slots[owner * CAP + rank] = x

        return carry

    lax.fori_loop(0, ROWS, step, 0)
    for layer in range(LAYERS_PER_BLOCK):
        for copy in copies[3 * layer : 3 * layer + 3]:
            copy.wait()
        saturs = []
        heads = []
        for level in range(layer * LEVELS_PER_LAYER, (layer + 1) * LEVELS_PER_LAYER):
            head = h[level]
            alpha = a[level]
            half_n = HALF_LOG2E * n[level]
            root = saturation_of(head, alpha * alpha, half_n, expo_of(half_n))[2]
            saturs.append(root * root)
            heads.append(head)
        means[layer] = (saturs[0] + saturs[1] + saturs[2] + saturs[3]) * 0.25
        means[LAYERS_PER_BLOCK + layer] = (heads[0] + heads[1] + heads[2] + heads[3]) * 0.25
    for copy in copies[3 * LAYERS_PER_BLOCK :]:
        copy.wait()
    half = groups // 2
    for j in range(groups):
        out, k = (keep, j) if j < half else (send, j - half)
        for c in range(CAP):
            row = slots[(me ^ j) * CAP + c]
            safe = jnp.maximum(row, 0)
            for q in range(8):
                value = means[q, pl.ds(safe, 1), :]
                out[pl.ds(k * PIECE + c * 8 + q, 1), :] = jnp.where(row >= 0, value, -1.0)
    blocks = count_gx // 2
    for j in range(count_gx):
        block = me_gx ^ j
        out, k = (keep, j) if j < blocks else (send, j - blocks)
        base = half * PIECE + k * 8
        out[pl.ds(base, 8), :] = jnp.zeros((8, COLS), jnp.float32)
        for c in range(CAP):
            out[pl.ds(base + 2 * c, 1), :] = tr[block * CAP + c]
            out[pl.ds(base + 2 * c + 1, 1), :] = rt[block * CAP + c].astype(jnp.float32)


def land_sort(count_gx, count_gz, keep, got, *outs):
    half, blocks = count_gx * count_gz // 2, count_gx // 2
    for gx in range(count_gx):
        src, k = (keep, gx) if gx < blocks else (got, gx - blocks)
        for dist in range(count_gz):
            at = (k * count_gz + dist) * PIECE
            outs[dist][gx * PIECE : (gx + 1) * PIECE] = src[at : at + PIECE]
            base = count_gx * PIECE + gx * 8
            outs[dist][base : base + 8] = src[half * PIECE + k * 8 : half * PIECE + k * 8 + 8]


def tile_values(count_gx, count_gz, hot, *refs):
    parts, out, y = refs[:count_gz], refs[count_gz], refs[count_gz + 1]
    values = []
    for gx in range(count_gx):
        for dist in range(count_gz):
            base = count_gx * PIECE + gx * 8
            values.append(parts[dist][base : base + 8])
            y[gx * count_gz + dist] = parts[dist][gx * PIECE : (gx + 1) * PIECE]
    t = jnp.concatenate(values, axis=0)
    out[0] = exact_dot(hot[...], t)
    out[1] = jnp.maximum(exact_dot(hot[...], pltpu.roll(t, t.shape[0] - 1, 0)), 1.0)


def exact_dot(hot, values):
    total = None
    rest = values
    left = hot.astype(jnp.bfloat16)
    for _ in range(3):
        part = rest.astype(jnp.bfloat16)
        rest = rest - part.astype(jnp.float32)
        term = jnp.dot(left, part, preferred_element_type=jnp.float32)
        total = term if total is None else total + term
    return total


def z_places(low):
    places = [H0 + (HALO - dist if low else HALO + LEVELS - 1 + dist) for dist in (1, 2, 3)]
    for first in (A0, N0, S0):
        places += [first + (HALO - 1 - dist if low else HALO - 2 + LEVELS + dist) for dist in (1, 2)]
    return places + [P0 + (0 if low else NP - 1), K_LO if low else K_HI, M_LO if low else M_HI]


def by_parity(axis, action, first, second):
    even = is_even(axis)

    @pl.when(even)
    def _():
        action(first, second)

    @pl.when(jnp.logical_not(even))
    def _():
        action(second, first)


OWN = (H0 + HALO, A0 + HALO - 1, N0 + HALO - 1, S0 + HALO - 1, P0 + HALO - 2)


def scaled(k, value):
    return (value, value * value, HALF_LOG2E * value, 0.5 * value, value)[k]


def packed_tile(tile, rows_of, count):
    lane_group = lax.broadcasted_iota(jnp.int32, (count, COLS), 1) // SIDE
    acc = jnp.zeros((count, COLS), jnp.float32)
    for j in range(8):
        p = tile * 8 + j
        value = rows_of(p) if p < PLANES else None
        if value is not None:
            acc = jnp.where(lane_group == j, pltpu.roll(value, SIDE * j + 8, 1), acc)
    return acc


OWN_AT = {first + level: k * LEVELS + level for k, first in enumerate(OWN) for level in range(LEVELS)}
EXT_AT = {p: k for k, p in enumerate(p for p in range(PLANES) if p not in OWN_AT)}


def own_planes(*refs):
    arrays, own, sem = refs[:5], refs[5], refs[6]
    copies = []
    for k, src in enumerate(arrays):
        copy = pltpu.make_async_copy(src, own.at[pl.ds(k * LEVELS, LEVELS)], sem.at[k])
        copy.start()
        copies.append(copy)
    for k, copy in enumerate(copies):
        copy.wait()
        if 0 < k < 4:
            for level in range(LEVELS):
                own[k * LEVELS + level] = scaled(k, own[k * LEVELS + level])


def own_part(*refs):
    arrays, rim, pack, own, sem = refs[:5], refs[5], refs[6], refs[7], refs[8]
    own_planes(*arrays, own, sem)
    for k in range(len(OWN_AT)):
        rim[k, 0:8] = own[k, 0:8]
        rim[k, 8:16] = own[k, ROWS - 8 : ROWS]
    for t in range(PACKS):
        pack[t] = packed_tile(t, lambda p: own[OWN_AT[p]] if p in OWN_AT else None, ROWS)


def own_curves(*refs):
    arrays, (params, ha, kc, mm, th, sem) = refs[:4], refs[4:]
    step = 4
    copies = []
    for first in range(0, LEVELS, step):
        for k, src in enumerate(arrays):
            if k == 0:
                dst = ha.at[pl.ds(HALO + first, step), pl.ds(8, ROWS), :]
            else:
                dst = params.at[pl.ds((k - 1) * LEVELS + first, step)]
            copies.append(pltpu.make_async_copy(src.at[pl.ds(first, step)], dst, sem.at[len(copies)]))
    for copy in copies:
        copy.start()
    for first in range(0, LEVELS, step):
        for copy in copies[first // step * 4 : first // step * 4 + 4]:
            copy.wait()
        for level in range(first, first + step):
            i = HALO + level
            alpha2, half_n, half_ks = (scaled(k, params[(k - 1) * LEVELS + level]) for k in (1, 2, 3))
            params[level] = alpha2
            params[LEVELS + level] = half_n
            params[2 * LEVELS + level] = half_ks
            head = ha[i, 8 : 8 + ROWS]
            expo = expo_of(half_n)
            satur, cond = curves(head, alpha2, half_n, half_ks, expo)
            kc[i, 8 : 8 + ROWS] = cond
            mm[i - 1, 0:ROWS] = expo
            th[i - 2, 0:ROWS] = satur


def x_faces(count_gx, rim, z_e, z_o, tile, ext, *sends):
    def take(upper, lower):
        for got, places in ((upper, z_places(False)), (lower, z_places(True))):
            for k, p in enumerate(places):
                ext[EXT_AT[p]] = got[k]

    by_parity("gz", take, z_e, z_o)
    ext[EXT_AT[TP]] = tile[0]
    ext[EXT_AT[RT]] = tile[1]

    def put(high, low):
        for p in range(PLANES):
            src, k, rows = (rim, OWN_AT[p], 16) if p in OWN_AT else (ext, EXT_AT[p], ROWS)
            if high is not None:
                high[p, pl.ds(0, HALO), :] = src[k, pl.ds(rows - HALO, HALO), :]
            if low is not None:
                low[p, pl.ds(0, HALO), :] = src[k, pl.ds(0, HALO), :]

    by_parity("gx", put, sends[0], sends[1] if count_gx > 2 else None)


def y_faces(count_gx, *refs):
    rim, own_pack, ext = refs[:3]
    if count_gx > 2:
        got_e, got_o = refs[4], refs[5]
    else:
        got_e, got_o = refs[4], None
    edge, strips, send_e, send_o, lines = refs[-5:]

    def take(high, low):
        for p in range(PLANES):
            edge[p] = rim[OWN_AT[p], 8:16] if p in OWN_AT else ext[EXT_AT[p], ROWS - EDGE : ROWS]
            if high is not None:
                edge[p, pl.ds(0, HALO), :] = high[p, pl.ds(0, HALO), :]
            if low is not None:
                edge[p, pl.ds(EDGE - HALO, HALO), :] = low[p, pl.ds(0, HALO), :]

    even_x = is_even("gx")

    @pl.when(even_x)
    def _():
        take(got_e, got_o)

    @pl.when(jnp.logical_not(even_x))
    def _():
        take(got_o, got_e)

    group = lax.broadcasted_iota(jnp.int32, (ROWS, COLS), 1) // SIDE
    for t in range(PACKS):
        rows = own_pack[t]
        for j in range(8):
            p = t * 8 + j
            if p in EXT_AT:
                rows = jnp.where(group == j, pltpu.roll(ext[EXT_AT[p]], SIDE * j + 8, 1), rows)
        last = packed_tile(t, lambda p: edge[p], EDGE)
        full = widened(jnp.concatenate([rows, last], axis=0))
        strips[t * COLS : (t + 1) * COLS, :] = full.T

    lane = lax.broadcasted_iota(jnp.int32, (Y_ROWS // 2, COLS), 1)

    def put(high, low):
        for send, last in ((high, True), (low, False)):
            at = 0
            for p in range(PLANES):
                count = columns_sent(p)
                if count:
                    start = p * SIDE + (8 - count if last else 8)
                    lines[pl.ds(at, count), :] = strips[pl.ds(start, count), :]
                    at += count
            lines[pl.ds(at, Y_ROWS - at), :] = jnp.zeros((Y_ROWS - at, COLS), jnp.float32)
            first, second = lines[0 : Y_ROWS // 2], lines[Y_ROWS // 2 : Y_ROWS]
            send[0 : Y_ROWS // 2] = jnp.where(lane < ROWS, first, pltpu.roll(second, ROWS, 1))
            extra = jnp.zeros((Y_EXTRA, COLS), jnp.float32)
            for g in range(Y_ROWS // Y_EXTRA):
                part = pltpu.roll(lines[g * Y_EXTRA : (g + 1) * Y_EXTRA], (EDGE * g - ROWS) % COLS, 1)
                extra = jnp.where(lane[0:Y_EXTRA] // EDGE == g, part, extra)
            send[Y_ROWS // 2 : Y_SEND] = extra

    by_parity("role", put, send_e, send_o)


def uptake_of(tpot, roots, head, layers, base_exp, first):
    total = jnp.zeros_like(tpot)
    for layer in range(layers):
        total = total + jnp.where(roots > float(layer), math.exp(-layer / 4.0), 0.0)
    share = tpot * base_exp / total
    result = []
    for q in range(LAYERS_PER_BLOCK + 2):
        depth = (first + (q - 1)).astype(jnp.float32)
        weight = jnp.where(depth < roots, math.exp(-(q - 1) / 4.0) * share, 0.0)
        result.append(weight / (1.0 + head[q] * head[q] * (1.0 / 2.25)))
    return result


def inner_lane(k):
    return k // 9 * 18 + k % 9


class Where:
    def __init__(self, count_role, count_gx, count_gz):
        me_role, me_gx, me_gz = place("role"), place("gx"), place("gz")
        f32 = jnp.float32
        self.layers = LAYERS_PER_BLOCK * count_gz
        self.first = me_gz * LAYERS_PER_BLOCK
        self.z_top = jnp.where(me_gz == 0, 0.0, 1.0).astype(f32)
        self.z_bottom = jnp.where(me_gz == count_gz - 1, 0.0, 1.0).astype(f32)
        self.x_first = jnp.where(me_gx == 0, 0.0, 1.0).astype(f32)
        self.x_last = jnp.where(me_gx == count_gx - 1, 0.0, 1.0).astype(f32)
        self.y_first = jnp.where(me_role == 0, 0.0, 1.0).astype(f32)
        self.y_last = jnp.where(me_role == count_role - 1, 0.0, 1.0).astype(f32)
        self.exp_first = jnp.exp(jnp.zeros((8, COLS), f32) - me_gz.astype(f32))


def widened(value):
    return jnp.concatenate([value] + [value[ROWS:WIDE]] * ((COLS - WIDE) // EDGE), axis=0)


def main_region(count_role, count_gx, count_gz, params, ext, edge, *refs):
    land_in, poro_in, refs = refs[:5], refs[5], refs[10:]
    out, inner, land_out, ha, kc, mm, th, hb, wd, sk, poro, poro_sem = refs[:12]
    heat_finish = heat(count_gx, count_gz, *land_in, land_out, *refs[12:])
    poro_copy = pltpu.make_async_copy(poro_in, poro, poro_sem)
    poro_copy.start()
    spot = Where(count_role, count_gx, count_gz)
    z_top, z_bottom = spot.z_top, spot.z_bottom

    def wide(p):
        return jnp.concatenate([ext[EXT_AT[p]], edge[p]], axis=0)

    def wide_own(k, level):
        rows = poro[level] if k == 4 else params[(k - 1) * LEVELS + level]
        return jnp.concatenate([rows, edge[OWN[k] + level]], axis=0)

    def inputs(j):
        if isinstance(j, int):
            return [wide(A0 + j), wide(N0 + j), wide(S0 + j)] + ([wide(P0 + j - 1)] if 0 < j < NC - 1 else [])
        return [wide_own(k, j - (HALO - 1)) for k in (1, 2, 3, 4)]

    def put(ref, i, value):
        ref[i, 8 : 8 + WIDE] = value
        ref[i, 0:8] = value[ROWS:WIDE]
        ref[i, 8 + WIDE : 16 + WIDE] = value[0:8]

    row = lax.broadcasted_iota(jnp.int32, (8, COLS), 0)
    x_low = jnp.where(row == 0, spot.x_first, 1.0)
    x_high = jnp.where(row == 7, spot.x_last, 1.0)

    def put_edge(ref, i, value):
        ref[i, 8 + ROWS : 8 + WIDE] = value
        ref[i, 0:8] = value
        ref[i, 8 + WIDE : 16 + WIDE] = ref[i, 8:16]

    for level in range(LEVELS):
        put_edge(ha, HALO + level, edge[OWN[0] + level])
    for i in range(HALO):
        put(ha, i, wide(H0 + i))
        put(ha, HALO + LEVELS + i, wide(H0 + HALO + LEVELS + i))
    put(kc, 0, wide(K_LO))
    put(kc, NH - 1, wide(K_HI))

    def mean4(ref, i):
        return (ref[i, 8 : 8 + WIDE] + ref[i + 1, 8 : 8 + WIDE] + ref[i + 2, 8 : 8 + WIDE] + ref[i + 3, 8 : 8 + WIDE]) * 0.25

    heads = [wide(M_LO)] + [mean4(ha, HALO + 4 * q) for q in range(LAYERS_PER_BLOCK)] + [wide(M_HI)]
    base = jnp.concatenate([spot.exp_first] * (WIDE // 8), axis=0)
    for q, value in enumerate(uptake_of(wide(TP), wide(RT), heads, spot.layers, base, spot.first)):
        sk[q] = value

    def first_curves(j):
        i = j + 1
        alpha2, half_n, half_ks, *poros = inputs(j)
        expo = expo_of(half_n)
        mm[j] = expo
        satur, cond = curves(ha[i, 8 : 8 + WIDE], alpha2, half_n, half_ks, expo)
        put(kc, i, cond)
        if poros:
            th[j - 1] = satur

    def later_curves(src, j):
        i = j + 1
        alpha2, half_n, half_ks, *poros = inputs(j)
        satur, cond = curves(src[i, 8 : 8 + WIDE], alpha2, half_n, half_ks, mm[j])
        put(kc, i, cond)
        if poros:
            wd[j - 1] = poros[0] * (satur - th[j - 1]) + sk[(i + 1) // LEVELS_PER_LAYER]

    def curves_of(body, extra):
        for j in range(HALO - 1 - extra, HALO - 1):
            body(j)
        loop(HALO - 1, HALO - 1 + LEVELS, body, 4)
        for j in range(HALO - 1 + LEVELS, HALO - 1 + LEVELS + extra):
            body(j)

    def stencil(src, i0, count, sweep, store):
        size = WIDE if sweep < SWEEPS - 1 else ROWS
        here = pl.ds(8, size)
        conds = [kc[i0 + g - 1, here, :] for g in range(count + 2)]
        heads = [src[i0 + g - 1, here, :] for g in range(count + 2)]
        faces = [conds[g] + conds[g + 1] for g in range(count + 1)]
        faces[0] = faces[0] * jnp.where(i0 == HALO, z_top, jnp.where(i0 == HALO + LEVELS, z_bottom, 1.0))
        end = i0 + count
        faces[count] = faces[count] * jnp.where(
            end == HALO, z_top, jnp.where(end == HALO + LEVELS, z_bottom, 1.0)
        )
        for g in range(count):
            i = i0 + g
            head, cond = heads[g + 1], conds[g + 1]
            kf_up, kf_down = faces[g], faces[g + 1]
            kf_xm = cond + kc[i, pl.ds(7, size), :]
            kf_xm = jnp.concatenate([kf_xm[0:8] * x_low, kf_xm[8:]], axis=0)
            kf_xp = cond + kc[i, pl.ds(9, size), :]
            parts = [kf_xp[: ROWS - 8], kf_xp[ROWS - 8 : ROWS] * x_high] + ([kf_xp[ROWS:]] if size > ROWS else [])
            kf_xp = jnp.concatenate(parts, axis=0)
            kf_ym = cond + pltpu.roll(cond, 1, 1)
            kf_yp = cond + pltpu.roll(cond, COLS - 1, 1)
            inflow = kf_up * (heads[g] + 1.0) + kf_down * (heads[g + 2] - 1.0)
            inflow = inflow + (kf_xm * src[i, pl.ds(7, size), :] + kf_xp * src[i, pl.ds(9, size), :])
            inflow = inflow + (kf_ym * pltpu.roll(head, 1, 1) + kf_yp * pltpu.roll(head, COLS - 1, 1))
            lost = wd[i - 2, 0:size, :] if sweep > 0 else sk[(i + 1) // LEVELS_PER_LAYER]
            diag = (1.0 + kf_up) + (kf_down + kf_xm) + (kf_xp + kf_ym) + kf_yp
            store(i, relax(head, inflow - lost, diag, sweep))

    def loop(lo, hi, body, unroll=1):
        def step(i, carry):
            body(i)
            return carry

        lax.fori_loop(lo, hi, step, 0, unroll=unroll)

    def levels_of(src, sweep, store):
        extra = SWEEPS - 1 - sweep
        if extra:
            stencil(src, HALO - extra, extra, sweep, store)
        loop(0, LEVELS // 8, lambda k: stencil(src, HALO + 8 * k, 8, sweep, store))
        if extra:
            stencil(src, HALO + LEVELS, extra, sweep, store)

    def edges(k):
        return edge[OWN[k] : OWN[k] + LEVELS].reshape(LEVELS * EDGE, COLS)

    half_n = edges(2)
    expo = expo_of(half_n)
    satur, cond = curves(edges(0), edges(1), half_n, edges(3), expo)
    for level in range(LEVELS):
        rows = slice(level * EDGE, (level + 1) * EDGE)
        put_edge(kc, HALO + level, cond[rows])
        mm[HALO - 1 + level, ROWS:WIDE] = expo[rows]
        th[HALO - 2 + level, ROWS:WIDE] = satur[rows]
    for j in (0, 1, NC - 2, NC - 1):
        first_curves(j)
    levels_of(ha, 0, lambda i, value: put(hb, i, value))
    land_sent = heat_finish()

    lane_wide = lax.broadcasted_iota(jnp.int32, (WIDE, COLS), 1)
    acc = jnp.zeros((WIDE, COLS), jnp.float32)
    for k in range(NC):
        lane = inner_lane(k)
        pick = (lane_wide == lane) | (lane_wide == lane + 9)
        acc = jnp.where(pick, pltpu.roll(hb[k + 1, 8 : 8 + WIDE], (lane - (COLS - 1 - NEAR)) % COLS, 1), acc)
    inner[...] = widened(acc).T

    poro_copy.wait()
    curves_of(lambda j: later_curves(hb, j), 2)
    levels_of(hb, 1, lambda i, value: put(ha, i, value))
    curves_of(lambda j: later_curves(ha, j), 1)

    def keep(i, value):
        out[i - HALO] = value

    levels_of(ha, 2, keep)
    land_sent.wait()


def edge_strips(count_role, count_gx, count_gz, main, inner, strips_in, y_e, y_o, out,
                strips, sa, sb, sc, ks, sm, sth, swd, ssk, turn, done, lines, sem):
    spot = Where(count_role, count_gx, count_gz)
    z_top, z_bottom = spot.z_top, spot.z_bottom
    f32 = jnp.float32
    strips[...] = strips_in[...]

    line = lax.broadcasted_iota(jnp.int32, (Y_EXTRA, COLS), 1)

    def take(high, low):
        for got, last in ((high, False), (low, True)):
            extra = got[Y_ROWS // 2 : Y_SEND]
            for g in range(Y_ROWS // Y_EXTRA):
                first = g * Y_EXTRA % (Y_ROWS // 2)
                rows = got[first : first + Y_EXTRA]
                if g * Y_EXTRA >= Y_ROWS // 2:
                    rows = pltpu.roll(rows, ROWS, 1)
                rows = jnp.where(line < ROWS, rows, pltpu.roll(extra, (ROWS - EDGE * g) % COLS, 1))
                rows = jnp.where(line < COLS - EDGE, rows, pltpu.roll(extra, (COLS - EDGE - EDGE * g) % COLS, 1))
                lines[g * Y_EXTRA : (g + 1) * Y_EXTRA] = rows
            at = 0
            for p in range(PLANES):
                count = columns_sent(p)
                if count:
                    start = p * SIDE + (SIDE - count if last else 0)
                    strips[pl.ds(start, count), :] = lines[pl.ds(at, count), :]
                    at += count

    by_parity("role", take, y_e, y_o)

    def strip(p, count=1):
        return strips[p * SIDE : (p + count) * SIDE, :]

    heads = [strip(M_LO)]
    for q in range(LAYERS_PER_BLOCK):
        at = H0 + HALO + 4 * q
        heads.append((strip(at) + strip(at + 1) + strip(at + 2) + strip(at + 3)) * 0.25)
    heads.append(strip(M_HI))
    base = jnp.concatenate([spot.exp_first] * 2, axis=0)
    for q, value in enumerate(uptake_of(strip(TP), strip(RT), heads, spot.layers, base, spot.first)):
        ssk[q * SIDE : (q + 1) * SIDE, :] = value

    lane = lax.broadcasted_iota(jnp.int32, (SIDE, COLS), 1)
    srow = lax.broadcasted_iota(jnp.int32, (SIDE, COLS), 0)
    s_xm = jnp.where(lane == 0, spot.x_first, 1.0)
    s_xp = jnp.where(lane == ROWS - 1, spot.x_last, 1.0)
    side_mask = jnp.where(srow < 8, spot.y_last, spot.y_first)
    s_ym = jnp.where(srow % 8 == 0, side_mask, 1.0)
    s_yp = jnp.where(srow % 8 == 7, side_mask, 1.0)

    def tiled(mask, count):
        return jnp.concatenate([mask] * count, axis=0)

    def y_shift(value, by):
        parts = value.reshape(value.shape[0] // 8, 8, COLS)
        return pltpu.roll(parts, by, 1).reshape(value.shape)

    def rows_of(i, count):
        return slice(i * SIDE, (i + count) * SIDE)

    def strip_curves(src, lo, hi, sweep):
        i = lo
        while i < hi:
            count = min(5, hi - i)
            j = i - 1
            here = rows_of(i, count)
            half_n = strip(N0 + j, count)
            if sweep == 0:
                expo = expo_of(half_n)
                sm[rows_of(j, count), :] = expo
            else:
                expo = sm[rows_of(j, count), :]
            satur, cond = curves(src[here, :], strip(A0 + j, count), half_n, strip(S0 + j, count), expo)
            ks[here, :] = cond
            start, stop = max(i, 2), min(i + count, NH - 2)
            if stop > start:
                part = satur[(start - i) * SIDE : (stop - i) * SIDE]
                at = rows_of(start - 2, stop - start)
                if sweep == 0:
                    sth[at, :] = part
                else:
                    swd[at, :] = strip(P0 + start - 2, stop - start) * (part - sth[at, :])
            i += count

    def strip_stencil(src, dst, lo, hi, sweep):
        i = lo
        while i < hi:
            count = min(5, hi - i)
            here = rows_of(i, count)
            above, below = rows_of(i - 1, count), rows_of(i + 1, count)
            head, cond = src[here, :], ks[here, :]
            kf_up = cond + ks[above, :]
            kf_down = cond + ks[below, :]
            if i <= HALO < i + count:
                level = lax.broadcasted_iota(jnp.int32, kf_up.shape, 0) // SIDE
                kf_up = jnp.where(level == HALO - i, kf_up * z_top, kf_up)
            if i <= HALO + LEVELS - 1 < i + count:
                level = lax.broadcasted_iota(jnp.int32, kf_up.shape, 0) // SIDE
                kf_down = jnp.where(level == HALO + LEVELS - 1 - i, kf_down * z_bottom, kf_down)
            kf_xm = (cond + pltpu.roll(cond, 1, 1)) * tiled(s_xm, count)
            kf_xp = (cond + pltpu.roll(cond, COLS - 1, 1)) * tiled(s_xp, count)
            kf_ym = (cond + y_shift(cond, 1)) * tiled(s_ym, count)
            kf_yp = (cond + y_shift(cond, 7)) * tiled(s_yp, count)
            inflow = kf_up * (src[above, :] + 1.0) + kf_down * (src[below, :] - 1.0)
            inflow = inflow + (kf_xm * pltpu.roll(head, 1, 1) + kf_xp * pltpu.roll(head, COLS - 1, 1))
            inflow = inflow + (kf_ym * y_shift(head, 1) + kf_yp * y_shift(head, 7))
            lost = jnp.concatenate([ssk[rows_of((k + 1) // LEVELS_PER_LAYER, 1), :] for k in range(i, i + count)], axis=0)
            if sweep > 0:
                lost = lost + swd[rows_of(i - 2, count), :]
            diag = (1.0 + kf_up) + (kf_down + kf_xm) + (kf_xp + kf_ym) + kf_yp
            dst[here, :] = relax(head, inflow - lost, diag, sweep)
            i += count

    ks[rows_of(0, 1), :] = strip(K_LO)
    ks[rows_of(NH - 1, 1), :] = strip(K_HI)
    strip_curves(strips, 1, NH - 1, 0)
    strip_stencil(strips, sa, 1, NH - 1, 0)
    for k in range(NC):
        lane = inner_lane(k)
        sa[pl.ds((k + 1) * SIDE + 3, 1), :] = inner[pl.ds(lane, 1), :]
        sa[pl.ds((k + 1) * SIDE + 8 + NEAR, 1), :] = inner[pl.ds(lane + 9, 1), :]
    strip_curves(sa, 1, NH - 1, 1)
    strip_stencil(sa, sb, 2, NH - 2, 1)
    strip_curves(sb, 2, NH - 2, 2)

    lane_rows = lax.broadcasted_iota(jnp.int32, (ROWS, COLS), 1)
    outer = (lane_rows < HALO) | (lane_rows >= COLS - HALO)
    copies = []
    half = LEVELS // 2
    for first in (0, half):
        strip_stencil(sb, sc, HALO + first, HALO + first + half, 2)
        pieces = [sc[i * SIDE + 8 - HALO : i * SIDE + 8 + HALO, :] for i in range(HALO + first, HALO + first + half)]
        pieces.append(jnp.zeros((COLS - 2 * HALO * half, COLS), f32))
        turn[...] = jnp.concatenate(pieces, axis=0).T[0:ROWS]
        for k in range(half):
            moved = pltpu.roll(turn[...], (COLS - HALO - 2 * HALO * k) % COLS, 1)
            level = first + k
            done[level] = jnp.where(outer, moved, main[level])
            copy = pltpu.make_async_copy(done.at[level], out.at[level], sem.at[level])
            copy.start()
            copies.append(copy)
    for copy in copies:
        copy.wait()


def heat(count_gx, count_gz, y, temp_in, tr_in, air_in, rt_in, land_out, out, sat, head, temp, tr, air, rt, sem, out_sem):
    copies = []
    for src, dst in ((temp_in, temp), (tr_in, tr), (air_in, air), (rt_in, rt)):
        copy = pltpu.make_async_copy(src, dst, sem.at[len(copies)])
        copy.start()
        copies.append(copy)
    def finish():
        me = place("gx") * count_gz + place("gz")
        layers = LAYERS_PER_BLOCK * count_gz
        for copy in copies:
            copy.wait()
        for gx in range(count_gx):
            for gz in range(count_gz):
                j = me ^ (gx * count_gz + gz)
                for c in range(CAP):
                    tile = y[j, c * 8 : c * 8 + 8]
                    at = pl.ds(gz * LAYERS_PER_BLOCK, LAYERS_PER_BLOCK)
                    sat[gx * CAP + c, at, :] = tile[0:LAYERS_PER_BLOCK]
                    head[gx * CAP + c, at, :] = tile[LAYERS_PER_BLOCK : 2 * LAYERS_PER_BLOCK]
        layer = lax.broadcasted_iota(jnp.int32, (layers, COLS), 0)
        decay = jnp.exp(layer.astype(jnp.float32) * -0.25)
        for slot in range(count_gx * CAP):
            roots = jnp.broadcast_to(rt[slot], (layers, COLS))
            weight = jnp.where(layer < roots, decay, 0.0)
            weight = weight / jnp.sum(weight, axis=0, keepdims=True)
            stress = 1.0 / (1.0 + head[slot] * head[slot] * (1.0 / 2.25))
            uptake = tr[slot] * weight * stress
            kappa = 0.25 + 0.9 * sat[slot]
            top = jnp.broadcast_to(air[slot], (layers, COLS))
            k_above = jnp.where(layer == 0, kappa, 0.5 * (kappa + pltpu.roll(kappa, 1, 0)))
            k_below = jnp.where(layer == layers - 1, 0.0, 0.5 * (kappa + pltpu.roll(kappa, layers - 1, 0)))
            old = temp[slot]
            new = old
            for _ in range(HEAT_STEPS):
                above = jnp.where(layer == 0, top, pltpu.roll(new, 1, 0))
                below = pltpu.roll(new, layers - 1, 0)
                new = new + 0.2 * (k_above * (above - new) + k_below * (below - new)) - 0.3 * uptake
            out[slot] = jnp.where(sat[slot] >= 0.0, new, old)
        sent = pltpu.make_async_copy(out, land_out, out_sem)
        sent.start()
        return sent

    return finish


def call(body, outs, ins, scratch=(), aliases=None, limit=16 * MIB, kept=True, work=0):
    return pl.pallas_call(
        body,
        out_shape=[pltpu.VMEM(shape, jnp.float32) if kept else jax.ShapeDtypeStruct(shape, jnp.float32) for shape in outs],
        in_specs=ins,
        out_specs=[VMEM] * len(outs),
        scratch_shapes=list(scratch),
        input_output_aliases=aliases or {},
        compiler_params=pltpu.CompilerParams(vmem_limit_bytes=limit),
        cost_estimate=pl.CostEstimate(flops=work, bytes_accessed=work, transcendentals=0) if work else None,
    )


DEEP = WIDE + 16
START_SHAPES = [(NH, DEEP, COLS), (NH, DEEP, COLS), (NC, WIDE, COLS), (NP, WIDE, COLS)]


def main_call(count_role, count_gx, count_gz):
    f32 = jnp.float32
    slots = count_gx * CAP
    land_shape = (slots, LAYERS_PER_BLOCK * count_gz, COLS)
    return pl.pallas_call(
        functools.partial(main_region, count_role, count_gx, count_gz),
        out_shape=[
            pltpu.VMEM((LEVELS, ROWS, COLS), f32),
            pltpu.VMEM((COLS, COLS), f32),
            jax.ShapeDtypeStruct(land_shape, f32),
        ]
        + [pltpu.VMEM(shape, f32) for shape in START_SHAPES],
        in_specs=[VMEM] * 4 + [HBM] * 5 + [VMEM] * 4,
        out_specs=[VMEM] * 2 + [HBM] + [VMEM] * 4,
        input_output_aliases={9 + k: 3 + k for k in range(4)},
        scratch_shapes=[
            pltpu.VMEM((NH, DEEP, COLS), f32),
            pltpu.VMEM((NP, WIDE, COLS), f32),
            pltpu.VMEM((LAYERS_PER_BLOCK + 2, WIDE, COLS), f32),
            pltpu.VMEM((LEVELS, ROWS, COLS), f32),
            pltpu.SemaphoreType.DMA(()),
            pltpu.VMEM(land_shape, f32),
            pltpu.VMEM(land_shape, f32),
            pltpu.VMEM(land_shape, f32),
            pltpu.VMEM(land_shape, f32),
            pltpu.VMEM((slots, 1, COLS), f32),
            pltpu.VMEM((slots, 1, COLS), f32),
            pltpu.VMEM((slots, 1, COLS), jnp.int32),
            pltpu.SemaphoreType.DMA((4,)),
            pltpu.SemaphoreType.DMA(()),
        ],
        compiler_params=pltpu.CompilerParams(vmem_limit_bytes=16 * MIB),
    )


def strip_call(count_role, count_gx, count_gz):
    f32 = jnp.float32
    return pl.pallas_call(
        functools.partial(edge_strips, count_role, count_gx, count_gz),
        out_shape=jax.ShapeDtypeStruct((LEVELS, ROWS, COLS), f32),
        in_specs=[VMEM] * 5,
        out_specs=HBM,
        scratch_shapes=[
            pltpu.VMEM((PACKS * COLS, COLS), f32),
            pltpu.VMEM((NH * SIDE, COLS), f32),
            pltpu.VMEM((NH * SIDE, COLS), f32),
            pltpu.VMEM((NH * SIDE, COLS), f32),
            pltpu.VMEM((NH * SIDE, COLS), f32),
            pltpu.VMEM((NC * SIDE, COLS), f32),
            pltpu.VMEM((NP * SIDE, COLS), f32),
            pltpu.VMEM((NP * SIDE, COLS), f32),
            pltpu.VMEM(((LAYERS_PER_BLOCK + 2) * SIDE, COLS), f32),
            pltpu.VMEM((ROWS, COLS), f32),
            pltpu.VMEM((LEVELS, ROWS, COLS), f32),
            pltpu.VMEM((Y_ROWS, COLS), f32),
            pltpu.SemaphoreType.DMA((LEVELS,)),
        ],
        compiler_params=pltpu.CompilerParams(vmem_limit_bytes=16 * MIB),
    )


def local(h, a, n, s, p, tile_owner, land_temp, tr, air, rt):
    sizes = tuple(lax.axis_size(axis) for axis in AXES)
    count_role, count_gx, count_gz = sizes
    groups = count_gx * count_gz
    slots = count_gx * CAP
    f32 = jnp.float32

    def swap(value, axis, odd):
        return lax.ppermute(value, AXES, pairing(sizes, axis, odd))

    owners = tile_owner.T
    land = (land_temp[0, 0], tr[0, 0, :, None], air[0, 0, :, None], rt[0, 0, :, None])
    h, a, n, s, p = (pltpu.with_memory_space_constraint(x, pltpu.HBM) for x in (h, a, n, s, p))
    land_temp, tr, air, rt = (pltpu.with_memory_space_constraint(x, pltpu.HBM) for x in land)

    z_send_e, z_send_o = call(
        z_faces,
        [(Z_SEND, ROWS, COLS)] * 2,
        [HBM] * 5,
        [
            pltpu.VMEM((2, 4, ROWS, COLS), f32),
            pltpu.VMEM((2, 3, ROWS, COLS), f32),
            pltpu.VMEM((2, 3, ROWS, COLS), f32),
            pltpu.VMEM((2, 3, ROWS, COLS), f32),
            pltpu.VMEM((2, 1, ROWS, COLS), f32),
            pltpu.SemaphoreType.DMA((10,)),
        ],
    )(h, a, n, s, p)
    z_e = swap(z_send_e, "gz", False)
    z_o = swap(z_send_o, "gz", True) if count_gz > 2 else z_e

    half = groups // 2
    blocks = count_gx // 2
    packed = half * 8 * CAP + blocks * 8
    x_count = 1 if count_gx == 2 else 2
    x_shape = (PLANES, 4, COLS)
    own_shapes = [(len(OWN_AT), 16, COLS), (PACKS, ROWS, COLS)]

    def land_stage():
        send, keep, hot = call(
            functools.partial(land_pack, count_gx, count_gz),
            [(packed, COLS), (packed, COLS), (ROWS, groups * 8)],
            [SMEM] + [HBM] * 5,
            [
                pltpu.VMEM((2 * LAYERS_PER_BLOCK, ROWS, COLS), f32),
                pltpu.SMEM((groups,), jnp.int32),
                pltpu.SMEM((groups * CAP,), jnp.int32),
                pltpu.VMEM((LEVELS, ROWS, COLS), f32),
                pltpu.VMEM((LEVELS, ROWS, COLS), f32),
                pltpu.VMEM((LEVELS, ROWS, COLS), f32),
                pltpu.VMEM((slots, 1, COLS), f32),
                pltpu.VMEM((slots, 1, COLS), jnp.int32),
                pltpu.SemaphoreType.DMA((3 * LAYERS_PER_BLOCK + 2,)),
            ],
        )(owners, h, a, n, tr, rt)

        got = lax.ppermute(send, AXES, xor_pairs(sizes, "gx", blocks))
        bit = blocks // 2
        if bit:
            pieces = [part[j * PIECE : (j + 1) * PIECE] for part in (keep, got) for j in range(half)]
            base = half * PIECE
            values = [part[base + j * 8 : base + (j + 1) * 8] for part in (keep, got) for j in range(blocks)]
            while bit:
                moving = [j for j in range(groups) if (j // count_gz) & bit]
                t_moving = [j for j in range(count_gx) if j & bit]
                sent = jnp.concatenate([pieces[j] for j in moving] + [values[j] for j in t_moving], axis=0)
                got = lax.ppermute(sent, AXES, xor_pairs(sizes, "gx", bit))
                for k, j in enumerate(moving):
                    pieces[j] = got[k * PIECE : (k + 1) * PIECE]
                for k, j in enumerate(t_moving):
                    base = len(moving) * PIECE + k * 8
                    values[j] = got[base : base + 8]
                bit //= 2
            keep = jnp.concatenate(pieces[:half] + values[:blocks], axis=0)
            got = jnp.concatenate(pieces[half:] + values[blocks:], axis=0)
        rim, pack = call(
            own_part,
            own_shapes,
            [HBM] * 5,
            [pltpu.VMEM((len(OWN_AT), ROWS, COLS), f32), pltpu.SemaphoreType.DMA((5,))],
        )(h, a, n, s, p)
        parts = call(
            functools.partial(land_sort, count_gx, count_gz),
            [(count_gx * (PIECE + 8), COLS)] * count_gz,
            [VMEM] * 2,
        )(keep, got)
        parts = [parts[0]] + [
            lax.ppermute(parts[dist], AXES, xor_pairs(sizes, "gz", dist)) for dist in range(1, count_gz)
        ]
        tile, y = call(
            functools.partial(tile_values, count_gx, count_gz),
            [(2, ROWS, COLS), (groups, PIECE, COLS)],
            [VMEM] * (1 + count_gz),
        )(hot, *parts)
        return [rim, pack, tile, y]

    def no_land_stage():
        shapes = own_shapes + [(2, ROWS, COLS), (groups, PIECE, COLS)]
        return [jnp.zeros(shape, f32) for shape in shapes]

    ahead = lax.optimization_barrier(jnp.bool_(True))
    rim, pack, tile, y = lax.cond(ahead, land_stage, no_land_stage)

    ext, *x_sends = call(
        functools.partial(x_faces, count_gx),
        [(len(EXT_AT), ROWS, COLS)] + [x_shape] * x_count,
        [VMEM] * 4,
    )(rim, z_e, z_o, tile)
    params, *start = call(
        own_curves,
        [(3 * LEVELS, ROWS, COLS)] + START_SHAPES,
        [HBM] * 4,
        [pltpu.SemaphoreType.DMA((LEVELS,))],
    )(h, a, n, s)
    x_got = [swap(value, "gx", bool(k)) for k, value in enumerate(x_sends)]

    edge, strips, y_send_e, y_send_o = call(
        functools.partial(y_faces, count_gx),
        [(PLANES, EDGE, COLS), (PACKS * COLS, COLS), (Y_SEND, COLS), (Y_SEND, COLS)],
        [VMEM] * 3 + [ANY] + [VMEM] * x_count,
        [pltpu.VMEM((Y_ROWS, COLS), f32)],
    )(rim, pack, ext, params, *x_got)
    y_e = swap(y_send_e, "role", False)
    y_o = swap(y_send_o, "role", True) if count_role > 2 else y_e

    main, inner, land_new, *_ = main_call(*sizes)(params, ext, edge, y, land_temp, tr, air, rt, p, *start)
    head = strip_call(*sizes)(main, inner, strips, y_e, y_o)
    return (head, land_new[None, None])


def solution(mesh):
    in_specs = (
        P("gz", "gx", "role"),
        P("gz", "gx", "role"),
        P("gz", "gx", "role"),
        P("gz", "gx", "role"),
        P("gz", "gx", "role"),
        P(),
        P("role", ("gx", "gz"), None, None, None),
        P("role", ("gx", "gz"), None, None),
        P("role", ("gx", "gz"), None, None),
        P("role", ("gx", "gz"), None, None),
    )
    out_specs = (P("gz", "gx", "role"), P("role", ("gx", "gz"), None, None, None))
    return jax.shard_map(local, mesh=mesh, in_specs=in_specs, out_specs=out_specs, check_vma=False)
```

```python
import functools
import math

import jax
import jax.numpy as jnp
from jax import lax
from jax.experimental import pallas as pl
from jax.experimental.pallas import tpu as pltpu
from jax.sharding import PartitionSpec as P

LAYERS_PER_BLOCK = 4
LEVELS_PER_LAYER = 4
CAP = 3
SWEEPS = 3
HEAT_STEPS = 4
HALO = SWEEPS
AXES = ("role", "gx", "gz")
VMEM = pl.BlockSpec(memory_space=pltpu.VMEM)
HBM = pl.BlockSpec(memory_space=pltpu.HBM)
ANY = pl.BlockSpec(memory_space=pl.ANY)
MIB = 1024 * 1024

LEVELS = 16
ROWS = 64
COLS = 128
EDGE = 8
WIDE = ROWS + EDGE
H0 = 0
NH = LEVELS + 2 * HALO
A0 = H0 + NH
NC = LEVELS + 2 * HALO - 2
N0 = A0 + NC
S0 = N0 + NC
K_LO = S0 + NC
K_HI = K_LO + 1
P0 = K_HI + 1
NP = LEVELS + 2 * HALO - 4
M_LO = P0 + NP
M_HI = M_LO + 1
TP = M_HI + 1
RT = TP + 1
PLANES = RT + 1
PACKS = (PLANES + 7) // 8
SIDE = 16
NEAR = 4
Z_SEND = 12
PIECE = 8 * CAP


def columns_sent(p):
    for first, count, reach in ((H0, NH, HALO), (A0, NC, HALO), (N0, NC, HALO), (S0, NC, HALO), (P0, NP, 1)):
        if first <= p < first + count:
            out = (count - LEVELS) // 2
            level = p - first - out
            away = max(0, -level, level - LEVELS + 1)
            return max(0, reach - away)
    return {M_LO: 1, M_HI: 1, TP: 2, RT: 2}.get(p, 0)


Y_ROWS = 256
Y_EXTRA = Y_ROWS // (ROWS // EDGE)
Y_SEND = Y_ROWS // 2 + Y_EXTRA


def omega(sweep):
    return 1.0 / (1.0 + 0.6 * math.cos(math.pi * (2 * sweep + 1) / (2 * SWEEPS)))


def place(axis):
    return lax.axis_index(axis)


def is_even(axis):
    return lax.rem(place(axis), 2) == 0


def pairing(sizes, axis, odd):
    pairs = []
    which = AXES.index(axis)
    for index in range(math.prod(sizes)):
        at = [index // (sizes[1] * sizes[2]), index // sizes[2] % sizes[1], index % sizes[2]]
        count = sizes[which]
        there = list(at)
        if not odd:
            there[which] = at[which] ^ 1
        else:
            there[which] = at[which] + (1 if at[which] % 2 else -1)
            if not 0 <= there[which] < count:
                there = list(at)
                if axis == "gx":
                    there[1] = count - 1 - at[1]
                else:
                    there[1] = at[1] ^ 1
        pairs.append((index, (there[0] * sizes[1] + there[1]) * sizes[2] + there[2]))
    return pairs


def xor_pairs(sizes, axis, bit):
    pairs = []
    which = AXES.index(axis)
    for index in range(math.prod(sizes)):
        at = [index // (sizes[1] * sizes[2]), index // sizes[2] % sizes[1], index % sizes[2]]
        at[which] ^= bit
        pairs.append((index, (at[0] * sizes[1] + at[1]) * sizes[2] + at[2]))
    return pairs


LOG2E = math.log2(math.e)
HALF_LOG2E = 0.5 * LOG2E


def saturation_of(head, alpha2, half_n, expo):
    logx = half_n * jnp.log(alpha2 * (head * head + 0.01))
    softer = LOG2E * jnp.log(1.0 + jnp.exp2(logx))
    return logx, softer, jnp.exp2(-0.5 * expo * softer)


def curves(head, alpha2, half_n, half_ks, expo):
    logx, softer, root = saturation_of(head, alpha2, half_n, expo)
    gap = 1.0 - jnp.exp2(expo * (logx - softer))
    return root * root, half_ks * root * (gap * gap)


def inverse(value):
    guess = pl.reciprocal(value, approx=True)
    return guess * (2.0 - value * guess)


def expo_of(half_n):
    return 1.0 - HALF_LOG2E * inverse(half_n)


def relax(head, inflow, diag, sweep):
    step = omega(sweep)
    return (1.0 - step) * head + (step * (head + inflow)) * inverse(diag)


def z_faces(h, a, n, s, p, out_e, out_o, hb, ab, nb, sb, pb, sem):
    copies = []
    for src, dst, count in ((h, hb, 4), (a, ab, 3), (n, nb, 3), (s, sb, 3), (p, pb, 1)):
        for side in range(2):
            start = 0 if side == 0 else LEVELS - count
            copy = pltpu.make_async_copy(src.at[pl.ds(start, count)], dst.at[side], sem.at[len(copies)])
            copy.start()
            copies.append(copy)
    def level(buf, side, count, dist):
        return buf[side, dist - 1 if side == 0 else count - dist]

    def put_heads(out, side):
        for dist in (1, 2, 3):
            out[dist - 1] = level(hb, side, 4, dist)
        out[11] = (hb[side, 0] + hb[side, 1] + hb[side, 2] + hb[side, 3]) * 0.25

    def put_rest(out, side):
        for dist in (1, 2):
            alpha = level(ab, side, 3, dist)
            out[2 + dist] = alpha * alpha
            out[4 + dist] = HALF_LOG2E * level(nb, side, 3, dist)
            out[6 + dist] = 0.5 * level(sb, side, 3, dist)
        out[9] = level(pb, side, 1, 1)
        alpha = level(ab, side, 3, 3)
        half_n = HALF_LOG2E * level(nb, side, 3, 3)
        half_ks = 0.5 * level(sb, side, 3, 3)
        out[10] = curves(level(hb, side, 4, 3), alpha * alpha, half_n, half_ks, expo_of(half_n))[1]

    for waited, put in ((copies[:2], put_heads), (copies[2:], put_rest)):
        for copy in waited:
            copy.wait()

        def both(first, second):
            put(out_e, first)
            put(out_o, second)

        by_parity("gz", both, 1, 0)


def land_pack(count_gx, count_gz, owners_in, h_in, a_in, n_in, tr_in, rt_in, send, keep, hot,
              owners, means, counts, slots, h, a, n, tr, rt, sem, owners_sem):
    groups = count_gx * count_gz
    me_role, me_gx = place("role"), place("gx")
    me = me_gx * count_gz + place("gz")
    owners_copy = pltpu.make_async_copy(owners_in, owners, owners_sem)
    owners_copy.start()
    copies = []
    for layer in range(LAYERS_PER_BLOCK):
        some = pl.ds(layer * LEVELS_PER_LAYER, LEVELS_PER_LAYER)
        for src, dst in ((h_in, h), (a_in, a), (n_in, n)):
            copies.append(pltpu.make_async_copy(src.at[some], dst.at[some], sem.at[len(copies)]))
    for src, dst in ((tr_in, tr), (rt_in, rt)):
        copies.append(pltpu.make_async_copy(src, dst, sem.at[len(copies)]))
    for copy in copies:
        copy.start()

    def clear_slot(i, carry):
        slots[i] = -1
        return carry

    def clear_count(i, carry):
        counts[i] = 0
        return carry

    lax.fori_loop(0, groups * CAP, clear_slot, 0)
    lax.fori_loop(0, groups, clear_count, 0)
    lane = lax.broadcasted_iota(jnp.int32, (1, groups * 8), 1)

    def step(x, carry):
        owner = owners[me_role, me_gx * ROWS + x]
        safe = jnp.maximum(owner, 0)
        rank = counts[safe]
        at = jnp.where(owner >= 0, (me ^ owner) * 8 + 2 * rank, -1)
        hot[pl.ds(x, 1), :] = jnp.where(lane == at, 1.0, 0.0)

        @pl.when(owner >= 0)
        def _():
            counts[owner] = rank + 1
            slots[owner * CAP + rank] = x

        return carry

    owners_copy.wait()
    lax.fori_loop(0, ROWS, step, 0, unroll=8)
    for layer in range(LAYERS_PER_BLOCK):
        for copy in copies[3 * layer : 3 * layer + 3]:
            copy.wait()
        saturs = []
        heads = []
        for level in range(layer * LEVELS_PER_LAYER, (layer + 1) * LEVELS_PER_LAYER):
            head = h[level]
            alpha = a[level]
            half_n = HALF_LOG2E * n[level]
            root = saturation_of(head, alpha * alpha, half_n, expo_of(half_n))[2]
            saturs.append(root * root)
            heads.append(head)
        means[layer] = (saturs[0] + saturs[1] + saturs[2] + saturs[3]) * 0.25
        means[LAYERS_PER_BLOCK + layer] = (heads[0] + heads[1] + heads[2] + heads[3]) * 0.25
    for copy in copies[3 * LAYERS_PER_BLOCK :]:
        copy.wait()
    half = groups // 2
    for j in range(groups):
        out, k = (keep, j) if j < half else (send, j - half)
        for c in range(CAP):
            row = slots[(me ^ j) * CAP + c]
            safe = jnp.maximum(row, 0)
            for q in range(8):
                value = means[q, pl.ds(safe, 1), :]
                out[pl.ds(k * PIECE + c * 8 + q, 1), :] = jnp.where(row >= 0, value, -1.0)
    blocks = count_gx // 2
    for j in range(count_gx):
        block = me_gx ^ j
        out, k = (keep, j) if j < blocks else (send, j - blocks)
        base = half * PIECE + k * 8
        out[pl.ds(base, 8), :] = jnp.zeros((8, COLS), jnp.float32)
        for c in range(CAP):
            out[pl.ds(base + 2 * c, 1), :] = tr[block * CAP + c]
            out[pl.ds(base + 2 * c + 1, 1), :] = rt[block * CAP + c].astype(jnp.float32)


def land_sort(count_gx, count_gz, keep, got, *outs):
    half, blocks = count_gx * count_gz // 2, count_gx // 2
    for gx in range(count_gx):
        src, k = (keep, gx) if gx < blocks else (got, gx - blocks)
        for dist in range(count_gz):
            at = (k * count_gz + dist) * PIECE
            outs[dist][gx * PIECE : (gx + 1) * PIECE] = src[at : at + PIECE]
            base = count_gx * PIECE + gx * 8
            outs[dist][base : base + 8] = src[half * PIECE + k * 8 : half * PIECE + k * 8 + 8]


def tile_values(count_gx, count_gz, hot, *refs):
    parts, out, y = refs[:count_gz], refs[count_gz], refs[count_gz + 1]
    values = []
    for gx in range(count_gx):
        for dist in range(count_gz):
            base = count_gx * PIECE + gx * 8
            values.append(parts[dist][base : base + 8])
            y[gx * count_gz + dist] = parts[dist][gx * PIECE : (gx + 1) * PIECE]
    t = jnp.concatenate(values, axis=0)
    out[0] = exact_dot(hot[...], t)
    out[1] = jnp.maximum(exact_dot(hot[...], pltpu.roll(t, t.shape[0] - 1, 0)), 1.0)


def exact_dot(hot, values):
    total = None
    rest = values
    left = hot.astype(jnp.bfloat16)
    for _ in range(3):
        part = rest.astype(jnp.bfloat16)
        rest = rest - part.astype(jnp.float32)
        term = jnp.dot(left, part, preferred_element_type=jnp.float32)
        total = term if total is None else total + term
    return total


def z_places(low):
    places = [H0 + (HALO - dist if low else HALO + LEVELS - 1 + dist) for dist in (1, 2, 3)]
    for first in (A0, N0, S0):
        places += [first + (HALO - 1 - dist if low else HALO - 2 + LEVELS + dist) for dist in (1, 2)]
    return places + [P0 + (0 if low else NP - 1), K_LO if low else K_HI, M_LO if low else M_HI]


def by_parity(axis, action, first, second):
    even = is_even(axis)

    @pl.when(even)
    def _():
        action(first, second)

    @pl.when(jnp.logical_not(even))
    def _():
        action(second, first)


OWN = (H0 + HALO, A0 + HALO - 1, N0 + HALO - 1, S0 + HALO - 1, P0 + HALO - 2)


def scaled(k, value):
    return (value, value * value, HALF_LOG2E * value, 0.5 * value, value)[k]


def packed_tile(tile, rows_of, count):
    lane_group = lax.broadcasted_iota(jnp.int32, (count, COLS), 1) // SIDE
    acc = jnp.zeros((count, COLS), jnp.float32)
    for j in range(8):
        p = tile * 8 + j
        value = rows_of(p) if p < PLANES else None
        if value is not None:
            acc = jnp.where(lane_group == j, pltpu.roll(value, SIDE * j + 8, 1), acc)
    return acc


OWN_AT = {first + level: k * LEVELS + level for k, first in enumerate(OWN) for level in range(LEVELS)}
EXT_AT = {p: k for k, p in enumerate(p for p in range(PLANES) if p not in OWN_AT)}


def own_planes(*refs):
    arrays, own, sem = refs[:5], refs[5], refs[6]
    copies = []
    for k, src in enumerate(arrays):
        copy = pltpu.make_async_copy(src, own.at[pl.ds(k * LEVELS, LEVELS)], sem.at[k])
        copy.start()
        copies.append(copy)
    for k, copy in enumerate(copies):
        copy.wait()
        if 0 < k < 4:
            for level in range(LEVELS):
                own[k * LEVELS + level] = scaled(k, own[k * LEVELS + level])


def own_part(*refs):
    arrays, rim, pack, own, sem = refs[:5], refs[5], refs[6], refs[7], refs[8]
    own_planes(*arrays, own, sem)
    for k in range(len(OWN_AT)):
        rim[k, 0:8] = own[k, 0:8]
        rim[k, 8:16] = own[k, ROWS - 8 : ROWS]
    for t in range(PACKS):
        pack[t] = packed_tile(t, lambda p: own[OWN_AT[p]] if p in OWN_AT else None, ROWS)


def own_curves(*refs):
    arrays, (params, ha, kc, mm, th, sem) = refs[:4], refs[4:]
    step = 4
    copies = []
    for first in range(0, LEVELS, step):
        for k, src in enumerate(arrays):
            if k == 0:
                dst = ha.at[pl.ds(HALO + first, step), pl.ds(8, ROWS), :]
            else:
                dst = params.at[pl.ds((k - 1) * LEVELS + first, step)]
            copies.append(pltpu.make_async_copy(src.at[pl.ds(first, step)], dst, sem.at[len(copies)]))
    for copy in copies:
        copy.start()
    for first in range(0, LEVELS, step):
        for copy in copies[first // step * 4 : first // step * 4 + 4]:
            copy.wait()
        for level in range(first, first + step):
            i = HALO + level
            alpha2, half_n, half_ks = (scaled(k, params[(k - 1) * LEVELS + level]) for k in (1, 2, 3))
            params[level] = alpha2
            params[LEVELS + level] = half_n
            params[2 * LEVELS + level] = half_ks
            head = ha[i, 8 : 8 + ROWS]
            expo = expo_of(half_n)
            satur, cond = curves(head, alpha2, half_n, half_ks, expo)
            kc[i, 8 : 8 + ROWS] = cond
            mm[i - 1, 0:ROWS] = expo
            th[i - 2, 0:ROWS] = satur


def x_faces(count_gx, rim, z_e, z_o, tile, ext, *sends):
    def take(upper, lower):
        for got, places in ((upper, z_places(False)), (lower, z_places(True))):
            for k, p in enumerate(places):
                ext[EXT_AT[p]] = got[k]

    by_parity("gz", take, z_e, z_o)
    ext[EXT_AT[TP]] = tile[0]
    ext[EXT_AT[RT]] = tile[1]

    def put(high, low):
        for p in range(PLANES):
            src, k, rows = (rim, OWN_AT[p], 16) if p in OWN_AT else (ext, EXT_AT[p], ROWS)
            if high is not None:
                high[p, pl.ds(0, HALO), :] = src[k, pl.ds(rows - HALO, HALO), :]
            if low is not None:
                low[p, pl.ds(0, HALO), :] = src[k, pl.ds(0, HALO), :]

    by_parity("gx", put, sends[0], sends[1] if count_gx > 2 else None)


def y_faces(count_gx, *refs):
    rim, own_pack, ext = refs[:3]
    if count_gx > 2:
        got_e, got_o = refs[4], refs[5]
    else:
        got_e, got_o = refs[4], None
    edge, strips, send_e, send_o, lines = refs[-5:]

    def take(high, low):
        for p in range(PLANES):
            edge[p] = rim[OWN_AT[p], 8:16] if p in OWN_AT else ext[EXT_AT[p], ROWS - EDGE : ROWS]
            if high is not None:
                edge[p, pl.ds(0, HALO), :] = high[p, pl.ds(0, HALO), :]
            if low is not None:
                edge[p, pl.ds(EDGE - HALO, HALO), :] = low[p, pl.ds(0, HALO), :]

    even_x = is_even("gx")

    @pl.when(even_x)
    def _():
        take(got_e, got_o)

    @pl.when(jnp.logical_not(even_x))
    def _():
        take(got_o, got_e)

    group = lax.broadcasted_iota(jnp.int32, (ROWS, COLS), 1) // SIDE
    for t in range(PACKS):
        rows = own_pack[t]
        for j in range(8):
            p = t * 8 + j
            if p in EXT_AT:
                rows = jnp.where(group == j, pltpu.roll(ext[EXT_AT[p]], SIDE * j + 8, 1), rows)
        last = packed_tile(t, lambda p: edge[p], EDGE)
        full = widened(jnp.concatenate([rows, last], axis=0))
        strips[t * COLS : (t + 1) * COLS, :] = full.T

    lane = lax.broadcasted_iota(jnp.int32, (Y_ROWS // 2, COLS), 1)

    def put(high, low):
        for send, last in ((high, True), (low, False)):
            at = 0
            for p in range(PLANES):
                count = columns_sent(p)
                if count:
                    start = p * SIDE + (8 - count if last else 8)
                    lines[pl.ds(at, count), :] = strips[pl.ds(start, count), :]
                    at += count
            lines[pl.ds(at, Y_ROWS - at), :] = jnp.zeros((Y_ROWS - at, COLS), jnp.float32)
            first, second = lines[0 : Y_ROWS // 2], lines[Y_ROWS // 2 : Y_ROWS]
            send[0 : Y_ROWS // 2] = jnp.where(lane < ROWS, first, pltpu.roll(second, ROWS, 1))
            extra = jnp.zeros((Y_EXTRA, COLS), jnp.float32)
            for g in range(Y_ROWS // Y_EXTRA):
                part = pltpu.roll(lines[g * Y_EXTRA : (g + 1) * Y_EXTRA], (EDGE * g - ROWS) % COLS, 1)
                extra = jnp.where(lane[0:Y_EXTRA] // EDGE == g, part, extra)
            send[Y_ROWS // 2 : Y_SEND] = extra

    by_parity("role", put, send_e, send_o)


def uptake_of(tpot, roots, head, layers, base_exp, first):
    total = jnp.zeros_like(tpot)
    for layer in range(layers):
        total = total + jnp.where(roots > float(layer), math.exp(-layer / 4.0), 0.0)
    share = tpot * base_exp / total
    result = []
    for q in range(LAYERS_PER_BLOCK + 2):
        depth = (first + (q - 1)).astype(jnp.float32)
        weight = jnp.where(depth < roots, math.exp(-(q - 1) / 4.0) * share, 0.0)
        result.append(weight / (1.0 + head[q] * head[q] * (1.0 / 2.25)))
    return result


def inner_lane(k):
    return k // 9 * 18 + k % 9


class Where:
    def __init__(self, count_role, count_gx, count_gz):
        me_role, me_gx, me_gz = place("role"), place("gx"), place("gz")
        f32 = jnp.float32
        self.layers = LAYERS_PER_BLOCK * count_gz
        self.first = me_gz * LAYERS_PER_BLOCK
        self.z_top = jnp.where(me_gz == 0, 0.0, 1.0).astype(f32)
        self.z_bottom = jnp.where(me_gz == count_gz - 1, 0.0, 1.0).astype(f32)
        self.x_first = jnp.where(me_gx == 0, 0.0, 1.0).astype(f32)
        self.x_last = jnp.where(me_gx == count_gx - 1, 0.0, 1.0).astype(f32)
        self.y_first = jnp.where(me_role == 0, 0.0, 1.0).astype(f32)
        self.y_last = jnp.where(me_role == count_role - 1, 0.0, 1.0).astype(f32)
        self.exp_first = jnp.exp(jnp.zeros((8, COLS), f32) - me_gz.astype(f32))


def widened(value):
    return jnp.concatenate([value] + [value[ROWS:WIDE]] * ((COLS - WIDE) // EDGE), axis=0)


def main_region(count_role, count_gx, count_gz, params, ext, edge, *refs):
    land_in, poro_in, refs = refs[:5], refs[5], refs[10:]
    out, inner, land_out, ha, kc, mm, th, hb, wd, sk, poro, poro_sem = refs[:12]
    heat_finish = heat(count_gx, count_gz, *land_in, land_out, *refs[12:])
    poro_copy = pltpu.make_async_copy(poro_in, poro, poro_sem)
    poro_copy.start()
    spot = Where(count_role, count_gx, count_gz)
    z_top, z_bottom = spot.z_top, spot.z_bottom

    def wide(p):
        return jnp.concatenate([ext[EXT_AT[p]], edge[p]], axis=0)

    def wide_own(k, level):
        rows = poro[level] if k == 4 else params[(k - 1) * LEVELS + level]
        return jnp.concatenate([rows, edge[OWN[k] + level]], axis=0)

    def inputs(j):
        if isinstance(j, int):
            return [wide(A0 + j), wide(N0 + j), wide(S0 + j)] + ([wide(P0 + j - 1)] if 0 < j < NC - 1 else [])
        return [wide_own(k, j - (HALO - 1)) for k in (1, 2, 3, 4)]

    def put(ref, i, value):
        ref[i, 8 : 8 + WIDE] = value
        ref[i, 0:8] = value[ROWS:WIDE]
        ref[i, 8 + WIDE : 16 + WIDE] = value[0:8]

    row = lax.broadcasted_iota(jnp.int32, (8, COLS), 0)
    x_low = jnp.where(row == 0, spot.x_first, 1.0)
    x_high = jnp.where(row == 7, spot.x_last, 1.0)

    def put_edge(ref, i, value):
        ref[i, 8 + ROWS : 8 + WIDE] = value
        ref[i, 0:8] = value
        ref[i, 8 + WIDE : 16 + WIDE] = ref[i, 8:16]

    for level in range(LEVELS):
        put_edge(ha, HALO + level, edge[OWN[0] + level])
    for i in range(HALO):
        put(ha, i, wide(H0 + i))
        put(ha, HALO + LEVELS + i, wide(H0 + HALO + LEVELS + i))
    put(kc, 0, wide(K_LO))
    put(kc, NH - 1, wide(K_HI))

    def mean4(ref, i):
        return (ref[i, 8 : 8 + WIDE] + ref[i + 1, 8 : 8 + WIDE] + ref[i + 2, 8 : 8 + WIDE] + ref[i + 3, 8 : 8 + WIDE]) * 0.25

    heads = [wide(M_LO)] + [mean4(ha, HALO + 4 * q) for q in range(LAYERS_PER_BLOCK)] + [wide(M_HI)]
    base = jnp.concatenate([spot.exp_first] * (WIDE // 8), axis=0)
    for q, value in enumerate(uptake_of(wide(TP), wide(RT), heads, spot.layers, base, spot.first)):
        sk[q] = value

    def first_curves(j):
        i = j + 1
        alpha2, half_n, half_ks, *poros = inputs(j)
        expo = expo_of(half_n)
        mm[j] = expo
        satur, cond = curves(ha[i, 8 : 8 + WIDE], alpha2, half_n, half_ks, expo)
        put(kc, i, cond)
        if poros:
            th[j - 1] = satur

    def later_curves(src, j):
        i = j + 1
        alpha2, half_n, half_ks, *poros = inputs(j)
        satur, cond = curves(src[i, 8 : 8 + WIDE], alpha2, half_n, half_ks, mm[j])
        put(kc, i, cond)
        if poros:
            wd[j - 1] = poros[0] * (satur - th[j - 1]) + sk[(i + 1) // LEVELS_PER_LAYER]

    def curves_of(body, extra):
        for j in range(HALO - 1 - extra, HALO - 1):
            body(j)
        loop(HALO - 1, HALO - 1 + LEVELS, body, 4)
        for j in range(HALO - 1 + LEVELS, HALO - 1 + LEVELS + extra):
            body(j)

    def stencil(src, i0, count, sweep, store):
        size = WIDE if sweep < SWEEPS - 1 else ROWS
        here = pl.ds(8, size)
        conds = [kc[i0 + g - 1, here, :] for g in range(count + 2)]
        heads = [src[i0 + g - 1, here, :] for g in range(count + 2)]
        faces = [conds[g] + conds[g + 1] for g in range(count + 1)]
        faces[0] = faces[0] * jnp.where(i0 == HALO, z_top, jnp.where(i0 == HALO + LEVELS, z_bottom, 1.0))
        end = i0 + count
        faces[count] = faces[count] * jnp.where(
            end == HALO, z_top, jnp.where(end == HALO + LEVELS, z_bottom, 1.0)
        )
        for g in range(count):
            i = i0 + g
            head, cond = heads[g + 1], conds[g + 1]
            kf_up, kf_down = faces[g], faces[g + 1]
            kf_xm = cond + kc[i, pl.ds(7, size), :]
            kf_xm = jnp.concatenate([kf_xm[0:8] * x_low, kf_xm[8:]], axis=0)
            kf_xp = cond + kc[i, pl.ds(9, size), :]
            parts = [kf_xp[: ROWS - 8], kf_xp[ROWS - 8 : ROWS] * x_high] + ([kf_xp[ROWS:]] if size > ROWS else [])
            kf_xp = jnp.concatenate(parts, axis=0)
            kf_ym = cond + pltpu.roll(cond, 1, 1)
            kf_yp = cond + pltpu.roll(cond, COLS - 1, 1)
            inflow = kf_up * (heads[g] + 1.0) + kf_down * (heads[g + 2] - 1.0)
            inflow = inflow + (kf_xm * src[i, pl.ds(7, size), :] + kf_xp * src[i, pl.ds(9, size), :])
            inflow = inflow + (kf_ym * pltpu.roll(head, 1, 1) + kf_yp * pltpu.roll(head, COLS - 1, 1))
            lost = wd[i - 2, 0:size, :] if sweep > 0 else sk[(i + 1) // LEVELS_PER_LAYER]
            diag = (1.0 + kf_up) + (kf_down + kf_xm) + (kf_xp + kf_ym) + kf_yp
            store(i, relax(head, inflow - lost, diag, sweep))

    def loop(lo, hi, body, unroll=1):
        def step(i, carry):
            body(i)
            return carry

        lax.fori_loop(lo, hi, step, 0, unroll=unroll)

    def levels_of(src, sweep, store):
        extra = SWEEPS - 1 - sweep
        if extra:
            stencil(src, HALO - extra, extra, sweep, store)
        loop(0, LEVELS // 8, lambda k: stencil(src, HALO + 8 * k, 8, sweep, store))
        if extra:
            stencil(src, HALO + LEVELS, extra, sweep, store)

    def edges(k):
        return edge[OWN[k] : OWN[k] + LEVELS].reshape(LEVELS * EDGE, COLS)

    half_n = edges(2)
    expo = expo_of(half_n)
    satur, cond = curves(edges(0), edges(1), half_n, edges(3), expo)
    for level in range(LEVELS):
        rows = slice(level * EDGE, (level + 1) * EDGE)
        put_edge(kc, HALO + level, cond[rows])
        mm[HALO - 1 + level, ROWS:WIDE] = expo[rows]
        th[HALO - 2 + level, ROWS:WIDE] = satur[rows]
    for j in (0, 1, NC - 2, NC - 1):
        first_curves(j)
    levels_of(ha, 0, lambda i, value: put(hb, i, value))
    land_sent = heat_finish()

    lane_wide = lax.broadcasted_iota(jnp.int32, (WIDE, COLS), 1)
    acc = jnp.zeros((WIDE, COLS), jnp.float32)
    for k in range(NC):
        lane = inner_lane(k)
        pick = (lane_wide == lane) | (lane_wide == lane + 9)
        acc = jnp.where(pick, pltpu.roll(hb[k + 1, 8 : 8 + WIDE], (lane - (COLS - 1 - NEAR)) % COLS, 1), acc)
    inner[...] = widened(acc).T

    poro_copy.wait()
    curves_of(lambda j: later_curves(hb, j), 2)
    levels_of(hb, 1, lambda i, value: put(ha, i, value))
    curves_of(lambda j: later_curves(ha, j), 1)

    def keep(i, value):
        out[i - HALO] = value

    levels_of(ha, 2, keep)
    land_sent.wait()


def edge_strips(count_role, count_gx, count_gz, main, inner, strips_in, y_e, y_o, out,
                strips, sa, sb, sc, ks, sm, sth, swd, ssk, turn, done, lines, sem):
    spot = Where(count_role, count_gx, count_gz)
    z_top, z_bottom = spot.z_top, spot.z_bottom
    f32 = jnp.float32
    strips[...] = strips_in[...]

    line = lax.broadcasted_iota(jnp.int32, (Y_EXTRA, COLS), 1)

    def take(high, low):
        for got, last in ((high, False), (low, True)):
            extra = got[Y_ROWS // 2 : Y_SEND]
            for g in range(Y_ROWS // Y_EXTRA):
                first = g * Y_EXTRA % (Y_ROWS // 2)
                rows = got[first : first + Y_EXTRA]
                if g * Y_EXTRA >= Y_ROWS // 2:
                    rows = pltpu.roll(rows, ROWS, 1)
                rows = jnp.where(line < ROWS, rows, pltpu.roll(extra, (ROWS - EDGE * g) % COLS, 1))
                rows = jnp.where(line < COLS - EDGE, rows, pltpu.roll(extra, (COLS - EDGE - EDGE * g) % COLS, 1))
                lines[g * Y_EXTRA : (g + 1) * Y_EXTRA] = rows
            at = 0
            for p in range(PLANES):
                count = columns_sent(p)
                if count:
                    start = p * SIDE + (SIDE - count if last else 0)
                    strips[pl.ds(start, count), :] = lines[pl.ds(at, count), :]
                    at += count

    by_parity("role", take, y_e, y_o)

    def strip(p, count=1):
        return strips[p * SIDE : (p + count) * SIDE, :]

    heads = [strip(M_LO)]
    for q in range(LAYERS_PER_BLOCK):
        at = H0 + HALO + 4 * q
        heads.append((strip(at) + strip(at + 1) + strip(at + 2) + strip(at + 3)) * 0.25)
    heads.append(strip(M_HI))
    base = jnp.concatenate([spot.exp_first] * 2, axis=0)
    for q, value in enumerate(uptake_of(strip(TP), strip(RT), heads, spot.layers, base, spot.first)):
        ssk[q * SIDE : (q + 1) * SIDE, :] = value

    lane = lax.broadcasted_iota(jnp.int32, (SIDE, COLS), 1)
    srow = lax.broadcasted_iota(jnp.int32, (SIDE, COLS), 0)
    s_xm = jnp.where(lane == 0, spot.x_first, 1.0)
    s_xp = jnp.where(lane == ROWS - 1, spot.x_last, 1.0)
    side_mask = jnp.where(srow < 8, spot.y_last, spot.y_first)
    s_ym = jnp.where(srow % 8 == 0, side_mask, 1.0)
    s_yp = jnp.where(srow % 8 == 7, side_mask, 1.0)

    def tiled(mask, count):
        return jnp.concatenate([mask] * count, axis=0)

    def y_shift(value, by):
        parts = value.reshape(value.shape[0] // 8, 8, COLS)
        return pltpu.roll(parts, by, 1).reshape(value.shape)

    def rows_of(i, count):
        return slice(i * SIDE, (i + count) * SIDE)

    def strip_curves(src, lo, hi, sweep):
        i = lo
        while i < hi:
            count = min(5, hi - i)
            j = i - 1
            here = rows_of(i, count)
            half_n = strip(N0 + j, count)
            if sweep == 0:
                expo = expo_of(half_n)
                sm[rows_of(j, count), :] = expo
            else:
                expo = sm[rows_of(j, count), :]
            satur, cond = curves(src[here, :], strip(A0 + j, count), half_n, strip(S0 + j, count), expo)
            ks[here, :] = cond
            start, stop = max(i, 2), min(i + count, NH - 2)
            if stop > start:
                part = satur[(start - i) * SIDE : (stop - i) * SIDE]
                at = rows_of(start - 2, stop - start)
                if sweep == 0:
                    sth[at, :] = part
                else:
                    swd[at, :] = strip(P0 + start - 2, stop - start) * (part - sth[at, :])
            i += count

    def strip_stencil(src, dst, lo, hi, sweep):
        i = lo
        while i < hi:
            count = min(5, hi - i)
            here = rows_of(i, count)
            above, below = rows_of(i - 1, count), rows_of(i + 1, count)
            head, cond = src[here, :], ks[here, :]
            kf_up = cond + ks[above, :]
            kf_down = cond + ks[below, :]
            if i <= HALO < i + count:
                level = lax.broadcasted_iota(jnp.int32, kf_up.shape, 0) // SIDE
                kf_up = jnp.where(level == HALO - i, kf_up * z_top, kf_up)
            if i <= HALO + LEVELS - 1 < i + count:
                level = lax.broadcasted_iota(jnp.int32, kf_up.shape, 0) // SIDE
                kf_down = jnp.where(level == HALO + LEVELS - 1 - i, kf_down * z_bottom, kf_down)
            kf_xm = (cond + pltpu.roll(cond, 1, 1)) * tiled(s_xm, count)
            kf_xp = (cond + pltpu.roll(cond, COLS - 1, 1)) * tiled(s_xp, count)
            kf_ym = (cond + y_shift(cond, 1)) * tiled(s_ym, count)
            kf_yp = (cond + y_shift(cond, 7)) * tiled(s_yp, count)
            inflow = kf_up * (src[above, :] + 1.0) + kf_down * (src[below, :] - 1.0)
            inflow = inflow + (kf_xm * pltpu.roll(head, 1, 1) + kf_xp * pltpu.roll(head, COLS - 1, 1))
            inflow = inflow + (kf_ym * y_shift(head, 1) + kf_yp * y_shift(head, 7))
            lost = jnp.concatenate([ssk[rows_of((k + 1) // LEVELS_PER_LAYER, 1), :] for k in range(i, i + count)], axis=0)
            if sweep > 0:
                lost = lost + swd[rows_of(i - 2, count), :]
            diag = (1.0 + kf_up) + (kf_down + kf_xm) + (kf_xp + kf_ym) + kf_yp
            dst[here, :] = relax(head, inflow - lost, diag, sweep)
            i += count

    ks[rows_of(0, 1), :] = strip(K_LO)
    ks[rows_of(NH - 1, 1), :] = strip(K_HI)
    strip_curves(strips, 1, NH - 1, 0)
    strip_stencil(strips, sa, 1, NH - 1, 0)
    for k in range(NC):
        lane = inner_lane(k)
        sa[pl.ds((k + 1) * SIDE + 3, 1), :] = inner[pl.ds(lane, 1), :]
        sa[pl.ds((k + 1) * SIDE + 8 + NEAR, 1), :] = inner[pl.ds(lane + 9, 1), :]
    strip_curves(sa, 1, NH - 1, 1)
    strip_stencil(sa, sb, 2, NH - 2, 1)
    strip_curves(sb, 2, NH - 2, 2)

    lane_rows = lax.broadcasted_iota(jnp.int32, (ROWS, COLS), 1)
    outer = (lane_rows < HALO) | (lane_rows >= COLS - HALO)
    copies = []
    half = LEVELS // 2
    for first in (0, half):
        strip_stencil(sb, sc, HALO + first, HALO + first + half, 2)
        pieces = [sc[i * SIDE + 8 - HALO : i * SIDE + 8 + HALO, :] for i in range(HALO + first, HALO + first + half)]
        pieces.append(jnp.zeros((COLS - 2 * HALO * half, COLS), f32))
        turn[...] = jnp.concatenate(pieces, axis=0).T[0:ROWS]
        for k in range(half):
            moved = pltpu.roll(turn[...], (COLS - HALO - 2 * HALO * k) % COLS, 1)
            level = first + k
            done[level] = jnp.where(outer, moved, main[level])
            copy = pltpu.make_async_copy(done.at[level], out.at[level], sem.at[level])
            copy.start()
            copies.append(copy)
    for copy in copies:
        copy.wait()


def heat(count_gx, count_gz, y, temp_in, tr_in, air_in, rt_in, land_out, out, sat, head, temp, tr, air, rt, sem, out_sem):
    copies = []
    for src, dst in ((temp_in, temp), (tr_in, tr), (air_in, air), (rt_in, rt)):
        copy = pltpu.make_async_copy(src, dst, sem.at[len(copies)])
        copy.start()
        copies.append(copy)
    def finish():
        me = place("gx") * count_gz + place("gz")
        layers = LAYERS_PER_BLOCK * count_gz
        for copy in copies:
            copy.wait()
        for gx in range(count_gx):
            for gz in range(count_gz):
                j = me ^ (gx * count_gz + gz)
                for c in range(CAP):
                    tile = y[j, c * 8 : c * 8 + 8]
                    at = pl.ds(gz * LAYERS_PER_BLOCK, LAYERS_PER_BLOCK)
                    sat[gx * CAP + c, at, :] = tile[0:LAYERS_PER_BLOCK]
                    head[gx * CAP + c, at, :] = tile[LAYERS_PER_BLOCK : 2 * LAYERS_PER_BLOCK]
        layer = lax.broadcasted_iota(jnp.int32, (layers, COLS), 0)
        decay = jnp.exp(layer.astype(jnp.float32) * -0.25)
        for slot in range(count_gx * CAP):
            roots = jnp.broadcast_to(rt[slot], (layers, COLS))
            weight = jnp.where(layer < roots, decay, 0.0)
            weight = weight / jnp.sum(weight, axis=0, keepdims=True)
            stress = 1.0 / (1.0 + head[slot] * head[slot] * (1.0 / 2.25))
            uptake = tr[slot] * weight * stress
            kappa = 0.25 + 0.9 * sat[slot]
            top = jnp.broadcast_to(air[slot], (layers, COLS))
            k_above = jnp.where(layer == 0, kappa, 0.5 * (kappa + pltpu.roll(kappa, 1, 0)))
            k_below = jnp.where(layer == layers - 1, 0.0, 0.5 * (kappa + pltpu.roll(kappa, layers - 1, 0)))
            old = temp[slot]
            new = old
            for _ in range(HEAT_STEPS):
                above = jnp.where(layer == 0, top, pltpu.roll(new, 1, 0))
                below = pltpu.roll(new, layers - 1, 0)
                new = new + 0.2 * (k_above * (above - new) + k_below * (below - new)) - 0.3 * uptake
            out[slot] = jnp.where(sat[slot] >= 0.0, new, old)
        sent = pltpu.make_async_copy(out, land_out, out_sem)
        sent.start()
        return sent

    return finish


def call(body, outs, ins, scratch=(), aliases=None, limit=16 * MIB, kept=True, work=0):
    return pl.pallas_call(
        body,
        out_shape=[pltpu.VMEM(shape, jnp.float32) if kept else jax.ShapeDtypeStruct(shape, jnp.float32) for shape in outs],
        in_specs=ins,
        out_specs=[VMEM] * len(outs),
        scratch_shapes=list(scratch),
        input_output_aliases=aliases or {},
        compiler_params=pltpu.CompilerParams(vmem_limit_bytes=limit),
        cost_estimate=pl.CostEstimate(flops=work, bytes_accessed=work, transcendentals=0) if work else None,
    )


DEEP = WIDE + 16
START_SHAPES = [(NH, DEEP, COLS), (NH, DEEP, COLS), (NC, WIDE, COLS), (NP, WIDE, COLS)]


def main_call(count_role, count_gx, count_gz):
    f32 = jnp.float32
    slots = count_gx * CAP
    land_shape = (slots, LAYERS_PER_BLOCK * count_gz, COLS)
    return pl.pallas_call(
        functools.partial(main_region, count_role, count_gx, count_gz),
        out_shape=[
            pltpu.VMEM((LEVELS, ROWS, COLS), f32),
            pltpu.VMEM((COLS, COLS), f32),
            jax.ShapeDtypeStruct(land_shape, f32),
        ]
        + [pltpu.VMEM(shape, f32) for shape in START_SHAPES],
        in_specs=[VMEM] * 4 + [HBM] * 5 + [VMEM] * 4,
        out_specs=[VMEM] * 2 + [HBM] + [VMEM] * 4,
        input_output_aliases={9 + k: 3 + k for k in range(4)},
        scratch_shapes=[
            pltpu.VMEM((NH, DEEP, COLS), f32),
            pltpu.VMEM((NP, WIDE, COLS), f32),
            pltpu.VMEM((LAYERS_PER_BLOCK + 2, WIDE, COLS), f32),
            pltpu.VMEM((LEVELS, ROWS, COLS), f32),
            pltpu.SemaphoreType.DMA(()),
            pltpu.VMEM(land_shape, f32),
            pltpu.VMEM(land_shape, f32),
            pltpu.VMEM(land_shape, f32),
            pltpu.VMEM(land_shape, f32),
            pltpu.VMEM((slots, 1, COLS), f32),
            pltpu.VMEM((slots, 1, COLS), f32),
            pltpu.VMEM((slots, 1, COLS), jnp.int32),
            pltpu.SemaphoreType.DMA((4,)),
            pltpu.SemaphoreType.DMA(()),
        ],
        compiler_params=pltpu.CompilerParams(vmem_limit_bytes=16 * MIB),
    )


def strip_call(count_role, count_gx, count_gz):
    f32 = jnp.float32
    return pl.pallas_call(
        functools.partial(edge_strips, count_role, count_gx, count_gz),
        out_shape=jax.ShapeDtypeStruct((LEVELS, ROWS, COLS), f32),
        in_specs=[VMEM] * 5,
        out_specs=HBM,
        scratch_shapes=[
            pltpu.VMEM((PACKS * COLS, COLS), f32),
            pltpu.VMEM((NH * SIDE, COLS), f32),
            pltpu.VMEM((NH * SIDE, COLS), f32),
            pltpu.VMEM((NH * SIDE, COLS), f32),
            pltpu.VMEM((NH * SIDE, COLS), f32),
            pltpu.VMEM((NC * SIDE, COLS), f32),
            pltpu.VMEM((NP * SIDE, COLS), f32),
            pltpu.VMEM((NP * SIDE, COLS), f32),
            pltpu.VMEM(((LAYERS_PER_BLOCK + 2) * SIDE, COLS), f32),
            pltpu.VMEM((ROWS, COLS), f32),
            pltpu.VMEM((LEVELS, ROWS, COLS), f32),
            pltpu.VMEM((Y_ROWS, COLS), f32),
            pltpu.SemaphoreType.DMA((LEVELS,)),
        ],
        compiler_params=pltpu.CompilerParams(vmem_limit_bytes=16 * MIB),
    )


def local(h, a, n, s, p, tile_owner, land_temp, tr, air, rt):
    sizes = tuple(lax.axis_size(axis) for axis in AXES)
    count_role, count_gx, count_gz = sizes
    groups = count_gx * count_gz
    slots = count_gx * CAP
    f32 = jnp.float32

    def swap(value, axis, odd):
        return lax.ppermute(value, AXES, pairing(sizes, axis, odd))

    owners = pltpu.with_memory_space_constraint(tile_owner.T, pltpu.HBM)
    land = (land_temp[0, 0], tr[0, 0, :, None], air[0, 0, :, None], rt[0, 0, :, None])
    h, a, n, s, p = (pltpu.with_memory_space_constraint(x, pltpu.HBM) for x in (h, a, n, s, p))
    land_temp, tr, air, rt = (pltpu.with_memory_space_constraint(x, pltpu.HBM) for x in land)

    z_send_e, z_send_o = call(
        z_faces,
        [(Z_SEND, ROWS, COLS)] * 2,
        [HBM] * 5,
        [
            pltpu.VMEM((2, 4, ROWS, COLS), f32),
            pltpu.VMEM((2, 3, ROWS, COLS), f32),
            pltpu.VMEM((2, 3, ROWS, COLS), f32),
            pltpu.VMEM((2, 3, ROWS, COLS), f32),
            pltpu.VMEM((2, 1, ROWS, COLS), f32),
            pltpu.SemaphoreType.DMA((10,)),
        ],
    )(h, a, n, s, p)
    z_e = swap(z_send_e, "gz", False)
    z_o = swap(z_send_o, "gz", True) if count_gz > 2 else z_e

    half = groups // 2
    blocks = count_gx // 2
    packed = half * 8 * CAP + blocks * 8
    x_count = 1 if count_gx == 2 else 2
    x_shape = (PLANES, 4, COLS)
    own_shapes = [(len(OWN_AT), 16, COLS), (PACKS, ROWS, COLS)]

    def land_stage():
        send, keep, hot = call(
            functools.partial(land_pack, count_gx, count_gz),
            [(packed, COLS), (packed, COLS), (ROWS, groups * 8)],
            [HBM] * 6,
            [
                pltpu.SMEM(tile_owner.shape[::-1], jnp.int32),
                pltpu.VMEM((2 * LAYERS_PER_BLOCK, ROWS, COLS), f32),
                pltpu.SMEM((groups,), jnp.int32),
                pltpu.SMEM((groups * CAP,), jnp.int32),
                pltpu.VMEM((LEVELS, ROWS, COLS), f32),
                pltpu.VMEM((LEVELS, ROWS, COLS), f32),
                pltpu.VMEM((LEVELS, ROWS, COLS), f32),
                pltpu.VMEM((slots, 1, COLS), f32),
                pltpu.VMEM((slots, 1, COLS), jnp.int32),
                pltpu.SemaphoreType.DMA((3 * LAYERS_PER_BLOCK + 2,)),
                pltpu.SemaphoreType.DMA(()),
            ],
        )(owners, h, a, n, tr, rt)

        got = lax.ppermute(send, AXES, xor_pairs(sizes, "gx", blocks))
        bit = blocks // 2
        if bit:
            pieces = [part[j * PIECE : (j + 1) * PIECE] for part in (keep, got) for j in range(half)]
            base = half * PIECE
            values = [part[base + j * 8 : base + (j + 1) * 8] for part in (keep, got) for j in range(blocks)]
            while bit:
                moving = [j for j in range(groups) if (j // count_gz) & bit]
                t_moving = [j for j in range(count_gx) if j & bit]
                sent = jnp.concatenate([pieces[j] for j in moving] + [values[j] for j in t_moving], axis=0)
                got = lax.ppermute(sent, AXES, xor_pairs(sizes, "gx", bit))
                for k, j in enumerate(moving):
                    pieces[j] = got[k * PIECE : (k + 1) * PIECE]
                for k, j in enumerate(t_moving):
                    base = len(moving) * PIECE + k * 8
                    values[j] = got[base : base + 8]
                bit //= 2
            keep = jnp.concatenate(pieces[:half] + values[:blocks], axis=0)
            got = jnp.concatenate(pieces[half:] + values[blocks:], axis=0)
        rim, pack = call(
            own_part,
            own_shapes,
            [HBM] * 5,
            [pltpu.VMEM((len(OWN_AT), ROWS, COLS), f32), pltpu.SemaphoreType.DMA((5,))],
        )(h, a, n, s, p)
        parts = call(
            functools.partial(land_sort, count_gx, count_gz),
            [(count_gx * (PIECE + 8), COLS)] * count_gz,
            [VMEM] * 2,
        )(keep, got)
        parts = [parts[0]] + [
            lax.ppermute(parts[dist], AXES, xor_pairs(sizes, "gz", dist)) for dist in range(1, count_gz)
        ]
        tile, y = call(
            functools.partial(tile_values, count_gx, count_gz),
            [(2, ROWS, COLS), (groups, PIECE, COLS)],
            [VMEM] * (1 + count_gz),
        )(hot, *parts)
        return [rim, pack, tile, y]

    def no_land_stage():
        shapes = own_shapes + [(2, ROWS, COLS), (groups, PIECE, COLS)]
        return [jnp.zeros(shape, f32) for shape in shapes]

    ahead = lax.optimization_barrier(jnp.bool_(True))
    rim, pack, tile, y = lax.cond(ahead, land_stage, no_land_stage)

    ext, *x_sends = call(
        functools.partial(x_faces, count_gx),
        [(len(EXT_AT), ROWS, COLS)] + [x_shape] * x_count,
        [VMEM] * 4,
    )(rim, z_e, z_o, tile)
    params, *start = call(
        own_curves,
        [(3 * LEVELS, ROWS, COLS)] + START_SHAPES,
        [HBM] * 4,
        [pltpu.SemaphoreType.DMA((LEVELS,))],
    )(h, a, n, s)
    x_got = [swap(value, "gx", bool(k)) for k, value in enumerate(x_sends)]

    edge, strips, y_send_e, y_send_o = call(
        functools.partial(y_faces, count_gx),
        [(PLANES, EDGE, COLS), (PACKS * COLS, COLS), (Y_SEND, COLS), (Y_SEND, COLS)],
        [VMEM] * 3 + [ANY] + [VMEM] * x_count,
        [pltpu.VMEM((Y_ROWS, COLS), f32)],
    )(rim, pack, ext, params, *x_got)
    y_e = swap(y_send_e, "role", False)
    y_o = swap(y_send_o, "role", True) if count_role > 2 else y_e

    main, inner, land_new, *_ = main_call(*sizes)(params, ext, edge, y, land_temp, tr, air, rt, p, *start)
    head = strip_call(*sizes)(main, inner, strips, y_e, y_o)
    return (head, land_new[None, None])


def solution(mesh):
    in_specs = (
        P("gz", "gx", "role"),
        P("gz", "gx", "role"),
        P("gz", "gx", "role"),
        P("gz", "gx", "role"),
        P("gz", "gx", "role"),
        P(),
        P("role", ("gx", "gz"), None, None, None),
        P("role", ("gx", "gz"), None, None),
        P("role", ("gx", "gz"), None, None),
        P("role", ("gx", "gz"), None, None),
    )
    out_specs = (P("gz", "gx", "role"), P("role", ("gx", "gz"), None, None, None))
    return jax.shard_map(local, mesh=mesh, in_specs=in_specs, out_specs=out_specs, check_vma=False)
```
